128 devices in a mesh: wide: 32 (over x, z, core), quad: 4 (over y).
Axes of the slice: x: 4, y: 4, z: 4, core: 2. Of those that a mesh axis runs over, the one named last changes fastest.
Arguments:
- fine_pops: float32 [19, 256, 128, 128], P(None, 'wide', 'quad'), may hold values from 0.36 to 8.24, as said below
- coarse_pops: float32 [19, 64, 64, 128], P(None, 'wide', 'quad'), may hold values from 0.36 to 8.24, as said below
- fine_solid: int32 [256, 128, 128], P('wide', 'quad'), may hold values 0 or 1
- coarse_solid: int32 [64, 64, 128], P('wide', 'quad'), may hold values 0 or 1
- fine_active: int32 [64, 32, 32], P('wide', 'quad'), may hold values from 0 to 1, as said below
- coarse_covered: int32 [64, 64, 128], P('wide', 'quad'), may hold values from 0 to 1, as said below
- rates: float32 [15], replicated, may hold values from 0.7 to 1.7
Outputs:
- fine_out: float32 [19, 256, 128, 128], P(None, 'wide', 'quad')
- coarse_out: float32 [19, 64, 64, 128], P(None, 'wide', 'quad')
The draws below stay inside these ranges and needn't reach their ends.
Inputs may be any that keep to these rules, and one draw needn't show every extreme that they name: `fine_pops`: populations are positive, each near w_q times 19. `coarse_pops`: populations are positive, each near w_q times 19. `fine_active`: 1 for an active fine block, 0 otherwise. coarse_covered[z, y, x] equals fine_active[x // 2, y // 2, z // 2].
All inputs are finite; a program needn't handle non-finite values. No bound on the sum of `fine_solid` or of `coarse_solid` on one device may be relied on, other than what follows from the above.
Results may differ from the reference program's by a relative error of at most 0.0003.
Values sent between devices are 32-bit elements; how exact they have to be, the bound alone decides.
No kernel may reach another device: no remote copies, remote signals or barrier semaphores. Data moves between devices by JAX's collectives and lax.ppermute only.
A program may use at most 128 MiB of HBM per device.

```python
import jax
import jax.numpy as jnp
from jax import lax

NXF = 256
NYF = 128
NZF = 128
NXC = 128
NYC = 64
NZC = 64


def population_draw(key, shape_all):
    factor = jnp.clip(0.5 * jax.random.normal(key, shape_all, jnp.float32), -1.0, 1.0)
    weights = jnp.asarray([1.0 / 3.0] + [1.0 / 18.0] * 6 + [1.0 / 36.0] * 12, jnp.float32).reshape((19, 1, 1, 1))
    return 19.0 * weights * (1.0 + 0.3 * factor)


def draw_fine_pops(key, part):
    key = jax.random.fold_in(key, 3)
    return population_draw(key, (19, NXF, NYF, NZF))


def draw_coarse_pops(key, part):
    key = jax.random.fold_in(key, 5)
    return population_draw(key, (19, NZC, NYC, NXC))


def block_mask(key):
    levels = jax.random.randint(jax.random.fold_in(key, 11), (NXF // 4, NYF // 4, NZF // 4), 0, 5)
    return (levels < 3).astype(jnp.int32)


def draw_fine_active(key, part):
    return block_mask(key)


def draw_coarse_covered(key, part):
    blocks = block_mask(key)
    grown = jnp.repeat(jnp.repeat(jnp.repeat(blocks, 2, axis=0), 2, axis=1), 2, axis=2)
    return jnp.transpose(grown, (2, 1, 0))


def touch_ends(array, stream_key, low, high):
    spot = [jax.random.randint(jax.random.fold_in(stream_key, axis), (), 0, length) for axis, length in enumerate(array.shape)]
    longest = array.shape.index(max(array.shape))
    next_to = spot[:longest] + [(spot[longest] + 1) % array.shape[longest]] + spot[longest + 1:]
    return array.at[tuple(spot)].set(low).at[tuple(next_to)].set(high)


def setup_inputs(seed: int = 0) -> dict:
    splits = jax.random.split(jax.random.key(seed), 8)
    fine_pops = draw_fine_pops(jax.random.fold_in(splits[7], 71), 0)
    coarse_pops = draw_coarse_pops(jax.random.fold_in(splits[7], 71), 0)
    fine_solid = touch_ends((jax.random.randint(splits[2], (NXF, NYF, NZF), 0, 5) < 1).astype(jnp.int32), jax.random.fold_in(splits[2], 1), 0, 1)
    coarse_solid = touch_ends((jax.random.randint(splits[3], (NZC, NYC, NXC), 0, 5) < 1).astype(jnp.int32), jax.random.fold_in(splits[3], 1), 0, 1)
    fine_active = draw_fine_active(jax.random.fold_in(splits[7], 71), 0)
    coarse_covered = draw_coarse_covered(jax.random.fold_in(splits[7], 71), 0)
    rates = jnp.clip(jax.random.uniform(splits[6], (15,), jnp.float32, 0.7, 1.7), 0.7, 1.7)
    return {"fine_pops": fine_pops, "coarse_pops": coarse_pops, "fine_solid": fine_solid, "coarse_solid": coarse_solid, "fine_active": fine_active, "coarse_covered": coarse_covered, "rates": rates}


velocity_list = [(0, 0, 0), (1, 0, 0), (-1, 0, 0), (0, 1, 0), (0, -1, 0), (0, 0, 1), (0, 0, -1), (1, 1, 0), (-1, -1, 0), (1, -1, 0), (-1, 1, 0), (1, 0, 1), (-1, 0, -1), (1, 0, -1), (-1, 0, 1), (0, 1, 1), (0, -1, -1), (0, 1, -1), (0, -1, 1)]
opposite_list = [0, 2, 1, 4, 3, 6, 5, 8, 7, 10, 9, 12, 11, 14, 13, 16, 15, 18, 17]
weight_list = [1.0 / 3.0] + [1.0 / 18.0] * 6 + [1.0 / 36.0] * 12
moment_patterns = [(0, 0, 0), (1, 0, 0), (0, 1, 0), (0, 0, 1), (1, 1, 0), (1, 0, 1), (0, 1, 1), (2, 0, 0), (0, 2, 0), (0, 0, 2), (1, 2, 0), (1, 0, 2), (2, 1, 0), (0, 1, 2), (2, 0, 1), (0, 2, 1), (2, 2, 0), (2, 0, 2), (0, 2, 2)]


def velocity_columns():
    return [[float(entry[axis_index]) for entry in velocity_list] for axis_index in range(3)]


def velocity_rows():
    return [[float(part_value) for part_value in entry] for entry in velocity_list]


def build_moments():
    columns = velocity_columns()
    table_rows = []
    for power_x, power_y, power_z in moment_patterns:
        table_rows.append([(columns[0][slot] ** power_x) * (columns[1][slot] ** power_y) * (columns[2][slot] ** power_z) for slot in range(19)])
    return table_rows


def invert_table(table_rows):
    order_size = len(table_rows)
    working = [list(table_rows[line]) + [1.0 if line == other else 0.0 for other in range(order_size)] for line in range(order_size)]
    for column in range(order_size):
        pivot_line = max(range(column, order_size), key=lambda line: abs(working[line][column]))
        working[column], working[pivot_line] = working[pivot_line], working[column]
        leading = working[column][column]
        working[column] = [entry / leading for entry in working[column]]
        for line in range(order_size):
            if line != column:
                factor = working[line][column]
                working[line] = [entry - factor * pivot_entry for entry, pivot_entry in zip(working[line], working[column])]
    return [line_values[order_size:] for line_values in working]


def make_kernel(rates_full):
    moment_table = build_moments()
    moment_inverse = invert_table(moment_table)
    inverse_rows = jnp.asarray(moment_inverse, jnp.float32) * rates_full[None, :]
    return jnp.dot(inverse_rows, jnp.asarray(moment_table, jnp.float32), precision=lax.Precision.HIGHEST, preferred_element_type=jnp.float32)


def collide(populations, kernel):
    shape_all = populations.shape
    flat = populations.reshape(19, -1)
    density = jnp.sum(flat, axis=0)
    momentum = jnp.dot(jnp.asarray(velocity_columns(), jnp.float32), flat, precision=lax.Precision.HIGHEST, preferred_element_type=jnp.float32)
    velocity = momentum / density[None, :]
    speed_square = jnp.sum(velocity * velocity, axis=0)
    along = jnp.dot(jnp.asarray(velocity_rows(), jnp.float32), velocity, precision=lax.Precision.HIGHEST, preferred_element_type=jnp.float32)
    weights = jnp.asarray(weight_list, jnp.float32)[:, None]
    equilibrium = weights * density[None, :] * (1.0 + 3.0 * along + 4.5 * along * along - 1.5 * speed_square[None, :])
    post = flat - jnp.dot(kernel, flat - equilibrium, precision=lax.Precision.HIGHEST, preferred_element_type=jnp.float32)
    return post.reshape(shape_all)


def stream(padded, post, order):
    extent = post.shape[1:]
    pieces = []
    for index in range(19):
        starts = [1 - velocity_list[index][axis] for axis in order]
        window = tuple(slice(start, start + length) for start, length in zip(starts, extent))
        moved = padded[(index,) + window]
        fluid_near = padded[(19,) + window]
        pieces.append(jnp.where(fluid_near > 0.5, moved, post[opposite_list[index]]))
    return jnp.stack(pieces)


def expand_blocks(mask):
    blocks_x, blocks_y, blocks_z = mask.shape
    grown = jnp.broadcast_to(mask[:, None, :, None, :, None], (blocks_x, 4, blocks_y, 4, blocks_z, 4))
    return grown.reshape(blocks_x * 4, blocks_y * 4, blocks_z * 4)


def level_step(populations, live, fluid, kernel, order):
    post = collide(populations, kernel)
    source = jnp.where(live[None], post, populations)
    stacked = jnp.concatenate([source, fluid[None]], axis=0)
    padded = jnp.pad(stacked, ((0, 0), (1, 1), (1, 1), (1, 1)))
    moved = stream(padded, post, order)
    return jnp.where(live[None], moved, populations)


def children_sum(populations):
    depth, extent_x, extent_y, extent_z = populations.shape
    grouped = populations.reshape(depth, extent_x // 2, 2, extent_y // 2, 2, extent_z // 2, 2).sum(axis=(2, 4, 6))
    return jnp.transpose(grouped, (0, 3, 2, 1))


def reference(fine_pops, coarse_pops, fine_solid, coarse_solid, fine_active, coarse_covered, rates):
    zeros_four = jnp.zeros((4,), jnp.float32)
    fine_kernel = make_kernel(jnp.concatenate([zeros_four, rates]))
    coarse_kernel = make_kernel(jnp.concatenate([zeros_four, 1.0 / (2.0 / rates - 0.5)]))
    fluid_fine = (fine_solid == 0)
    live_fine = (expand_blocks(fine_active) == 1) & fluid_fine
    fluid_fine_value = fluid_fine.astype(jnp.float32)
    first = level_step(fine_pops, live_fine, fluid_fine_value, fine_kernel, (0, 1, 2))
    fine_out = level_step(first, live_fine, fluid_fine_value, fine_kernel, (0, 1, 2))
    restricted = children_sum(first + fine_out) * 0.0625
    coarse_pre = jnp.where(coarse_covered[None] == 1, restricted, coarse_pops)
    live_coarse = coarse_solid == 0
    coarse_out = level_step(coarse_pre, live_coarse, live_coarse.astype(jnp.float32), coarse_kernel, (2, 1, 0))
    return (fine_out, coarse_out)
```

```python
import jax
import jax.numpy as jnp
from jax import lax
from jax.experimental import pallas as pl
from jax.experimental.pallas import tpu as pltpu
from jax.sharding import PartitionSpec as P

VEL = [
    (0, 0, 0),
    (1, 0, 0),
    (-1, 0, 0),
    (0, 1, 0),
    (0, -1, 0),
    (0, 0, 1),
    (0, 0, -1),
    (1, 1, 0),
    (-1, -1, 0),
    (1, -1, 0),
    (-1, 1, 0),
    (1, 0, 1),
    (-1, 0, -1),
    (1, 0, -1),
    (-1, 0, 1),
    (0, 1, 1),
    (0, -1, -1),
    (0, 1, -1),
    (0, -1, 1),
]
OPP = [0, 2, 1, 4, 3, 6, 5, 8, 7, 10, 9, 12, 11, 14, 13, 16, 15, 18, 17]


def moving(axis, sign):
    return [q for q in range(19) if VEL[q][axis] == sign]


XP, XM = moving(0, 1), moving(0, -1)
YP, YM = moving(1, 1), moving(1, -1)
ZP, ZM = moving(2, 1), moving(2, -1)
WALL = 1e30
WALL_TEST = 1e29
F32 = jnp.float32
MIB = 1 << 20

Y_FINE = 80
Y_TILES = Y_FINE + 2
X_FINE = 125
X_TILES = X_FINE + 13


def collide(f, rate):
    r_xy, r_xz, r_yz, r_xx, r_yy, r_zz = rate[:6]
    r_xyy, r_xzz, r_yxx, r_yzz, r_zxx, r_zyy, r_xxyy, r_xxzz, r_yyzz = rate[6:]
    sx, dx = f[1] + f[2], f[1] - f[2]
    sy, dy = f[3] + f[4], f[3] - f[4]
    sz, dz = f[5] + f[6], f[5] - f[6]

    def plane(i):
        a, b = f[i] + f[i + 1], f[i + 2] + f[i + 3]
        c, d = f[i] - f[i + 1], f[i + 2] - f[i + 3]
        return a + b, a - b, c + d, c - d

    m_xxyy, m_xy, m_xyy, m_yxx = plane(7)
    m_xxzz, m_xz, m_xzz, m_zxx = plane(11)
    m_yyzz, m_yz, m_yzz, m_zyy = plane(15)
    m_xx = sx + (m_xxyy + m_xxzz)
    m_yy = sy + (m_xxyy + m_yyzz)
    m_zz = sz + (m_xxzz + m_yyzz)
    jx = dx + (m_xyy + m_xzz)
    jy = dy + (m_yxx + m_yzz)
    jz = dz + (m_zxx + m_zyy)
    rho = (f[0] + sx) + (sy + sz) + ((m_xxyy + m_xxzz) + m_yyzz)
    inv = 1.0 / rho
    ux, uy, uz = jx * inv, jy * inv, jz * inv
    xx, yy, zz = jx * ux, jy * uy, jz * uz
    third = rho * (1.0 / 3.0)
    ninth = rho * (1.0 / 9.0)
    jx3, jy3, jz3 = jx * (1.0 / 3.0), jy * (1.0 / 3.0), jz * (1.0 / 3.0)
    xx3, yy3, zz3 = xx * (1.0 / 3.0), yy * (1.0 / 3.0), zz * (1.0 / 3.0)
    h_xx = (m_xx - third - xx) * r_xx
    h_yy = (m_yy - third - yy) * r_yy
    h_zz = (m_zz - third - zz) * r_zz
    post = [None] * 19

    def diagonal(i, fourth, cross, first, second):
        p, m = fourth + cross, fourth - cross
        s, d = first + second, first - second
        post[i] = f[i] - (p + s)
        post[i + 1] = f[i + 1] - (p - s)
        post[i + 2] = f[i + 2] - (m + d)
        post[i + 3] = f[i + 3] - (m - d)

    a_xy = (m_xxyy - ninth - (xx3 + yy3 - 0.5 * zz3)) * r_xxyy
    a_xz = (m_xxzz - ninth - (xx3 + zz3 - 0.5 * yy3)) * r_xxzz
    a_yz = (m_yyzz - ninth - (yy3 + zz3 - 0.5 * xx3)) * r_yyzz
    c_xyy, c_yxx = (m_xyy - jx3) * r_xyy, (m_yxx - jy3) * r_yxx
    c_xzz, c_zxx = (m_xzz - jx3) * r_xzz, (m_zxx - jz3) * r_zxx
    c_yzz, c_zyy = (m_yzz - jy3) * r_yzz, (m_zyy - jz3) * r_zyy
    diagonal(7, a_xy, (m_xy - jx * uy) * r_xy, c_xyy, c_yxx)
    diagonal(11, a_xz, (m_xz - jx * uz) * r_xz, c_xzz, c_zxx)
    diagonal(15, a_yz, (m_yz - jy * uz) * r_yz, c_yzz, c_zyy)

    def straight(i, h, a, c):
        p, n = h - 2.0 * a, 2.0 * c
        post[i] = f[i] - (p - n)
        post[i + 1] = f[i + 1] - (p + n)

    straight(1, h_xx, a_xy + a_xz, c_xyy + c_xzz)
    straight(3, h_yy, a_xy + a_yz, c_yxx + c_yzz)
    straight(5, h_zz, a_xz + a_yz, c_zxx + c_zyy)
    post[0] = f[0] + (2.0 * (h_xx + h_yy + h_zz) - 4.0 * (a_xy + a_xz + a_yz))
    return post


def scaled_rates(rates_ref, coarse):
    base = 15 if coarse else 0
    return [rates_ref[base + i] for i in range(15)]


def iota(shape, axis):
    return lax.broadcasted_iota(jnp.int32, shape, axis)


def wall_where(code, value):
    return jnp.where(code > 0.5, value, WALL)


def first_kernel(
    rates, f, solid, active, cp, c_solid, c_cov, src, xu, xd, yu, yd, zu, zd, act
):
    fine = scaled_rates(rates, False)
    coarse = scaled_rates(rates, True)
    grow_z = (iota((32, 128), 1) // 4 == iota((32, 128), 0)).astype(F32)
    grow_y = (iota((32, 8), 0) // 4 == iota((32, 8), 1)).astype(F32)
    for b in range(2):
        wide_z = jnp.dot(active[b].astype(F32), grow_z, preferred_element_type=F32)
        act[b] = jnp.dot(grow_y, wide_z, preferred_element_type=F32)

    def plane(x, carry):
        for t in range(4):
            rows = pl.ds(8 * t, 8)
            old = [f[q, x, rows] for q in range(19)]
            fluid = solid[x, rows] == 0
            on = act[x // 4, rows]
            live = fluid & (on > 0.5)
            post = collide(old, fine)
            for q in range(19):
                src[q, x, rows] = jnp.where(live, post[q], old[q])
            src[19, x, rows] = jnp.where(fluid, 1.0 + on, 0.0)
        for p in range(10):
            yu[8 * p + x, 0:4] = src[2 * p, x, 28:32]
            yu[8 * p + x, 4:8] = src[2 * p + 1, x, 28:32]
            yd[8 * p + x, 0:4] = src[2 * p, x, 0:4]
            yd[8 * p + x, 4:8] = src[2 * p + 1, x, 0:4]
        return carry

    lax.fori_loop(0, 8, plane, 0)
    for q in range(20):
        xu[q] = src[q, 7]
        xd[q] = src[q, 0]
    for i in range(5):
        xu[20 + i] = wall_where(src[19, 6], src[XP[i], 6])
        xd[20 + i] = wall_where(src[19, 1], src[XM[i], 1])

    for z in range(2):
        for t in range(2):
            rows = pl.ds(8 * t, 8)
            post = collide([cp[q, z, rows] for q in range(19)], coarse)
            code = jnp.where(c_solid[z, rows] == 0, 1.0 + c_cov[z, rows].astype(F32), 0.0)
            values, to = (ZP, zu) if z == 1 else (ZM, zd)
            for i in range(5):
                to[i, rows] = post[values[i]]
            to[5, rows] = code
            values, to, row = (YM, yd, 0) if t == 0 else (YP, yu, 7)
            for i in range(6):
                place = 6 * z + i
                value = code if i == 5 else post[values[i]]
                to[Y_FINE + place // 8, place % 8 : place % 8 + 1] = value[row : row + 1]


def halo_tile(q, x, ru, rd, sub):
    place = 8 * (q // 2) + x
    low, high = rd[place], ru[place]
    if q % 2 == 0:
        high = pltpu.roll(high, 4, 0)
    else:
        low = pltpu.roll(low, 4, 0)
    return jnp.where(sub < 4, low, high)


def halo_code(x, ru, rd, sub, has_prev, has_next):
    inside = jnp.where(sub < 4, has_next, has_prev)
    return halo_tile(19, x, ru, rd, sub) * inside


def edges():
    quad, wide = lax.axis_index("quad"), lax.axis_index("wide")
    return (
        (quad > 0).astype(F32),
        (quad < lax.axis_size("quad") - 1).astype(F32),
        (wide > 0).astype(F32),
        (wide < lax.axis_size("wide") - 1).astype(F32),
    )


def second_kernel(xu, xd, zu, zd, ru, rd, pu, pd):
    has_prev, has_next, _, _ = edges()
    sub = iota((8, 128), 0)
    for face, out, near, far, values in ((xu, pu, 7, 6, XP), (xd, pd, 0, 1, XM)):
        far_code = halo_code(far, ru, rd, sub, has_prev, has_next)
        for i in range(25):
            for t in range(4):
                out[5 * i + t] = face[i, 8 * t : 8 * t + 8]
            if i < 19:
                tile = halo_tile(i, near, ru, rd, sub)
            elif i == 19:
                tile = halo_code(near, ru, rd, sub, has_prev, has_next)
            else:
                tile = wall_where(far_code, halo_tile(values[i - 20], far, ru, rd, sub))
            out[5 * i + 4] = tile
    for face, out, z, up, down in ((zu, pu, 1, 15, 18), (zd, pd, 0, 17, 16)):
        for i in range(6):
            for t in range(2):
                out[X_FINE + 2 * i + t] = face[i, 8 * t : 8 * t + 8]

        def arrived(from_, place):
            return from_[Y_FINE + place // 8, place % 8 : place % 8 + 1]

        last = X_FINE + 12
        out[last] = jnp.zeros((8, 128), F32)
        out[last, 0:1] = arrived(ru, 6 * z + YP.index(up))
        out[last, 1:2] = arrived(rd, 6 * z + YM.index(down))
        out[last, 2:3] = arrived(ru, 6 * z + 5) * has_prev
        out[last, 3:4] = arrived(rd, 6 * z + 5) * has_next


def streamed(q, x, walled, source, live, lane):
    cx, cy, cz = VEL[q]
    if q == 0:
        return source[0, x]
    value = walled[q, x - cx]
    rows = value.shape[0]
    if cy:
        value = pltpu.roll(value, cy % rows, 0)
    if cz:
        value = pltpu.roll(value, cz % 128, 1)
    open_ = value < WALL_TEST
    if cz:
        open_ = open_ & (lane != (0 if cz == 1 else 127))
    return jnp.where(live, jnp.where(open_, value, source[OPP[q], x]), source[q, x])


def third_kernel(
    rates, src, ru, rd, rxu, rxd, fine_out, send, ext, walled, first, ext2, walled2, sums, raw, up, down
):
    has_prev, has_next, has_left, has_right = edges()
    fine = scaled_rates(rates, False)
    coarse = scaled_rates(rates, True)
    sub = iota((8, 128), 0)
    lane = iota((40, 128), 1)

    def own(x, carry):
        code_halo = halo_code(x, ru, rd, sub, has_prev, has_next)
        ext[19, x + 2, 0:32] = src[19, x]
        ext[19, x + 2, 32:40] = code_halo
        for q in range(19):
            tile = halo_tile(q, x, ru, rd, sub)
            ext[q, x + 2, 0:32] = src[q, x]
            ext[q, x + 2, 32:40] = tile
            walled[q, x + 2, 0:32] = wall_where(src[19, x], src[q, x])
            walled[q, x + 2, 32:40] = wall_where(code_halo, tile)
        return carry

    lax.fori_loop(0, 8, own, 0)
    for from_, near, far, values, inside in ((rxu, 1, 0, XP, has_left), (rxd, 10, 11, XM, has_right)):
        for t in range(5):
            rows = pl.ds(8 * t, 8)
            code = from_[5 * 19 + t] * inside
            ext[19, near, rows] = code
            for q in range(19):
                tile = from_[5 * q + t]
                ext[q, near, rows] = tile
                walled[q, near, rows] = wall_where(code, tile)
            for i in range(5):
                tile = from_[5 * (20 + i) + t]
                walled[values[i], far, rows] = jnp.where(inside > 0.5, tile, WALL)

    def substep_one(x, carry):
        live = ext[19, x] > 1.5
        for q in range(19):
            first[q, x] = streamed(q, x, walled, ext, live, lane)
        for t in range(5):
            rows = pl.ds(8 * t, 8)
            code = ext[19, x, rows]
            live_t = code > 1.5
            old = [first[q, x, rows] for q in range(19)]
            post = collide(old, fine)
            for q in range(19):
                value = jnp.where(live_t, post[q], old[q])
                ext2[q, x, rows] = value
                walled2[q, x, rows] = wall_where(code, value)
        return carry

    lax.fori_loop(1, 11, substep_one, 0)

    def substep_two(b, carry):
        x = 2 + 2 * b
        lives = [ext[19, x + e] > 1.5 for e in range(2)]
        for q in range(19):
            total = None
            for e in range(2):
                value = streamed(q, x + e, walled2, ext2, lives[e], lane)
                fine_out[q, 2 * b + e] = value[0:32]
                value = value + first[q, x + e]
                total = value if total is None else total + value
            sums[b, 40 * q : 40 * q + 40] = total
        return carry

    lax.fori_loop(0, 4, substep_two, 0)

    def taken(k, rows_):
        return 2 * iota((rows_, 128), 0) + (k - 1)

    z_lane = iota((32, 128), 1)
    own_1 = jnp.where(z_lane // 2 == taken(1, 32), 0.0625, 0.0)
    own_2 = jnp.where(z_lane // 2 == taken(2, 32), 0.0625, 0.0)
    own_rows = jnp.concatenate([own_1, own_2], axis=0)
    before = (z_lane == 2 * taken(0, 32)).astype(F32)
    after = (z_lane == 2 * taken(3, 32)).astype(F32)
    even = iota((8, 128), 1) % 2 == 0
    raw[...] = jnp.zeros(raw.shape, F32)
    up[...] = jnp.zeros(up.shape, F32)
    down[...] = jnp.zeros(down.shape, F32)
    dims = (((1,), (1,)), ((), ()))

    def block(b, carry):
        for t in range(3):
            cells = []
            for q in range(19):
                start = 40 * q + 16 * t
                value = sums[b, pl.ds(start, 8, stride=2)] + sums[b, pl.ds(start + 1, 8, stride=2)]
                if t < 2:
                    raw[16 * q + 8 * t : 16 * q + 8 * t + 8] = value
                cells.append((value + pltpu.roll(value, 127, 1)) * 0.0625)
            post = collide(cells, coarse)
            if t < 2:
                for i in range(5):
                    up[16 * i + 8 * t : 16 * i + 8 * t + 8] = post[ZP[i]]
                    down[16 * i + 8 * t : 16 * i + 8 * t + 8] = post[ZM[i]]
            else:
                for i in range(5):
                    prev = jnp.where(even, 16.0 * post[YP[i]], 0.0)
                    next_ = jnp.where(even, 16.0 * post[YM[i]], 0.0)
                    raw[304 + i : 305 + i] = prev[3:4]
                    raw[309 + i : 310 + i] = next_[0:1]
                up[80:81] = post[15][3:4]
                up[81:82] = post[18][0:1]
                down[80:81] = post[17][3:4]
                down[81:82] = post[16][0:1]
        for n in range(3):
            got = lax.dot_general(
                own_rows,
                raw[128 * n : 128 * n + 128],
                dims,
                precision=lax.Precision.HIGHEST,
                preferred_element_type=F32,
            )
            for k in range(2):
                send[pl.ds(8 * b + 2 * n + k, 32, stride=32)] = got[32 * k : 32 * k + 32]
        for k, (rows_, ref) in enumerate(((before, up), (after, down))):
            got = lax.dot_general(
                rows_,
                ref[...],
                dims,
                precision=lax.Precision.HIGHEST,
                preferred_element_type=F32,
            )
            send[pl.ds(8 * b + 6 + k, 32, stride=32)] = got
        return carry

    lax.fori_loop(0, 4, block, 0)


def fourth_kernel(
    rates, got, cp, c_solid, c_cov, ru, rd, rxu, rxd, out, turned, pre, walled, source
):
    has_prev, has_next, has_left, has_right = edges()
    coarse = scaled_rates(rates, True)
    for k in range(2):
        for n in range(4):
            turned[k, 128 * n : 128 * n + 128] = got[pl.ds(2 * n + k, 128, stride=8)].T

    def pick(code, here, there):
        return jnp.where(code > 1.5, here, jnp.where(code > 0.5, there, WALL))

    def arrived(from_, place):
        return from_[place // 8, place % 8 : place % 8 + 1]

    for k in range(2):
        for t in range(2):
            rows = pl.ds(8 * t, 8)
            fluid = c_solid[k, rows] == 0
            covered = c_cov[k, rows] == 1
            old = []
            for q in range(19):
                start = 16 * q + 8 * t
                old.append(jnp.where(covered, turned[k, start : start + 8], cp[q, k, rows]))
            post = collide(old, coarse)
            for q in range(19):
                value = jnp.where(fluid, post[q], old[q])
                source[q, k + 1, rows] = value
                walled[q, k + 1, rows] = jnp.where(fluid, value, WALL)
        prev_code = arrived(ru, 6 * k + 5) * has_prev
        next_code = arrived(rd, 6 * k + 5) * has_next
        for i in range(5):
            walled[YP[i], k + 1, 23:24] = pick(
                prev_code, turned[k, 304 + i : 305 + i], arrived(ru, 6 * k + i)
            )
            walled[YM[i], k + 1, 16:17] = pick(
                next_code, turned[k, 309 + i : 310 + i], arrived(rd, 6 * k + i)
            )
        values, from_, z, inside = ((ZP, rxu, 0, has_left), (ZM, rxd, 3, has_right))[k]
        prev_q, next_q = ((15, 18), (17, 16))[k]
        for t in range(2):
            code = from_[10 + t] * inside
            for i in range(5):
                start = 384 + 16 * i + 8 * t
                walled[values[i], z, 8 * t : 8 * t + 8] = pick(
                    code, turned[k, start : start + 8], from_[2 * i + t]
                )
        walled[prev_q, z, 23:24] = pick(
            from_[12, 2:3] * inside, turned[k, 464:465], from_[12, 0:1]
        )
        walled[next_q, z, 16:17] = pick(
            from_[12, 3:4] * inside, turned[k, 465:466], from_[12, 1:2]
        )

    lane = iota((16, 128), 1)
    for z in (1, 2):
        fluid = c_solid[z - 1] == 0
        for q in range(19):
            cx, cy, cz = VEL[q]
            value = walled[q, z - cz]
            if cy:
                value = pltpu.roll(value, cy % 24, 0)
            value = value[0:16]
            if cx:
                value = pltpu.roll(value, cx % 128, 1)
            open_ = value < WALL_TEST
            if cx:
                open_ = open_ & (lane != (0 if cx == 1 else 127))
            bounced = jnp.where(open_, value, source[OPP[q], z, 0:16])
            out[q, z - 1] = jnp.where(fluid, bounced, source[q, z, 0:16])


def shape(*dims):
    return jax.ShapeDtypeStruct(dims, F32)


def call(kernel, name, out_shape, n_vmem, scratch, smem=True):
    spec = pl.BlockSpec(memory_space=pltpu.VMEM)
    in_specs = ([pl.BlockSpec(memory_space=pltpu.SMEM)] if smem else []) + [spec] * n_vmem
    return pl.pallas_call(
        kernel,
        out_shape=out_shape,
        in_specs=in_specs,
        out_specs=[spec] * len(out_shape),
        scratch_shapes=[pltpu.VMEM(s, F32) for s in scratch],
        compiler_params=pltpu.CompilerParams(vmem_limit_bytes=56 * MIB),
        name=name,
    )


def ring(axis, step):
    count = lax.axis_size(axis)
    return [(i, (i + step) % count) for i in range(count)]


def shards(fine_pops, coarse_pops, fine_solid, coarse_solid, fine_active, coarse_covered, rates):
    factors = jnp.asarray([0.25] * 3 + [0.5] * 3 + [0.25] * 9, F32)
    both = jnp.concatenate([rates * factors, factors / (2.0 / rates - 0.5)])
    src, xu, xd, yu, yd, zu, zd = call(
        first_kernel,
        "collide_own",
        [
            shape(20, 8, 32, 128),
            shape(25, 32, 128),
            shape(25, 32, 128),
            shape(Y_TILES, 8, 128),
            shape(Y_TILES, 8, 128),
            shape(6, 16, 128),
            shape(6, 16, 128),
        ],
        6,
        [(2, 32, 128)],
    )(both, fine_pops, fine_solid, fine_active, coarse_pops, coarse_solid, coarse_covered)
    ru = lax.ppermute(yu, "quad", ring("quad", 1))
    rd = lax.ppermute(yd, "quad", ring("quad", -1))
    pu, pd = call(
        second_kernel,
        "pack_faces",
        [shape(X_TILES, 8, 128), shape(X_TILES, 8, 128)],
        6,
        [],
        smem=False,
    )(xu, xd, zu, zd, ru, rd)
    rxu = lax.ppermute(pu, "wide", ring("wide", 1))
    rxd = lax.ppermute(pd, "wide", ring("wide", -1))
    fine_out, send = call(
        third_kernel,
        "two_substeps",
        [shape(19, 8, 32, 128), shape(1024, 128)],
        5,
        [
            (20, 12, 40, 128),
            (19, 12, 40, 128),
            (19, 12, 40, 128),
            (19, 12, 40, 128),
            (19, 12, 40, 128),
            (4, 768, 128),
            (384, 128),
            (128, 128),
            (128, 128),
        ],
    )(both, src, ru, rd, rxu, rxd)
    got = lax.all_to_all(send, "wide", split_axis=0, concat_axis=0, tiled=True)
    (coarse_out,) = call(
        fourth_kernel,
        "coarse_step",
        [shape(19, 2, 16, 128)],
        8,
        [(2, 512, 128), (19, 4, 24, 128), (19, 4, 24, 128), (19, 4, 24, 128)],
    )(
        both,
        got,
        coarse_pops,
        coarse_solid,
        coarse_covered,
        ru[Y_FINE:],
        rd[Y_FINE:],
        rxu[X_FINE:],
        rxd[X_FINE:],
    )
    return (fine_out, coarse_out)


def solution(mesh):
    in_specs = (
        P(None, "wide", "quad", None),
        P(None, "wide", "quad", None),
        P("wide", "quad", None),
        P("wide", "quad", None),
        P("wide", "quad", None),
        P("wide", "quad", None),
        P(),
    )
    out_specs = (P(None, "wide", "quad", None), P(None, "wide", "quad", None))
    return jax.shard_map(shards, mesh=mesh, in_specs=in_specs, out_specs=out_specs, check_vma=False)
```

```python
import jax
import jax.numpy as jnp
from jax import lax
from jax.experimental import pallas as pl
from jax.experimental.pallas import tpu as pltpu
from jax.sharding import PartitionSpec as P

VEL = [
    (0, 0, 0),
    (1, 0, 0),
    (-1, 0, 0),
    (0, 1, 0),
    (0, -1, 0),
    (0, 0, 1),
    (0, 0, -1),
    (1, 1, 0),
    (-1, -1, 0),
    (1, -1, 0),
    (-1, 1, 0),
    (1, 0, 1),
    (-1, 0, -1),
    (1, 0, -1),
    (-1, 0, 1),
    (0, 1, 1),
    (0, -1, -1),
    (0, 1, -1),
    (0, -1, 1),
]
OPP = [0, 2, 1, 4, 3, 6, 5, 8, 7, 10, 9, 12, 11, 14, 13, 16, 15, 18, 17]


def moving(axis, sign):
    return [q for q in range(19) if VEL[q][axis] == sign]


XP, XM = moving(0, 1), moving(0, -1)
YP, YM = moving(1, 1), moving(1, -1)
ZP, ZM = moving(2, 1), moving(2, -1)
WALL = 1e30
WALL_TEST = 1e29
F32 = jnp.float32
MIB = 1 << 20

Y_FOURTH = 480
Y_COARSE = 520
Y_ROWS = 536
X_TILES = 25
X_COARSE = 25
X_ALL = X_COARSE + 13

FACTOR = [0.25] * 3 + [0.5] * 3 + [0.25] * 9

def collide(f, rate):
    r_xy, r_xz, r_yz, r_xx, r_yy, r_zz = rate[:6]
    r_xyy, r_xzz, r_yxx, r_yzz, r_zxx, r_zyy, r_xxyy, r_xxzz, r_yyzz = rate[6:]
    sx, dx = f[1] + f[2], f[1] - f[2]
    sy, dy = f[3] + f[4], f[3] - f[4]
    sz, dz = f[5] + f[6], f[5] - f[6]

    def plane(i):
        a, b = f[i] + f[i + 1], f[i + 2] + f[i + 3]
        c, d = f[i] - f[i + 1], f[i + 2] - f[i + 3]
        return a + b, a - b, c + d, c - d

    m_xxyy, m_xy, m_xyy, m_yxx = plane(7)
    m_xxzz, m_xz, m_xzz, m_zxx = plane(11)
    m_yyzz, m_yz, m_yzz, m_zyy = plane(15)
    m_xx = sx + (m_xxyy + m_xxzz)
    m_yy = sy + (m_xxyy + m_yyzz)
    m_zz = sz + (m_xxzz + m_yyzz)
    jx = dx + (m_xyy + m_xzz)
    jy = dy + (m_yxx + m_yzz)
    jz = dz + (m_zxx + m_zyy)
    rho = (f[0] + sx) + (sy + sz) + ((m_xxyy + m_xxzz) + m_yyzz)
    inv = 1.0 / rho
    ux, uy, uz = jx * inv, jy * inv, jz * inv
    xx, yy, zz = jx * ux, jy * uy, jz * uz
    third = rho * (1.0 / 3.0)
    ninth = rho * (1.0 / 9.0)
    jx3, jy3, jz3 = jx * (1.0 / 3.0), jy * (1.0 / 3.0), jz * (1.0 / 3.0)
    xx3, yy3, zz3 = xx * (1.0 / 3.0), yy * (1.0 / 3.0), zz * (1.0 / 3.0)
    h_xx = (m_xx - third - xx) * r_xx
    h_yy = (m_yy - third - yy) * r_yy
    h_zz = (m_zz - third - zz) * r_zz
    post = [None] * 19

    def diagonal(i, fourth, cross, first, second):
        p, m = fourth + cross, fourth - cross
        s, d = first + second, first - second
        post[i] = f[i] - (p + s)
        post[i + 1] = f[i + 1] - (p - s)
        post[i + 2] = f[i + 2] - (m + d)
        post[i + 3] = f[i + 3] - (m - d)

    a_xy = (m_xxyy - ninth - (xx3 + yy3 - 0.5 * zz3)) * r_xxyy
    a_xz = (m_xxzz - ninth - (xx3 + zz3 - 0.5 * yy3)) * r_xxzz
    a_yz = (m_yyzz - ninth - (yy3 + zz3 - 0.5 * xx3)) * r_yyzz
    c_xyy, c_yxx = (m_xyy - jx3) * r_xyy, (m_yxx - jy3) * r_yxx
    c_xzz, c_zxx = (m_xzz - jx3) * r_xzz, (m_zxx - jz3) * r_zxx
    c_yzz, c_zyy = (m_yzz - jy3) * r_yzz, (m_zyy - jz3) * r_zyy
    diagonal(7, a_xy, (m_xy - jx * uy) * r_xy, c_xyy, c_yxx)
    diagonal(11, a_xz, (m_xz - jx * uz) * r_xz, c_xzz, c_zxx)
    diagonal(15, a_yz, (m_yz - jy * uz) * r_yz, c_yzz, c_zyy)

    def straight(i, h, a, c):
        p, n = h - 2.0 * a, 2.0 * c
        post[i] = f[i] - (p - n)
        post[i + 1] = f[i + 1] - (p + n)

    straight(1, h_xx, a_xy + a_xz, c_xyy + c_xzz)
    straight(3, h_yy, a_xy + a_yz, c_yxx + c_yzz)
    straight(5, h_zz, a_xz + a_yz, c_zxx + c_zyy)
    post[0] = f[0] + (2.0 * (h_xx + h_yy + h_zz) - 4.0 * (a_xy + a_xz + a_yz))
    return post


def iota(shape, axis):
    return lax.broadcasted_iota(jnp.int32, shape, axis)


def fine_rates(rates):
    return [rates[i] * FACTOR[i] for i in range(15)]


def coarse_rate(rates, i):
    rate = jnp.full((8, 128), rates[i], F32)
    return FACTOR[i] / (2.0 / rate - 0.5)


def wall_where(code, value):
    return jnp.where(code > 0.5, value, WALL)


def grown_blocks(active):
    grow = (iota((32, 128), 1) // 4 == iota((32, 128), 0)).astype(F32)
    return jnp.dot(active.astype(F32), grow, preferred_element_type=F32)


def edges():
    quad, wide = lax.axis_index("quad"), lax.axis_index("wide")
    return (
        (quad > 0).astype(F32),
        (quad < lax.axis_size("quad") - 1).astype(F32),
        (wide > 0).astype(F32),
        (wide < lax.axis_size("wide") - 1).astype(F32),
    )


def rows_kernel(
    rates_in, f, solid, active, cp, c_solid, c_cov, yu, yd, zu, zd,
    rates, low, high, solid_low, solid_high, act, cps, c_solids, c_covs, sems,
):
    small = [
        pltpu.make_async_copy(solid.at[:, 0:8], solid_low, sems.at[0]),
        pltpu.make_async_copy(solid.at[:, 24:32], solid_high, sems.at[1]),
        pltpu.make_async_copy(active, act, sems.at[2]),
        pltpu.make_async_copy(rates_in, rates, sems.at[22]),
        pltpu.make_async_copy(c_solid, c_solids, sems.at[3]),
        pltpu.make_async_copy(c_cov, c_covs, sems.at[4]),
        pltpu.make_async_copy(cp, cps, sems.at[5]),
    ]
    large = []
    for x in range(8):
        large.append(
            (
                pltpu.make_async_copy(f.at[:, x, 0:8], low.at[x], sems.at[6 + x]),
                pltpu.make_async_copy(f.at[:, x, 24:32], high.at[x], sems.at[14 + x]),
            )
        )
    for copy in small[:4]:
        copy.start()
    for pair in large:
        for copy in pair:
            copy.start()
    for copy in small[4:]:
        copy.start()
    for copy in small[:4]:
        copy.wait()
    fine = fine_rates(rates)
    upper = iota((8, 128), 0) < 4
    for x in range(8):
        if x % 4 == 0:
            grown = grown_blocks(act[x // 4])
            on = jnp.where(upper, grown[0:1], grown[7:8])
        for copy in large[x]:
            copy.wait()
        old = [jnp.where(upper, low[x, q], high[x, q]) for q in range(19)]
        fluid = jnp.where(upper, solid_low[x], solid_high[x]) == 0
        live = fluid & (on > 0.5)
        post = collide(old, fine)
        source = [jnp.where(live, post[q], old[q]) for q in range(19)]
        source.append(jnp.where(fluid, 1.0 + on, 0.0))
        for q in range(20):
            start = 60 * x + 3 * q
            yu[start : start + 3] = source[q][5:8]
            yd[start : start + 3] = source[q][0:3]
        for i in range(5):
            start = Y_FOURTH + 8 * i + x
            yu[start : start + 1] = jnp.where(fluid, source[YP[i]], WALL)[4:5]
            yd[start : start + 1] = jnp.where(fluid, source[YM[i]], WALL)[3:4]
    for copy in small[4:]:
        copy.wait()
    coarse = [coarse_rate(rates, i) for i in range(15)]
    for z in range(2):
        for t in range(2):
            rows = pl.ds(8 * t, 8)
            post = collide([cps[q, z, rows] for q in range(19)], coarse)
            code = jnp.where(c_solids[z, rows] == 0, 1.0 + c_covs[z, rows].astype(F32), 0.0)
            values, to = (ZP, zu) if z == 1 else (ZM, zd)
            for i in range(5):
                to[i, rows] = post[values[i]]
            to[5, rows] = code
            values, to, row = (YM, yd, 0) if t == 0 else (YP, yu, 7)
            for i in range(6):
                place = Y_COARSE + 6 * z + i
                value = code if i == 5 else post[values[i]]
                to[place : place + 1] = value[row : row + 1]


def cells_kernel(rates, f, solid, active, ext, crate, act):
    fine = fine_rates(rates)
    for i in range(15):
        crate[i] = coarse_rate(rates, i)
    grow_y = (iota((32, 8), 0) // 4 == iota((32, 8), 1)).astype(F32)
    for b in range(2):
        act[b] = jnp.dot(grow_y, grown_blocks(active[b]), preferred_element_type=F32)

    def plane(x, carry):
        for t in range(4):
            rows = pl.ds(8 * t, 8)
            old = [f[q, x, rows] for q in range(19)]
            fluid = solid[x, rows] == 0
            on = act[x // 4, rows]
            live = fluid & (on > 0.5)
            post = collide(old, fine)
            for q in range(19):
                ext[q, x, rows] = jnp.where(live, post[q], old[q])
            ext[19, x, rows] = jnp.where(fluid, 1.0 + on, 0.0)
        return carry

    lax.fori_loop(0, 8, plane, 0)


def fill_rows(q, x, ru, rd, to):
    start = 60 * x + 3 * q
    to[0:3] = rd[start : start + 3]
    to[5:8] = ru[start : start + 3]
    if q in YM:
        fourth = Y_FOURTH + 8 * YM.index(q) + x
        to[3:4] = rd[fourth : fourth + 1]
    if q in YP:
        fourth = Y_FOURTH + 8 * YP.index(q) + x
        to[4:5] = ru[fourth : fourth + 1]


def fill_code(x, ru, rd, to, has_prev, has_next):
    start = 60 * x + 57
    to[0:3] = rd[start : start + 3] * has_next
    to[5:8] = ru[start : start + 3] * has_prev
    to[3:4] = jnp.full((1, 128), has_next, F32)
    to[4:5] = jnp.full((1, 128), has_prev, F32)


def upwards():
    return lax.axis_index("quad") % 2 == 0


def put_both(first, second, place, up, down):
    goes_up = upwards()
    first[place] = jnp.where(goes_up, up, down)
    second[place] = jnp.where(goes_up, down, up)


def faces_kernel(ext, zu, zd, ru, rd, pa, pb, code, tile):
    has_prev, has_next, _, _ = edges()
    for n, x, values in ((0, 7, XP), (1, 0, XM)):
        fill_code(x, ru, rd, code.at[n], has_prev, has_next)
        for i in range(5):
            fill_rows(values[i], x, ru, rd, tile.at[n, i])
    for i in range(5):
        for t in range(4):
            rows = pl.ds(8 * t, 8)
            up = wall_where(ext[19, 7, rows], ext[XP[i], 7, rows])
            down = wall_where(ext[19, 0, rows], ext[XM[i], 0, rows])
            put_both(pa, pb, 5 * i + t, up, down)
        up, down = wall_where(code[0], tile[0, i]), wall_where(code[1], tile[1, i])
        put_both(pa, pb, 5 * i + 4, up, down)
    for i in range(6):
        for t in range(2):
            rows = pl.ds(8 * t, 8)
            put_both(pa, pb, X_COARSE + 2 * i + t, zu[i, rows], zd[i, rows])
    for n, z, up, down in ((0, 1, 15, 18), (1, 0, 17, 16)):

        def arrived(from_, place):
            return from_[Y_COARSE + place : Y_COARSE + place + 1]

        tile[n, 0] = jnp.zeros((8, 128), F32)
        tile[n, 0, 0:1] = arrived(ru, 6 * z + YP.index(up))
        tile[n, 0, 1:2] = arrived(rd, 6 * z + YM.index(down))
        tile[n, 0, 2:3] = arrived(ru, 6 * z + 5) * has_prev
        tile[n, 0, 3:4] = arrived(rd, 6 * z + 5) * has_next
    put_both(pa, pb, X_COARSE + 12, tile[0, 0], tile[1, 0])


def streamed(q, x, values, open_cells, live, lane, outer=None):
    cx, cy, cz = VEL[q]
    if q == 0:
        return values[0, x]
    if cx and outer is not None and outer[0] == cx:
        value = outer[1](q)
    else:
        value = jnp.where(open_cells[cx], values[q, x - cx], WALL)
    if cy:
        value = pltpu.roll(value, cy % 40, 0)
    if cz:
        value = pltpu.roll(value, cz % 128, 1)
    open_ = value < WALL_TEST
    if cz:
        open_ = open_ & (lane != (0 if cz == 1 else 127))
    return jnp.where(live, jnp.where(open_, value, values[OPP[q], x]), values[q, x])


def step_plane(x, ext, first, src2, fine, lane, outer=None):
    open_cells = {}
    for cx in (-1, 0, 1):
        if outer is None or outer[0] != cx:
            open_cells[cx] = ext[19, x - cx] > 0.5
    live = ext[19, x] > 1.5
    for q in range(19):
        first[q, x] = streamed(q, x, ext, open_cells, live, lane, outer)
    for t in range(5):
        rows = pl.ds(8 * t, 8)
        live_t = ext[19, x, rows] > 1.5
        old = [first[q, x, rows] for q in range(19)]
        post = collide(old, fine)
        for q in range(19):
            src2[q, x, rows] = jnp.where(live_t, post[q], old[q])


def inner_one_kernel(rates, ext_in, ru, rd, ext, first, src2):
    has_prev, has_next, _, _ = edges()
    fine = fine_rates(rates)
    lane = iota((40, 128), 1)

    def copy(x, carry):
        for q in range(20):
            ext[q, x, 0:32] = ext_in[q, x, 0:32]
        return carry

    lax.fori_loop(0, 8, copy, 0)
    for x in range(8):
        for q in range(19):
            fill_rows(q, x, ru, rd, ext.at[q, x, 32:40])
        fill_code(x, ru, rd, ext.at[19, x, 32:40], has_prev, has_next)

    def plane(x, carry):
        step_plane(x, ext, first, src2, fine, lane)
        return carry

    lax.fori_loop(1, 7, plane, 0)


def arrived_face(first, second, from_left, inside):
    values = XP if from_left else XM
    in_first = upwards() if from_left else jnp.logical_not(upwards())

    def get(q):
        rows = pl.ds(5 * values.index(q), 5)
        value = jnp.where(in_first, first[rows], second[rows]).reshape(40, 128)
        return jnp.where(inside > 0.5, value, WALL)

    return get


def outer_one_kernel(rates, ext, ra, rb, first_in, src2_in, first, src2, pa, pb):
    _, _, has_left, has_right = edges()
    fine = fine_rates(rates)
    lane = iota((40, 128), 1)
    step_plane(0, ext, first, src2, fine, lane, (1, arrived_face(ra, rb, True, has_left)))
    step_plane(7, ext, first, src2, fine, lane, (-1, arrived_face(ra, rb, False, has_right)))
    for i in range(5):
        for t in range(5):
            rows = pl.ds(8 * t, 8)
            up = wall_where(ext[19, 7, rows], src2[XP[i], 7, rows])
            down = wall_where(ext[19, 0, rows], src2[XM[i], 0, rows])
            put_both(pa, pb, 5 * i + t, up, down)


def second_plane(x, ext, first, src2, lane, emit, outer=None):
    open_cells = {}
    for cx in (-1, 0, 1):
        if outer is None or outer[0] != cx:
            open_cells[cx] = ext[19, x - cx] > 0.5
    live = ext[19, x] > 1.5
    for q in range(19):
        emit(q, streamed(q, x, src2, open_cells, live, lane, outer), first[q, x])


def destinations(sums, coarse, raw, up, down, send, b):
    def taken(k):
        return 2 * iota((32, 128), 0) + (k - 1)

    z_lane = iota((32, 128), 1)
    own_1 = jnp.where(z_lane // 2 == taken(1), 0.0625, 0.0)
    own_2 = jnp.where(z_lane // 2 == taken(2), 0.0625, 0.0)
    own_rows = jnp.concatenate([own_1, own_2], axis=0)
    before = (z_lane == 2 * taken(0)).astype(F32)
    after = (z_lane == 2 * taken(3)).astype(F32)
    even = iota((8, 128), 1) % 2 == 0
    dims = (((1,), (1,)), ((), ()))
    for t in range(3):
        cells = []
        for q in range(19):
            start = 40 * q + 16 * t
            value = sums[pl.ds(start, 8, stride=2)] + sums[pl.ds(start + 1, 8, stride=2)]
            if t < 2:
                raw[16 * q + 8 * t : 16 * q + 8 * t + 8] = value
            cells.append((value + pltpu.roll(value, 127, 1)) * 0.0625)
        post = collide(cells, coarse)
        if t < 2:
            for i in range(5):
                up[16 * i + 8 * t : 16 * i + 8 * t + 8] = post[ZP[i]]
                down[16 * i + 8 * t : 16 * i + 8 * t + 8] = post[ZM[i]]
        else:
            for i in range(5):
                prev = jnp.where(even, 16.0 * post[YP[i]], 0.0)
                next_ = jnp.where(even, 16.0 * post[YM[i]], 0.0)
                raw[304 + i : 305 + i] = prev[3:4]
                raw[309 + i : 310 + i] = next_[0:1]
            up[80:81] = post[15][3:4]
            up[81:82] = post[18][0:1]
            down[80:81] = post[17][3:4]
            down[81:82] = post[16][0:1]

    def picked(rows, cells):
        return lax.dot_general(
            rows, cells, dims, precision=lax.Precision.HIGHEST, preferred_element_type=F32
        )

    for n in range(3):
        got = picked(own_rows, raw[128 * n : 128 * n + 128])
        for k in range(2):
            send[pl.ds(8 * b + 2 * n + k, 32, stride=32)] = got[32 * k : 32 * k + 32]
    for k, (rows, ref) in enumerate(((before, up), (after, down))):
        send[pl.ds(8 * b + 6 + k, 32, stride=32)] = picked(rows, ref[...])


def clear(*refs):
    for ref in refs:
        ref[...] = jnp.zeros(ref.shape, F32)


def inner_two_kernel(
    ext, first, src2, crate, fine_out, sums, send, planes, raw, up, down, sem
):
    lane = iota((40, 128), 1)
    clear(raw, up, down)

    def out_copy(x):
        return pltpu.make_async_copy(planes.at[x - 1], fine_out.at[:, x], sem.at[x - 1])

    def plane(x, carry):
        def emit(q, value, before):
            planes[x - 1, q] = value[0:32]
            total = value + before
            place = (x // 2, pl.ds(40 * q, 40))
            fresh = (x % 2 == 0) | (x == 1)
            sums[place] = jnp.where(fresh, total, sums[place] + total)

        second_plane(x, ext, first, src2, lane, emit)
        out_copy(x).start()
        return carry

    lax.fori_loop(1, 7, plane, 0)
    coarse = [crate[i] for i in range(15)]

    def block(b, carry):
        destinations(sums.at[b], coarse, raw, up, down, send, b)
        return carry

    lax.fori_loop(1, 3, block, 0)
    for x in range(1, 7):
        out_copy(x).wait()


def outer_two_kernel(
    ext, first, src2, crate, ra, rb, sums_in, send_in, fine_in,
    send, fine_out, sums, planes, raw, up, down, sem,
):
    _, _, has_left, has_right = edges()
    lane = iota((40, 128), 1)
    clear(raw, up, down)
    sides = (
        (0, (1, arrived_face(ra, rb, True, has_left))),
        (7, (-1, arrived_face(ra, rb, False, has_right))),
    )
    copies = []
    for n, (x, outer) in enumerate(sides):

        def emit(q, value, before):
            planes[n, q] = value[0:32]
            rows = pl.ds(40 * q, 40)
            sums[n, rows] = value + before + sums_in[3 * n, rows]

        second_plane(x, ext, first, src2, lane, emit, outer)
        copy = pltpu.make_async_copy(planes.at[n], fine_out.at[:, x], sem.at[n])
        copy.start()
        copies.append(copy)
    coarse = [crate[i] for i in range(15)]
    for n in range(2):
        destinations(sums.at[n], coarse, raw, up, down, send, 3 * n)
    for copy in copies:
        copy.wait()


def coarse_kernel(
    got, crate, cp, c_solid, c_cov, ru, rd, ra, rb, out, turned, walled, source, message
):
    has_prev, has_next, has_left, has_right = edges()
    coarse = [crate[i] for i in range(15)]
    for k in range(2):
        for n in range(4):
            turned[k, 128 * n : 128 * n + 128] = got[pl.ds(2 * n + k, 128, stride=8)].T

    goes_up = upwards()
    for i in range(13):
        first, second = ra[X_COARSE + i], rb[X_COARSE + i]
        message[0, i] = jnp.where(goes_up, first, second)
        message[1, i] = jnp.where(goes_up, second, first)

    def pick(code, here, there):
        return jnp.where(code > 1.5, here, jnp.where(code > 0.5, there, WALL))

    def arrived(from_, place):
        return from_[Y_COARSE + place : Y_COARSE + place + 1]

    for k in range(2):
        for t in range(2):
            rows = pl.ds(8 * t, 8)
            fluid = c_solid[k, rows] == 0
            covered = c_cov[k, rows] == 1
            old = []
            for q in range(19):
                start = 16 * q + 8 * t
                old.append(jnp.where(covered, turned[k, start : start + 8], cp[q, k, rows]))
            post = collide(old, coarse)
            for q in range(19):
                value = jnp.where(fluid, post[q], old[q])
                source[q, k + 1, rows] = value
                walled[q, k + 1, rows] = jnp.where(fluid, value, WALL)
        prev_code = arrived(ru, 6 * k + 5) * has_prev
        next_code = arrived(rd, 6 * k + 5) * has_next
        for i in range(5):
            walled[YP[i], k + 1, 23:24] = pick(
                prev_code, turned[k, 304 + i : 305 + i], arrived(ru, 6 * k + i)
            )
            walled[YM[i], k + 1, 16:17] = pick(
                next_code, turned[k, 309 + i : 310 + i], arrived(rd, 6 * k + i)
            )
        values, from_, z, inside = ((ZP, message.at[0], 0, has_left), (ZM, message.at[1], 3, has_right))[k]
        prev_q, next_q = ((15, 18), (17, 16))[k]
        for t in range(2):
            code = from_[10 + t] * inside
            for i in range(5):
                start = 384 + 16 * i + 8 * t
                walled[values[i], z, 8 * t : 8 * t + 8] = pick(
                    code, turned[k, start : start + 8], from_[2 * i + t]
                )
        walled[prev_q, z, 23:24] = pick(
            from_[12, 2:3] * inside, turned[k, 464:465], from_[12, 0:1]
        )
        walled[next_q, z, 16:17] = pick(
            from_[12, 3:4] * inside, turned[k, 465:466], from_[12, 1:2]
        )

    lane = iota((16, 128), 1)
    for z in (1, 2):
        fluid = c_solid[z - 1] == 0
        for q in range(19):
            cx, cy, cz = VEL[q]
            value = walled[q, z - cz]
            if cy:
                value = pltpu.roll(value, cy % 24, 0)
            value = value[0:16]
            if cx:
                value = pltpu.roll(value, cx % 128, 1)
            open_ = value < WALL_TEST
            if cx:
                open_ = open_ & (lane != (0 if cx == 1 else 127))
            bounced = jnp.where(open_, value, source[OPP[q], z, 0:16])
            out[q, z - 1] = jnp.where(fluid, bounced, source[q, z, 0:16])


def shape(*dims):
    return jax.ShapeDtypeStruct(dims, F32)


SMEM = pl.BlockSpec(memory_space=pltpu.SMEM)
VMEM = pl.BlockSpec(memory_space=pltpu.VMEM)
HBM = pl.BlockSpec(memory_space=pltpu.HBM)


def call(kernel, name, ins, outs, scratch=(), aliases=None, cells=0):
    return pl.pallas_call(
        kernel,
        out_shape=[shape(*dims) for dims, _ in outs],
        in_specs=ins,
        out_specs=[place for _, place in outs],
        scratch_shapes=[s if not isinstance(s, tuple) else pltpu.VMEM(s, F32) for s in scratch],
        input_output_aliases=aliases or {},
        compiler_params=pltpu.CompilerParams(vmem_limit_bytes=24 * MIB),
        cost_estimate=pl.CostEstimate(
            flops=300 * cells, bytes_accessed=160 * cells, transcendentals=cells
        ),
        name=name,
    )


def over_quad(up, down):
    count = lax.axis_size("quad")
    ring = [(i, (i + 1) % count) for i in range(count)]
    return lax.ppermute(up, "quad", ring), lax.ppermute(down, "quad", [(j, i) for i, j in ring])


def over_wide(first, second):
    wide, quad = lax.axis_size("wide"), lax.axis_size("quad")
    path = []
    for q in range(0, quad, 2):
        line = [(w, q) for w in range(wide)] + [(w, q + 1) for w in reversed(range(wide))]
        path += list(zip(line, line[1:] + line[:1]))
    path = [(a[0] * quad + a[1], b[0] * quad + b[1]) for a, b in path]
    axes = ("wide", "quad")
    return (
        lax.ppermute(first, axes, path),
        lax.ppermute(second, axes, [(j, i) for i, j in path]),
    )


def shards(fine_pops, coarse_pops, fine_solid, coarse_solid, fine_active, coarse_covered, rates):
    i32 = jnp.int32
    dma = pltpu.SemaphoreType.DMA
    ext_shape, pops_shape = (20, 8, 40, 128), (19, 8, 40, 128)
    yu, yd, zu, zd = call(
        rows_kernel,
        "collide_rows",
        [HBM] * 7,
        [((Y_ROWS, 128), VMEM)] * 2 + [((6, 16, 128), VMEM)] * 2,
        [
            pltpu.SMEM((15,), F32),
            (8, 19, 8, 128),
            (8, 19, 8, 128),
            pltpu.VMEM((8, 8, 128), i32),
            pltpu.VMEM((8, 8, 128), i32),
            pltpu.VMEM((2, 8, 32), i32),
            (19, 2, 16, 128),
            pltpu.VMEM((2, 16, 128), i32),
            pltpu.VMEM((2, 16, 128), i32),
            dma((23,)),
        ],
    )(
        *[
            pltpu.with_memory_space_constraint(a, pltpu.HBM)
            for a in (
                rates, fine_pops, fine_solid, fine_active, coarse_pops, coarse_solid, coarse_covered
            )
        ]
    )
    ru, rd = over_quad(yu, yd)
    ext, crate = call(
        cells_kernel,
        "collide_cells",
        [SMEM] + [VMEM] * 3,
        [(ext_shape, VMEM), ((15, 8, 128), VMEM)],
        [(2, 32, 128)],
        cells=32768,
    )(rates, fine_pops, fine_solid, fine_active)
    pa, pb = call(
        faces_kernel,
        "pack_faces",
        [VMEM] * 5,
        [((X_ALL, 8, 128), VMEM)] * 2,
        [(2, 8, 128), (2, 5, 8, 128)],
    )(ext, zu, zd, ru, rd)
    ra, rb = over_wide(pa, pb)
    ext, first, src2 = call(
        inner_one_kernel,
        "substep_one_inner",
        [SMEM] + [VMEM] * 3,
        [(ext_shape, VMEM), (pops_shape, VMEM), (pops_shape, VMEM)],
        cells=24576,
    )(rates, ext, ru, rd)
    first, src2, pa, pb = call(
        outer_one_kernel,
        "substep_one_faces",
        [SMEM] + [VMEM] * 5,
        [(pops_shape, VMEM)] * 2 + [((X_TILES, 8, 128), VMEM)] * 2,
        aliases={4: 0, 5: 1},
    )(rates, ext, ra, rb, first, src2)
    ra2, rb2 = over_wide(pa, pb)
    work = [(384, 128), (128, 128), (128, 128)]
    fine_out, sums, send = call(
        inner_two_kernel,
        "substep_two_inner",
        [VMEM] * 4,
        [((19, 8, 32, 128), HBM), ((4, 768, 128), VMEM), ((1024, 128), VMEM)],
        [(6, 19, 32, 128)] + work + [dma((6,))],
        cells=24576,
    )(ext, first, src2, crate)
    send, fine_out = call(
        outer_two_kernel,
        "substep_two_faces",
        [VMEM] * 8 + [HBM],
        [((1024, 128), VMEM), ((19, 8, 32, 128), HBM)],
        [(2, 768, 128), (2, 19, 32, 128)] + work + [dma((2,))],
        aliases={7: 0, 8: 1},
    )(ext, first, src2, crate, ra2, rb2, sums, send, fine_out)
    got = lax.all_to_all(send, "wide", split_axis=0, concat_axis=0, tiled=True)
    (coarse_out,) = call(
        coarse_kernel,
        "coarse_step",
        [VMEM] * 9,
        [((19, 2, 16, 128), VMEM)],
        [(2, 512, 128), (19, 4, 24, 128), (19, 4, 24, 128), (2, 13, 8, 128)],
    )(got, crate, coarse_pops, coarse_solid, coarse_covered, ru, rd, ra, rb)
    return (fine_out, coarse_out)


def solution(mesh):
    in_specs = (
        P(None, "wide", "quad", None),
        P(None, "wide", "quad", None),
        P("wide", "quad", None),
        P("wide", "quad", None),
        P("wide", "quad", None),
        P("wide", "quad", None),
        P(),
    )
    out_specs = (P(None, "wide", "quad", None), P(None, "wide", "quad", None))
    return jax.shard_map(shards, mesh=mesh, in_specs=in_specs, out_specs=out_specs, check_vma=False)
```

```python
import functools

import jax
import jax.numpy as jnp
from jax import lax
from jax.experimental import pallas as pl
from jax.experimental.pallas import tpu as pltpu
from jax.sharding import PartitionSpec as P

VEL = [
    (0, 0, 0),
    (1, 0, 0),
    (-1, 0, 0),
    (0, 1, 0),
    (0, -1, 0),
    (0, 0, 1),
    (0, 0, -1),
    (1, 1, 0),
    (-1, -1, 0),
    (1, -1, 0),
    (-1, 1, 0),
    (1, 0, 1),
    (-1, 0, -1),
    (1, 0, -1),
    (-1, 0, 1),
    (0, 1, 1),
    (0, -1, -1),
    (0, 1, -1),
    (0, -1, 1),
]
OPP = [0, 2, 1, 4, 3, 6, 5, 8, 7, 10, 9, 12, 11, 14, 13, 16, 15, 18, 17]


def moving(axis, sign):
    return [q for q in range(19) if VEL[q][axis] == sign]


XP, XM = moving(0, 1), moving(0, -1)
YP, YM = moving(1, 1), moving(1, -1)
ZP, ZM = moving(2, 1), moving(2, -1)
WALL = 1e30
WALL_TEST = 1e29
F32 = jnp.float32
MIB = 1 << 20

FACES = (0, 7)
INNER = (1, 2, 3, 4, 5, 6)
NEXT = ((1, XM), (6, XP))
ACROSS = [q for q in range(19) if VEL[q][0] == 0]
Y_COARSE = 130
Y_NEXT = 142
Y_FACES = 176
Y_INNER = 392
X_COARSE = 100
X_ALL = X_COARSE + 13
CHUNK = 25

FACTOR = [0.25] * 3 + [0.5] * 3 + [0.25] * 9

def collide(f, rate):
    r_xy, r_xz, r_yz, r_xx, r_yy, r_zz = rate[:6]
    r_xyy, r_xzz, r_yxx, r_yzz, r_zxx, r_zyy, r_xxyy, r_xxzz, r_yyzz = rate[6:]
    sx, dx = f[1] + f[2], f[1] - f[2]
    sy, dy = f[3] + f[4], f[3] - f[4]
    sz, dz = f[5] + f[6], f[5] - f[6]

    def plane(i):
        a, b = f[i] + f[i + 1], f[i + 2] + f[i + 3]
        c, d = f[i] - f[i + 1], f[i + 2] - f[i + 3]
        return a + b, a - b, c + d, c - d

    m_xxyy, m_xy, m_xyy, m_yxx = plane(7)
    m_xxzz, m_xz, m_xzz, m_zxx = plane(11)
    m_yyzz, m_yz, m_yzz, m_zyy = plane(15)
    m_xx = sx + (m_xxyy + m_xxzz)
    m_yy = sy + (m_xxyy + m_yyzz)
    m_zz = sz + (m_xxzz + m_yyzz)
    jx = dx + (m_xyy + m_xzz)
    jy = dy + (m_yxx + m_yzz)
    jz = dz + (m_zxx + m_zyy)
    rho = (f[0] + sx) + (sy + sz) + ((m_xxyy + m_xxzz) + m_yyzz)
    inv = 1.0 / rho
    ux, uy, uz = jx * inv, jy * inv, jz * inv
    xx, yy, zz = jx * ux, jy * uy, jz * uz
    third = rho * (1.0 / 3.0)
    ninth = rho * (1.0 / 9.0)
    jx3, jy3, jz3 = jx * (1.0 / 3.0), jy * (1.0 / 3.0), jz * (1.0 / 3.0)
    xx3, yy3, zz3 = xx * (1.0 / 3.0), yy * (1.0 / 3.0), zz * (1.0 / 3.0)
    h_xx = (m_xx - third - xx) * r_xx
    h_yy = (m_yy - third - yy) * r_yy
    h_zz = (m_zz - third - zz) * r_zz
    post = [None] * 19

    def diagonal(i, fourth, cross, first, second):
        p, m = fourth + cross, fourth - cross
        s, d = first + second, first - second
        post[i] = f[i] - (p + s)
        post[i + 1] = f[i + 1] - (p - s)
        post[i + 2] = f[i + 2] - (m + d)
        post[i + 3] = f[i + 3] - (m - d)

    a_xy = (m_xxyy - ninth - (xx3 + yy3 - 0.5 * zz3)) * r_xxyy
    a_xz = (m_xxzz - ninth - (xx3 + zz3 - 0.5 * yy3)) * r_xxzz
    a_yz = (m_yyzz - ninth - (yy3 + zz3 - 0.5 * xx3)) * r_yyzz
    c_xyy, c_yxx = (m_xyy - jx3) * r_xyy, (m_yxx - jy3) * r_yxx
    c_xzz, c_zxx = (m_xzz - jx3) * r_xzz, (m_zxx - jz3) * r_zxx
    c_yzz, c_zyy = (m_yzz - jy3) * r_yzz, (m_zyy - jz3) * r_zyy
    diagonal(7, a_xy, (m_xy - jx * uy) * r_xy, c_xyy, c_yxx)
    diagonal(11, a_xz, (m_xz - jx * uz) * r_xz, c_xzz, c_zxx)
    diagonal(15, a_yz, (m_yz - jy * uz) * r_yz, c_yzz, c_zyy)

    def straight(i, h, a, c):
        p, n = h - 2.0 * a, 2.0 * c
        post[i] = f[i] - (p - n)
        post[i + 1] = f[i + 1] - (p + n)

    straight(1, h_xx, a_xy + a_xz, c_xyy + c_xzz)
    straight(3, h_yy, a_xy + a_yz, c_yxx + c_yzz)
    straight(5, h_zz, a_xz + a_yz, c_zxx + c_zyy)
    post[0] = f[0] + (2.0 * (h_xx + h_yy + h_zz) - 4.0 * (a_xy + a_xz + a_yz))
    return post


def iota(shape, axis):
    return lax.broadcasted_iota(jnp.int32, shape, axis)


def write_rates(rates, fine, coarse):
    for i in range(15):
        rate = jnp.full((8, 128), rates[i], F32)
        fine[i] = rate * FACTOR[i]
        coarse[i] = FACTOR[i] / (2.0 / rate - 0.5)


def read_rates(ref):
    return [ref[i] for i in range(15)]


def wall_where(code, value):
    return jnp.where(code > 0.5, value, WALL)


def grown_blocks(active):
    grow = (iota((32, 128), 1) // 4 == iota((32, 128), 0)).astype(F32)
    return jnp.dot(active.astype(F32), grow, preferred_element_type=F32)


def edges():
    quad, wide = lax.axis_index("quad"), lax.axis_index("wide")
    return (
        (quad > 0).astype(F32),
        (quad < lax.axis_size("quad") - 1).astype(F32),
        (wide > 0).astype(F32),
        (wide < lax.axis_size("wide") - 1).astype(F32),
    )


def collide_plane(x, f, solid, on, fine, ext):
    for t in range(4):
        rows = pl.ds(8 * t, 8)
        old = [f[q, rows] for q in range(19)]
        fluid = solid[x, rows] == 0
        live = fluid & (on[x // 4, rows] > 0.5)
        post = collide(old, fine)
        for q in range(19):
            ext[q, x, rows] = jnp.where(live, post[q], old[q])
        ext[19, x, rows] = jnp.where(fluid, 1.0 + on[x // 4, rows], 0.0)


def grow(active, on):
    grow_y = (iota((32, 8), 0) // 4 == iota((32, 8), 1)).astype(F32)
    for b in range(2):
        on[b] = jnp.dot(grow_y, grown_blocks(active[b]), preferred_element_type=F32)


def pack_rows(planes, ext, yu, yd):
    fourth = 60 * len(planes)
    for n, x in enumerate(planes):
        for q in range(20):
            start = 60 * n + 3 * q
            yu[start : start + 3] = ext[q, x, 24:32][5:8]
            yd[start : start + 3] = ext[q, x, 0:8][0:3]
        for i in range(5):
            start = fourth + len(planes) * i + n
            yu[start : start + 1] = wall_where(ext[19, x, 24:32], ext[YP[i], x, 24:32])[4:5]
            yd[start : start + 1] = wall_where(ext[19, x, 0:8], ext[YM[i], x, 0:8])[3:4]


def faces_first_kernel(
    rates_in, f, solid_in, active_in, cp, c_solid, c_cov,
    ext, yu, yd, zu, zd, solid, on, frate, crate,
    rates, held, active, cps, c_solids, c_covs, sems,
):
    small = [
        pltpu.make_async_copy(rates_in, rates, sems.at[0]),
        pltpu.make_async_copy(solid_in, solid, sems.at[1]),
        pltpu.make_async_copy(active_in, active, sems.at[2]),
    ]
    coarse_copies = [
        pltpu.make_async_copy(cp, cps, sems.at[3]),
        pltpu.make_async_copy(c_solid, c_solids, sems.at[4]),
        pltpu.make_async_copy(c_cov, c_covs, sems.at[5]),
    ]
    planes = [
        pltpu.make_async_copy(f.at[:, x], held.at[n], sems.at[6 + n])
        for n, x in enumerate((0, 7, 1, 6))
    ]
    for copy in small + planes + coarse_copies:
        copy.start()
    for copy in small:
        copy.wait()
    write_rates(rates, frate, crate)
    fine = read_rates(frate)
    grow(active, on)
    for n, x in enumerate((0, 7, 1, 6)):
        planes[n].wait()
        collide_plane(x, held.at[n], solid, on, fine, ext)
    pack_rows(FACES, ext, yu, yd)
    for e, (x, values) in enumerate(NEXT):
        for i, q in enumerate(values):
            start = Y_NEXT + 15 * e + 3 * i
            high = wall_where(ext[19, x, 24:32], ext[q, x, 24:32])
            low = wall_where(ext[19, x, 0:8], ext[q, x, 0:8])
            yu[start : start + 3] = high[5:8]
            yd[start : start + 3] = low[0:3]
            fourth = Y_NEXT + 30 + e
            if q in YP:
                yu[fourth : fourth + 1] = high[4:5]
            if q in YM:
                yd[fourth : fourth + 1] = low[3:4]
    for copy in coarse_copies:
        copy.wait()
    coarse = read_rates(crate)
    for z in range(2):
        for t in range(2):
            rows = pl.ds(8 * t, 8)
            post = collide([cps[q, z, rows] for q in range(19)], coarse)
            code = jnp.where(c_solids[z, rows] == 0, 1.0 + c_covs[z, rows].astype(F32), 0.0)
            values, to = (ZP, zu) if z == 1 else (ZM, zd)
            for i in range(5):
                to[i, rows] = post[values[i]]
            to[5, rows] = code
            values, to, row = (YM, yd, 0) if t == 0 else (YP, yu, 7)
            for i in range(6):
                place = Y_COARSE + 6 * z + i
                value = code if i == 5 else post[values[i]]
                to[place : place + 1] = value[row : row + 1]


def inner_first_kernel(frate, f, solid, on, ext_in, ext, yu, yd):
    fine = read_rates(frate)

    def plane(x, carry):
        collide_plane(x, f.at[:, x], solid, on, fine, ext)
        return carry

    lax.fori_loop(2, 6, plane, 0)
    pack_rows(INNER, ext, yu, yd)


def fill_rows(q, planes, n, ru, rd, to):
    start = 60 * n + 3 * q
    to[0:3] = rd[start : start + 3]
    to[5:8] = ru[start : start + 3]
    fourth = 60 * len(planes) + n
    if q in YM:
        place = fourth + len(planes) * YM.index(q)
        to[3:4] = rd[place : place + 1]
    if q in YP:
        place = fourth + len(planes) * YP.index(q)
        to[4:5] = ru[place : place + 1]


def fill_code(n, ru, rd, to, has_prev, has_next):
    start = 60 * n + 57
    to[0:3] = rd[start : start + 3] * has_next
    to[5:8] = ru[start : start + 3] * has_prev
    to[3:4] = jnp.full((1, 128), has_next, F32)
    to[4:5] = jnp.full((1, 128), has_prev, F32)


def upwards():
    return lax.axis_index("wide") % 2 == 0


def face_planes_kernel(ext, held):
    for face, x in enumerate(FACES):
        for q in range(20):
            held[q, face, 0:32] = ext[q, x, 0:32]
        near, values = NEXT[face]
        for i, q in enumerate(values):
            held[20 + i, face, 0:32] = wall_where(ext[19, near, 0:32], ext[q, near, 0:32])


def faces_kernel(planes, zu, zd, ru, rd, pa, pb, held, beyond, tile, both):
    has_prev, has_next, _, _ = edges()
    lane = iota((40, 128), 1)
    inside = jnp.where(iota((8, 128), 0) < 4, has_next, has_prev) > 0.5
    for face, x in enumerate(FACES):
        place = jnp.where(upwards() == (x == 7), 0, 1)
        for q in range(19):
            held[q, 0, 0:32] = planes[q, face, 0:32]
            fill_rows(q, FACES, face, ru, rd, held.at[q, 0, 32:40])
        held[19, 0, 0:32] = planes[19, face, 0:32]
        fill_code(face, ru, rd, held.at[19, 0, 32:40], has_prev, has_next)
        values = NEXT[face][1]
        for i, q in enumerate(values):
            beyond[i, 0:32] = planes[20 + i, face, 0:32]
            start = Y_NEXT + 15 * face + 3 * i
            fourth = Y_NEXT + 30 + face
            tile[0:3] = rd[start : start + 3]
            tile[5:8] = ru[start : start + 3]
            if q in YM:
                tile[3:4] = rd[fourth : fourth + 1]
            if q in YP:
                tile[4:5] = ru[fourth : fourth + 1]
            beyond[i, 32:40] = jnp.where(inside, tile[...], WALL)
        code = held[19, 0]
        live, open_cells = code > 1.5, {0: code > 0.5}
        outer = (VEL[values[0]][0], lambda q: beyond[values.index(q)])
        for i in range(20):
            if i < 14:
                q = (ACROSS + values)[i]
                part = streamed(q, 0, held, open_cells, live, lane, outer)
            elif i < 19:
                part = wall_where(code, held[values[i - 14], 0])
            else:
                part = code
            for t in range(5):
                both[place, 5 * i + t] = part[8 * t : 8 * t + 8]
        z, arriving, leaving, from_ = ((0, 17, 16, zd), (1, 15, 18, zu))[face]
        for i in range(6):
            for t in range(2):
                both[place, X_COARSE + 2 * i + t] = from_[i, 8 * t : 8 * t + 8]

        def arrived(rows, i):
            row = Y_COARSE + 6 * z + i
            return rows[row : row + 1]

        tile[0:1] = arrived(ru, YP.index(arriving))
        tile[1:2] = arrived(rd, YM.index(leaving))
        tile[2:3] = arrived(ru, 5) * has_prev
        tile[3:4] = arrived(rd, 5) * has_next
        both[place, X_COARSE + 12] = tile[...]
    pa[...] = both[0]
    pb[...] = both[1]


def streamed(q, x, values, open_cells, live, lane, outer=None):
    cx, cy, cz = VEL[q]
    if q == 0:
        return values[0, x]
    if cx and outer is not None and outer[0] == cx:
        value = outer[1](q)
    else:
        value = jnp.where(open_cells[cx], values[q, x - cx], WALL)
    if cy:
        value = pltpu.roll(value, cy % 40, 0)
    if cz:
        value = pltpu.roll(value, cz % 128, 1)
    open_ = value < WALL_TEST
    if cz:
        open_ = open_ & (lane != (0 if cz == 1 else 127))
    return jnp.where(live, jnp.where(open_, value, values[OPP[q], x]), values[q, x])


def step_plane(x, ext, first, src2, fine, lane, outer=None):
    open_cells = {}
    for cx in (-1, 0, 1):
        if outer is None or outer[0] != cx:
            open_cells[cx] = ext[19, x - cx] > 0.5
    live = ext[19, x] > 1.5
    for q in range(19):
        first[q, x] = streamed(q, x, ext, open_cells, live, lane, outer)
    for t in range(5):
        rows = pl.ds(8 * t, 8)
        live_t = ext[19, x, rows] > 1.5
        old = [first[q, x, rows] for q in range(19)]
        post = collide(old, fine)
        for q in range(19):
            src2[q, x, rows] = jnp.where(live_t, post[q], old[q])


def fill_kernel(ext_in, ru, rd, ru2, rd2, ext):
    has_prev, has_next, _, _ = edges()
    for planes, up, down in ((FACES, ru, rd), (INNER, ru2, rd2)):
        for n, x in enumerate(planes):
            for q in range(19):
                fill_rows(q, planes, n, up, down, ext.at[q, x, 32:40])
            fill_code(n, up, down, ext.at[19, x, 32:40], has_prev, has_next)


def second_plane(x, ext, first, src2, lane, emit, outer=None):
    open_cells = {}
    for cx in (-1, 0, 1):
        if outer is None or outer[0] != cx:
            open_cells[cx] = ext[19, x - cx] > 0.5
    live = ext[19, x] > 1.5
    for q in range(19):
        emit(q, streamed(q, x, src2, open_cells, live, lane, outer), first[q, x])


def own_planes():
    z_pair = iota((32, 128), 1) // 2
    plane = 2 * iota((32, 128), 0)
    return [jnp.where(z_pair == plane + k, 0.0625, 0.0) for k in range(2)]


def picked(rows, cells):
    return lax.dot_general(
        rows,
        cells,
        (((1,), (1,)), ((), ())),
        precision=lax.Precision.HIGHEST,
        preferred_element_type=F32,
    )


def destinations(sums, coarse, raw, mixed, rest, send, b):
    even = iota((8, 128), 1) % 2 == 0

    def alone(value, shift):
        value = jnp.where(even, 16.0 * value, 0.0)
        return pltpu.roll(value, 2 * shift % 128, 1) if shift else value

    for t in range(3):
        cells = []
        for q in range(19):
            start = 40 * q + 16 * t
            value = sums[pl.ds(start, 8, stride=2)] + sums[pl.ds(start + 1, 8, stride=2)]
            if t < 2:
                place = 16 * q + 8 * t
                if q < 16:
                    raw[place : place + 8] = value
                else:
                    mixed[0, place - 256 : place - 248] = value
                    mixed[1, place - 256 : place - 248] = value
            cells.append((value + pltpu.roll(value, 127, 1)) * 0.0625)
        post = collide(cells, coarse)
        if t < 2:
            for i in range(5):
                place = 48 + 16 * i + 8 * t
                mixed[0, place : place + 8] = alone(post[ZP[i]], 1)
                mixed[1, place : place + 8] = alone(post[ZM[i]], -1)
        else:
            last = [alone(post[q], 0)[3:4] for q in YP] + [alone(post[q], 0)[0:1] for q in YM]
            for k in range(2):
                corners = ((15, 18), (17, 16))[k]
                shift = (1, -1)[k]
                here = last + [alone(post[corners[0]], shift)[3:4], alone(post[corners[1]], shift)[0:1]]
                for i in range(12):
                    rest[pl.ds(64 * k + 12 * b + i, 1)] = here[i]
    planes = own_planes()
    both = jnp.concatenate(planes, axis=0)
    for n in range(2):
        got = picked(both, raw[128 * n : 128 * n + 128])
        for k in range(2):
            send[pl.ds(6 * b + 2 * k + n, 32, stride=CHUNK)] = got[32 * k : 32 * k + 32]
    for k in range(2):
        send[pl.ds(6 * b + 4 + k, 32, stride=CHUNK)] = picked(planes[k], mixed[k])


def inner_kernel(
    frate, ext, crate, first, src2, fine_out, send, rest, planes, sums, raw, mixed, sem
):
    fine = read_rates(frate)
    lane = iota((40, 128), 1)
    rest[...] = jnp.zeros(rest.shape, F32)

    def substep_one(x, carry):
        step_plane(x, ext, first, src2, fine, lane)
        return carry

    lax.fori_loop(1, 7, substep_one, 0)

    def out_copy(x):
        return pltpu.make_async_copy(planes.at[x - 2], fine_out.at[:, x], sem.at[x - 2])

    def pair(b, carry):
        for e in range(2):
            x = 2 * b + e

            def emit(q, value, before):
                planes[x - 2, q] = value[0:32]
                rows = pl.ds(40 * q, 40)
                total = value + before
                sums[b - 1, rows] = total if e == 0 else sums[b - 1, rows] + total

            second_plane(x, ext, first, src2, lane, emit)
            out_copy(x).start()
        return carry

    lax.fori_loop(1, 3, pair, 0)
    coarse = read_rates(crate)
    for b in (1, 2):
        destinations(sums.at[b - 1], coarse, raw, mixed, rest, send, b)
    for x in range(2, 6):
        out_copy(x).wait()


def side(
    left, message, inside, frate, ext, crate, first, src2, send, rest, fine_out,
    planes, sums, raw, mixed, before, outside, sem,
):
    fine = read_rates(frate)
    lane = iota((40, 128), 1)
    entering, leaving = (XP, XM) if left else (XM, XP)
    cx = 1 if left else -1
    x, near, b = (0, 1, 0) if left else (7, 6, 3)

    def arrived(i):
        return message[5 * i : 5 * i + 5].reshape(40, 128)

    def part(i):
        return jnp.where(inside > 0.5, arrived(i), WALL)

    code = arrived(19)
    for i, q in enumerate(ACROSS + entering):
        before[q] = arrived(i)
    open_cells = ext[19, x] > 0.5
    for q in leaving:
        _, cy, cz = VEL[q]
        value = jnp.where(open_cells, ext[q, x], WALL)
        if cy:
            value = pltpu.roll(value, cy % 40, 0)
        if cz:
            value = pltpu.roll(value, cz % 128, 1)
        open_ = value < WALL_TEST
        if cz:
            open_ = open_ & (lane != (0 if cz == 1 else 127))
        before[q] = jnp.where(open_, value, arrived(14 + entering.index(OPP[q])))
    for t in range(5):
        rows = pl.ds(8 * t, 8)
        code_t = message[95 + t] * inside
        old = [before[q, rows] for q in range(19)]
        post = collide(old, fine)
        for i, q in enumerate(entering):
            value = jnp.where(code_t > 1.5, post[q], old[q])
            outside[i, rows] = wall_where(code_t, value)
    step_plane(
        x, ext, first, src2, fine, lane, (cx, lambda q: part(14 + entering.index(q)))
    )
    copies = []
    for e, (plane, outer) in enumerate(
        ((x, (cx, lambda q: outside[entering.index(q)])), (near, None))
    ):

        def emit(q, value, earlier):
            planes[e, q] = value[0:32]
            rows = pl.ds(40 * q, 40)
            total = value + earlier
            sums[rows] = total if e == 0 else sums[rows] + total

        second_plane(plane, ext, first, src2, lane, emit, outer)
        copy = pltpu.make_async_copy(planes.at[e], fine_out.at[:, plane], sem.at[e])
        copy.start()
        copies.append(copy)
    destinations(sums, read_rates(crate), raw, mixed, rest, send, b)
    for copy in copies:
        copy.wait()


def side_kernel(
    second, frate, ext, crate, message, first_in, src2_in, send_in, rest_in, fine_in,
    first, src2, send, rest, fine_out, planes, sums, raw, mixed, before, outside, sem,
):
    _, _, has_left, has_right = edges()
    on_left = upwards() if second else jnp.logical_not(upwards())
    refs = (
        frate, ext, crate, first, src2, send, rest, fine_out,
        planes, sums, raw, mixed, before, outside, sem,
    )

    @pl.when(on_left)
    def _():
        side(True, message, has_left, *refs)

    @pl.when(jnp.logical_not(on_left))
    def _():
        side(False, message, has_right, *refs)

    if second:
        of_first, of_second = (picked(plane, rest[...]) for plane in own_planes())
        send[pl.ds(CHUNK - 1, 32, stride=CHUNK)] = jnp.where(
            iota((32, 128), 1) < 64, of_first, of_second
        )


def coarse_kernel(
    got, crate, cp, c_solid, c_cov, ru, rd, ra, rb, out, mesh, turned, rest, walled, source, message
):
    has_prev, has_next, has_left, has_right = edges()
    coarse = read_rates(crate)
    for m in range(6):
        for b in range(4):
            mesh[m, pl.ds(b, 32, stride=4)] = got[pl.ds(6 * b + m, 32, stride=CHUNK)]
    left = got[pl.ds(CHUNK - 1, 32, stride=CHUNK)]
    for b in range(4):
        mesh[6, pl.ds(b, 32, stride=4)] = pltpu.roll(left, -12 * b % 128, 1) if b else left
    for k in range(2):
        for n, m in enumerate((2 * k, 2 * k + 1, 4 + k)):
            turned[k, 128 * n : 128 * n + 128] = mesh[m].T
    rest[...] = mesh[6].T

    goes_up = upwards()
    for i in range(13):
        first, second = ra[X_COARSE + i], rb[X_COARSE + i]
        message[0, i] = jnp.where(goes_up, second, first)
        message[1, i] = jnp.where(goes_up, first, second)

    def pick(code, here, there):
        return jnp.where(code > 1.5, here, jnp.where(code > 0.5, there, WALL))

    def arrived(from_, place):
        return from_[Y_COARSE + place : Y_COARSE + place + 1]

    for k in range(2):
        for t in range(2):
            rows = pl.ds(8 * t, 8)
            fluid = c_solid[k, rows] == 0
            covered = c_cov[k, rows] == 1
            old = []
            for q in range(19):
                start = 16 * q + 8 * t
                old.append(jnp.where(covered, turned[k, start : start + 8], cp[q, k, rows]))
            post = collide(old, coarse)
            for q in range(19):
                value = jnp.where(fluid, post[q], old[q])
                source[q, k + 1, rows] = value
                walled[q, k + 1, rows] = jnp.where(fluid, value, WALL)
        prev_code = arrived(ru, 6 * k + 5) * has_prev
        next_code = arrived(rd, 6 * k + 5) * has_next
        for i in range(5):
            walled[YP[i], k + 1, 23:24] = pick(
                prev_code, rest[64 * k + i : 64 * k + i + 1], arrived(ru, 6 * k + i)
            )
            walled[YM[i], k + 1, 16:17] = pick(
                next_code, rest[64 * k + 5 + i : 64 * k + 6 + i], arrived(rd, 6 * k + i)
            )
        values, from_, z, inside = ((ZP, message.at[0], 0, has_left), (ZM, message.at[1], 3, has_right))[k]
        prev_q, next_q = ((15, 18), (17, 16))[k]
        for t in range(2):
            code = from_[10 + t] * inside
            for i in range(5):
                start = 304 + 16 * i + 8 * t
                walled[values[i], z, 8 * t : 8 * t + 8] = pick(
                    code, turned[k, start : start + 8], from_[2 * i + t]
                )
        walled[prev_q, z, 23:24] = pick(
            from_[12, 2:3] * inside, rest[64 * k + 10 : 64 * k + 11], from_[12, 0:1]
        )
        walled[next_q, z, 16:17] = pick(
            from_[12, 3:4] * inside, rest[64 * k + 11 : 64 * k + 12], from_[12, 1:2]
        )

    lane = iota((16, 128), 1)
    for z in (1, 2):
        fluid = c_solid[z - 1] == 0
        for q in range(19):
            cx, cy, cz = VEL[q]
            value = walled[q, z - cz]
            if cy:
                value = pltpu.roll(value, cy % 24, 0)
            value = value[0:16]
            if cx:
                value = pltpu.roll(value, cx % 128, 1)
            open_ = value < WALL_TEST
            if cx:
                open_ = open_ & (lane != (0 if cx == 1 else 127))
            bounced = jnp.where(open_, value, source[OPP[q], z, 0:16])
            out[q, z - 1] = jnp.where(fluid, bounced, source[q, z, 0:16])


VMEM = pl.BlockSpec(memory_space=pltpu.VMEM)
HBM = pl.BlockSpec(memory_space=pltpu.HBM)


def call(kernel, name, ins, outs, scratch=(), aliases=None, weight=1):
    return pl.pallas_call(
        kernel,
        out_shape=[jax.ShapeDtypeStruct(out[0], (out + (F32,))[2]) for out in outs],
        in_specs=ins,
        out_specs=[out[1] for out in outs],
        scratch_shapes=[s if not isinstance(s, tuple) else pltpu.VMEM(s, F32) for s in scratch],
        input_output_aliases=aliases or {},
        compiler_params=pltpu.CompilerParams(vmem_limit_bytes=24 * MIB),
        cost_estimate=pl.CostEstimate(
            flops=weight * 1_000_000_000, bytes_accessed=0, transcendentals=0
        ),
        name=name,
    )


def over_quad(up, down):
    count = lax.axis_size("quad")
    ring = [(i, (i + 1) % count) for i in range(count)]
    return lax.ppermute(up, "quad", ring), lax.ppermute(down, "quad", [(j, i) for i, j in ring])


def over_wide(first, second):
    wide, quad = lax.axis_size("wide"), lax.axis_size("quad")
    near, far = [], []
    for w in range(wide):
        for q in range(quad):
            near.append((w * quad + q, (w ^ 1) * quad + q))
            if w in (0, wide - 1):
                far.append((w * quad + q, w * quad + (q ^ 1)))
            else:
                far.append((w * quad + q, (w + 1 if w % 2 else w - 1) * quad + q))
    axes = ("wide", "quad")
    return lax.ppermute(first, axes, near), lax.ppermute(second, axes, far)


def shards(fine_pops, coarse_pops, fine_solid, coarse_solid, fine_active, coarse_covered, rates):
    i32 = jnp.int32
    dma = pltpu.SemaphoreType.DMA
    ext_shape, pops_shape = (20, 8, 40, 128), (19, 8, 40, 128)
    def in_hbm(*arrays):
        return [pltpu.with_memory_space_constraint(a, pltpu.HBM) for a in arrays]

    ext, yu, yd, zu, zd, solid, on, frate, crate = call(
        faces_first_kernel,
        "collide_faces",
        [HBM] * 7,
        [(ext_shape, VMEM)]
        + [((Y_FACES, 128), VMEM)] * 2
        + [((6, 16, 128), VMEM)] * 2
        + [((8, 32, 128), VMEM, i32), ((2, 32, 128), VMEM)]
        + [((15, 8, 128), VMEM)] * 2,
        [
            pltpu.SMEM((15,), F32),
            (4, 19, 32, 128),
            pltpu.VMEM((2, 8, 32), i32),
            (19, 2, 16, 128),
            pltpu.VMEM((2, 16, 128), i32),
            pltpu.VMEM((2, 16, 128), i32),
            dma((10,)),
        ],
    )(
        *in_hbm(
            rates, fine_pops, fine_solid, fine_active, coarse_pops, coarse_solid, coarse_covered
        )
    )
    ru, rd = over_quad(yu, yd)
    ext, yu, yd = call(
        inner_first_kernel,
        "collide_inner",
        [VMEM] * 5,
        [(ext_shape, VMEM)] + [((Y_INNER, 128), VMEM)] * 2,
        aliases={4: 0},
        weight=2,
    )(frate, fine_pops, solid, on, ext)
    ru2, rd2 = over_quad(yu, yd)
    (face_planes,) = call(
        face_planes_kernel,
        "copy_faces",
        [VMEM],
        [((25, 2, 32, 128), VMEM)],
        weight=20,
    )(ext)
    pa, pb = call(
        faces_kernel,
        "substep_one_faces",
        [VMEM] * 5,
        [((X_ALL, 8, 128), VMEM)] * 2,
        [(20, 1, 40, 128), (5, 40, 128), (8, 128), (2, X_ALL, 8, 128)],
    )(face_planes, zu, zd, ru, rd)
    ra, rb = over_wide(pa, pb)
    (ext,) = call(
        fill_kernel,
        "fill_rows",
        [VMEM] * 5,
        [(ext_shape, VMEM)],
        aliases={0: 0},
    )(ext, ru, rd, ru2, rd2)
    kept = [(pops_shape, VMEM)] * 2
    sent = [((32 * CHUNK, 128), VMEM), ((128, 128), VMEM)]
    out_shape = ((19, 8, 32, 128), HBM)
    work = [(256, 128), (2, 128, 128)]
    first, src2, fine_out, send, rest = call(
        inner_kernel,
        "substeps_inner",
        [VMEM] * 3,
        kept + [out_shape] + sent,
        [(4, 19, 32, 128), (2, 768, 128)] + work + [dma((4,))],
        weight=50,
    )(frate, ext, crate)
    for second, message in ((False, ra), (True, rb)):
        first, src2, send, rest, fine_out = call(
            functools.partial(side_kernel, second),
            "substeps_second_side" if second else "substeps_first_side",
            [VMEM] * 8 + [HBM],
            kept + sent + [out_shape],
            [(2, 19, 32, 128), (768, 128)]
            + work
            + [(19, 40, 128), (5, 40, 128), dma((2,))],
            aliases={4: 0, 5: 1, 6: 2, 7: 3, 8: 4},
            weight=2,
        )(frate, ext, crate, message, first, src2, send, rest, fine_out)
    count = lax.axis_size("wide")
    got = lax.all_to_all(
        send.reshape(count, 1, CHUNK * 128), "wide", split_axis=0, concat_axis=0, tiled=True
    ).reshape(count * CHUNK, 128)
    (coarse_out,) = call(
        coarse_kernel,
        "coarse_step",
        [VMEM] * 9,
        [((19, 2, 16, 128), VMEM)],
        [(7, 128, 128), (2, 384, 128), (128, 128), (19, 4, 24, 128), (19, 4, 24, 128), (2, 13, 8, 128)],
    )(got, crate, coarse_pops, coarse_solid, coarse_covered, ru, rd, ra, rb)
    return (fine_out, coarse_out)


def solution(mesh):
    in_specs = (
        P(None, "wide", "quad", None),
        P(None, "wide", "quad", None),
        P("wide", "quad", None),
        P("wide", "quad", None),
        P("wide", "quad", None),
        P("wide", "quad", None),
        P(),
    )
    out_specs = (P(None, "wide", "quad", None), P(None, "wide", "quad", None))
    return jax.shard_map(shards, mesh=mesh, in_specs=in_specs, out_specs=out_specs, check_vma=False)
```

```python
import functools

import jax
import jax.numpy as jnp
from jax import lax
from jax.experimental import pallas as pl
from jax.experimental.pallas import tpu as pltpu
from jax.sharding import PartitionSpec as P

VEL = [
    (0, 0, 0),
    (1, 0, 0),
    (-1, 0, 0),
    (0, 1, 0),
    (0, -1, 0),
    (0, 0, 1),
    (0, 0, -1),
    (1, 1, 0),
    (-1, -1, 0),
    (1, -1, 0),
    (-1, 1, 0),
    (1, 0, 1),
    (-1, 0, -1),
    (1, 0, -1),
    (-1, 0, 1),
    (0, 1, 1),
    (0, -1, -1),
    (0, 1, -1),
    (0, -1, 1),
]
OPP = [0, 2, 1, 4, 3, 6, 5, 8, 7, 10, 9, 12, 11, 14, 13, 16, 15, 18, 17]


def moving(axis, sign):
    return [q for q in range(19) if VEL[q][axis] == sign]


XP, XM = moving(0, 1), moving(0, -1)
YP, YM = moving(1, 1), moving(1, -1)
ZP, ZM = moving(2, 1), moving(2, -1)
WALL = 1e30
WALL_TEST = 1e29
F32 = jnp.float32
MIB = 1 << 20

FACES = (0, 7)
INNER = (1, 2, 3, 4, 5, 6)
NEXT = ((1, XM), (6, XP))
ACROSS = [q for q in range(19) if VEL[q][0] == 0]
Y_COARSE = 130
Y_NEXT = 142
Y_FACES = 176
Y_INNER = 392
X_COARSE = 70
X_ALL = X_COARSE + 13
CHUNK = 25

FACTOR = [0.25] * 3 + [0.5] * 3 + [0.25] * 9

def collide(f, rate):
    r_xy, r_xz, r_yz, r_xx, r_yy, r_zz = rate[:6]
    r_xyy, r_xzz, r_yxx, r_yzz, r_zxx, r_zyy, r_xxyy, r_xxzz, r_yyzz = rate[6:]
    sx, dx = f[1] + f[2], f[1] - f[2]
    sy, dy = f[3] + f[4], f[3] - f[4]
    sz, dz = f[5] + f[6], f[5] - f[6]

    def plane(i):
        a, b = f[i] + f[i + 1], f[i + 2] + f[i + 3]
        c, d = f[i] - f[i + 1], f[i + 2] - f[i + 3]
        return a + b, a - b, c + d, c - d

    m_xxyy, m_xy, m_xyy, m_yxx = plane(7)
    m_xxzz, m_xz, m_xzz, m_zxx = plane(11)
    m_yyzz, m_yz, m_yzz, m_zyy = plane(15)
    m_xx = sx + (m_xxyy + m_xxzz)
    m_yy = sy + (m_xxyy + m_yyzz)
    m_zz = sz + (m_xxzz + m_yyzz)
    jx = dx + (m_xyy + m_xzz)
    jy = dy + (m_yxx + m_yzz)
    jz = dz + (m_zxx + m_zyy)
    rho = (f[0] + sx) + (sy + sz) + ((m_xxyy + m_xxzz) + m_yyzz)
    inv = 1.0 / rho
    ux, uy, uz = jx * inv, jy * inv, jz * inv
    xx, yy, zz = jx * ux, jy * uy, jz * uz
    third = rho * (1.0 / 3.0)
    ninth = rho * (1.0 / 9.0)
    jx3, jy3, jz3 = jx * (1.0 / 3.0), jy * (1.0 / 3.0), jz * (1.0 / 3.0)
    xx3, yy3, zz3 = xx * (1.0 / 3.0), yy * (1.0 / 3.0), zz * (1.0 / 3.0)
    h_xx = (m_xx - third - xx) * r_xx
    h_yy = (m_yy - third - yy) * r_yy
    h_zz = (m_zz - third - zz) * r_zz
    post = [None] * 19

    def diagonal(i, fourth, cross, first, second):
        p, m = fourth + cross, fourth - cross
        s, d = first + second, first - second
        post[i] = f[i] - (p + s)
        post[i + 1] = f[i + 1] - (p - s)
        post[i + 2] = f[i + 2] - (m + d)
        post[i + 3] = f[i + 3] - (m - d)

    a_xy = (m_xxyy - ninth - (xx3 + yy3 - 0.5 * zz3)) * r_xxyy
    a_xz = (m_xxzz - ninth - (xx3 + zz3 - 0.5 * yy3)) * r_xxzz
    a_yz = (m_yyzz - ninth - (yy3 + zz3 - 0.5 * xx3)) * r_yyzz
    c_xyy, c_yxx = (m_xyy - jx3) * r_xyy, (m_yxx - jy3) * r_yxx
    c_xzz, c_zxx = (m_xzz - jx3) * r_xzz, (m_zxx - jz3) * r_zxx
    c_yzz, c_zyy = (m_yzz - jy3) * r_yzz, (m_zyy - jz3) * r_zyy
    diagonal(7, a_xy, (m_xy - jx * uy) * r_xy, c_xyy, c_yxx)
    diagonal(11, a_xz, (m_xz - jx * uz) * r_xz, c_xzz, c_zxx)
    diagonal(15, a_yz, (m_yz - jy * uz) * r_yz, c_yzz, c_zyy)

    def straight(i, h, a, c):
        p, n = h - 2.0 * a, 2.0 * c
        post[i] = f[i] - (p - n)
        post[i + 1] = f[i + 1] - (p + n)

    straight(1, h_xx, a_xy + a_xz, c_xyy + c_xzz)
    straight(3, h_yy, a_xy + a_yz, c_yxx + c_yzz)
    straight(5, h_zz, a_xz + a_yz, c_zxx + c_zyy)
    post[0] = f[0] + (2.0 * (h_xx + h_yy + h_zz) - 4.0 * (a_xy + a_xz + a_yz))
    return post


def iota(shape, axis):
    return lax.broadcasted_iota(jnp.int32, shape, axis)


def write_rates(rates, fine, coarse):
    for i in range(15):
        rate = jnp.full((8, 128), rates[i], F32)
        fine[i] = rate * FACTOR[i]
        coarse[i] = FACTOR[i] / (2.0 / rate - 0.5)


def read_rates(ref):
    return [ref[i] for i in range(15)]


def wall_where(code, value):
    return jnp.where(code > 0.5, value, WALL)


def grown_blocks(active):
    grow = (iota((32, 128), 1) // 4 == iota((32, 128), 0)).astype(F32)
    return jnp.dot(active.astype(F32), grow, preferred_element_type=F32)


def edges():
    quad, wide = lax.axis_index("quad"), lax.axis_index("wide")
    return (
        (quad > 0).astype(F32),
        (quad < lax.axis_size("quad") - 1).astype(F32),
        (wide > 0).astype(F32),
        (wide < lax.axis_size("wide") - 1).astype(F32),
    )


def collide_plane(x, f, solid, on, fine, ext):
    for t in range(4):
        rows = pl.ds(8 * t, 8)
        old = [f[q, rows] for q in range(19)]
        fluid = solid[x, rows] == 0
        live = fluid & (on[x // 4, rows] > 0.5)
        post = collide(old, fine)
        for q in range(19):
            ext[q, x, rows] = jnp.where(live, post[q], old[q])
        ext[19, x, rows] = jnp.where(fluid, 1.0 + on[x // 4, rows], 0.0)


def grow(active, on):
    grow_y = (iota((32, 8), 0) // 4 == iota((32, 8), 1)).astype(F32)
    for b in range(2):
        on[b] = jnp.dot(grow_y, grown_blocks(active[b]), preferred_element_type=F32)


def pack_rows(planes, ext, yu, yd):
    fourth = 60 * len(planes)
    for n, x in enumerate(planes):
        for q in range(20):
            start = 60 * n + 3 * q
            yu[start : start + 3] = ext[q, x, 24:32][5:8]
            yd[start : start + 3] = ext[q, x, 0:8][0:3]
        for i in range(5):
            start = fourth + len(planes) * i + n
            yu[start : start + 1] = wall_where(ext[19, x, 24:32], ext[YP[i], x, 24:32])[4:5]
            yd[start : start + 1] = wall_where(ext[19, x, 0:8], ext[YM[i], x, 0:8])[3:4]


def even_quad():
    return lax.axis_index("quad") % 2 == 0


def order_rows(up, down, first, second):
    first[...] = jnp.where(even_quad(), up[...], down[...])
    second[...] = jnp.where(even_quad(), down[...], up[...])


def faces_first_kernel(
    rates_in, f, solid_in, active_in, cp, c_solid, c_cov,
    ext, ya, yb, zu, zd, solid, on, frate, crate,
    rates, held, active, cps, c_solids, c_covs, yu, yd, sems,
):
    small = [
        pltpu.make_async_copy(rates_in, rates, sems.at[0]),
        pltpu.make_async_copy(solid_in, solid, sems.at[1]),
        pltpu.make_async_copy(active_in, active, sems.at[2]),
    ]
    coarse_copies = [
        pltpu.make_async_copy(cp, cps, sems.at[3]),
        pltpu.make_async_copy(c_solid, c_solids, sems.at[4]),
        pltpu.make_async_copy(c_cov, c_covs, sems.at[5]),
    ]
    planes = [
        pltpu.make_async_copy(f.at[:, x], held.at[n], sems.at[6 + n])
        for n, x in enumerate((0, 7, 1, 6))
    ]
    for copy in small + planes + coarse_copies:
        copy.start()
    for copy in small:
        copy.wait()
    write_rates(rates, frate, crate)
    fine = read_rates(frate)
    grow(active, on)
    for n, x in enumerate((0, 7, 1, 6)):
        planes[n].wait()
        collide_plane(x, held.at[n], solid, on, fine, ext)
    pack_rows(FACES, ext, yu, yd)
    for e, (x, values) in enumerate(NEXT):
        for i, q in enumerate(values):
            start = Y_NEXT + 15 * e + 3 * i
            high = wall_where(ext[19, x, 24:32], ext[q, x, 24:32])
            low = wall_where(ext[19, x, 0:8], ext[q, x, 0:8])
            yu[start : start + 3] = high[5:8]
            yd[start : start + 3] = low[0:3]
            fourth = Y_NEXT + 30 + e
            if q in YP:
                yu[fourth : fourth + 1] = high[4:5]
            if q in YM:
                yd[fourth : fourth + 1] = low[3:4]
    for copy in coarse_copies:
        copy.wait()
    coarse = read_rates(crate)
    for z in range(2):
        for t in range(2):
            rows = pl.ds(8 * t, 8)
            post = collide([cps[q, z, rows] for q in range(19)], coarse)
            code = jnp.where(c_solids[z, rows] == 0, 1.0 + c_covs[z, rows].astype(F32), 0.0)
            values, to = (ZP, zu) if z == 1 else (ZM, zd)
            for i in range(5):
                to[i, rows] = post[values[i]]
            to[5, rows] = code
            values, to, row = (YM, yd, 0) if t == 0 else (YP, yu, 7)
            for i in range(6):
                place = Y_COARSE + 6 * z + i
                value = code if i == 5 else post[values[i]]
                to[place : place + 1] = value[row : row + 1]
    order_rows(yu, yd, ya, yb)


def inner_first_kernel(frate, f, solid, on, ext_in, ext, ya, yb, yu, yd):
    fine = read_rates(frate)

    def plane(x, carry):
        collide_plane(x, f.at[:, x - 2], solid, on, fine, ext)
        return carry

    lax.fori_loop(2, 6, plane, 0)
    pack_rows(INNER, ext, yu, yd)
    order_rows(yu, yd, ya, yb)


def fill_rows(q, planes, n, ru, rd, to):
    start = 60 * n + 3 * q
    to[0:3] = rd[start : start + 3]
    to[5:8] = ru[start : start + 3]
    fourth = 60 * len(planes) + n
    if q in YM:
        place = fourth + len(planes) * YM.index(q)
        to[3:4] = rd[place : place + 1]
    if q in YP:
        place = fourth + len(planes) * YP.index(q)
        to[4:5] = ru[place : place + 1]


def fill_code(n, ru, rd, to, has_prev, has_next):
    start = 60 * n + 57
    to[0:3] = rd[start : start + 3] * has_next
    to[5:8] = ru[start : start + 3] * has_prev
    to[3:4] = jnp.full((1, 128), has_next, F32)
    to[4:5] = jnp.full((1, 128), has_prev, F32)


def upwards():
    return lax.axis_index("wide") % 2 == 0


def face_planes_kernel(ext, held):
    for face, x in enumerate(FACES):
        for q in range(20):
            held[q, face, 0:32] = ext[q, x, 0:32]
        near, values = NEXT[face]
        for i, q in enumerate(values):
            held[20 + i, face, 0:32] = wall_where(ext[19, near, 0:32], ext[q, near, 0:32])


def faces_kernel(planes, zu, zd, qa, qb, pa, pb, ru, rd, held, beyond, tile, both):
    has_prev, has_next, _, _ = edges()
    order_rows(qb, qa, ru, rd)
    lane = iota((40, 128), 1)
    inside = jnp.where(iota((8, 128), 0) < 4, has_next, has_prev) > 0.5
    for face, x in enumerate(FACES):
        place = jnp.where(upwards() == (x == 7), 0, 1)
        for q in range(19):
            held[q, 0, 0:32] = planes[q, face, 0:32]
            fill_rows(q, FACES, face, ru, rd, held.at[q, 0, 32:40])
        held[19, 0, 0:32] = planes[19, face, 0:32]
        fill_code(face, ru, rd, held.at[19, 0, 32:40], has_prev, has_next)
        values = NEXT[face][1]
        for i, q in enumerate(values):
            beyond[i, 0:32] = planes[20 + i, face, 0:32]
            start = Y_NEXT + 15 * face + 3 * i
            fourth = Y_NEXT + 30 + face
            tile[0:3] = rd[start : start + 3]
            tile[5:8] = ru[start : start + 3]
            if q in YM:
                tile[3:4] = rd[fourth : fourth + 1]
            if q in YP:
                tile[4:5] = ru[fourth : fourth + 1]
            beyond[i, 32:40] = jnp.where(inside, tile[...], WALL)
        code = held[19, 0]
        live, open_cells = code > 1.5, {0: code > 0.5}
        outer = (VEL[values[0]][0], lambda q: beyond[values.index(q)])
        staying = {q: streamed(q, 0, held, open_cells, live, lane, outer) for q in ACROSS}
        total = None
        for q, part in staying.items():
            total = part if total is None else total + part
        along_y = (staying[3] - staying[4]) + (staying[15] - staying[16]) + (staying[17] - staying[18])
        along_z = (staying[5] - staying[6]) + (staying[15] - staying[16]) - (staying[17] - staying[18])
        for i in range(14):
            if i < 3:
                part = (total, along_y, along_z)[i]
            elif i < 8:
                part = streamed(values[i - 3], 0, held, open_cells, live, lane, outer)
            elif i < 13:
                part = wall_where(code, held[values[i - 8], 0])
            else:
                part = code
            for t in range(5):
                both[place, 5 * i + t] = part[8 * t : 8 * t + 8]
        z, arriving, leaving, from_ = ((0, 17, 16, zd), (1, 15, 18, zu))[face]
        for i in range(6):
            for t in range(2):
                both[place, X_COARSE + 2 * i + t] = from_[i, 8 * t : 8 * t + 8]

        def arrived(rows, i):
            row = Y_COARSE + 6 * z + i
            return rows[row : row + 1]

        tile[0:1] = arrived(ru, YP.index(arriving))
        tile[1:2] = arrived(rd, YM.index(leaving))
        tile[2:3] = arrived(ru, 5) * has_prev
        tile[3:4] = arrived(rd, 5) * has_next
        both[place, X_COARSE + 12] = tile[...]
    pa[...] = both[0]
    pb[...] = both[1]


def streamed(q, x, values, open_cells, live, lane, outer=None):
    cx, cy, cz = VEL[q]
    if q == 0:
        return values[0, x]
    if cx and outer is not None and outer[0] == cx:
        value = outer[1](q)
    else:
        value = jnp.where(open_cells[cx], values[q, x - cx], WALL)
    if cy:
        value = pltpu.roll(value, cy % 40, 0)
    if cz:
        value = pltpu.roll(value, cz % 128, 1)
    open_ = value < WALL_TEST
    if cz:
        open_ = open_ & (lane != (0 if cz == 1 else 127))
    return jnp.where(live, jnp.where(open_, value, values[OPP[q], x]), values[q, x])


def step_plane(x, ext, first, src2, fine, lane, outer=None):
    open_cells = {}
    for cx in (-1, 0, 1):
        if outer is None or outer[0] != cx:
            open_cells[cx] = ext[19, x - cx] > 0.5
    live = ext[19, x] > 1.5
    for q in range(19):
        first[q, x] = streamed(q, x, ext, open_cells, live, lane, outer)
    for t in range(5):
        rows = pl.ds(8 * t, 8)
        live_t = ext[19, x, rows] > 1.5
        old = [first[q, x, rows] for q in range(19)]
        post = collide(old, fine)
        for q in range(19):
            src2[q, x, rows] = jnp.where(live_t, post[q], old[q])


def fill_kernel(ext_in, ru, rd, qa, qb, ext, ru2, rd2):
    has_prev, has_next, _, _ = edges()
    order_rows(qb, qa, ru2, rd2)
    for planes, up, down in ((FACES, ru, rd), (INNER, ru2, rd2)):
        for n, x in enumerate(planes):
            for q in range(19):
                fill_rows(q, planes, n, up, down, ext.at[q, x, 32:40])
            fill_code(n, up, down, ext.at[19, x, 32:40], has_prev, has_next)


def second_plane(x, ext, first, src2, lane, emit, outer=None):
    open_cells = {}
    for cx in (-1, 0, 1):
        if outer is None or outer[0] != cx:
            open_cells[cx] = ext[19, x - cx] > 0.5
    live = ext[19, x] > 1.5
    for q in range(19):
        emit(q, streamed(q, x, src2, open_cells, live, lane, outer), first[q, x])


def own_planes():
    z_pair = iota((32, 128), 1) // 2
    plane = 2 * iota((32, 128), 0)
    return [jnp.where(z_pair == plane + k, 0.0625, 0.0) for k in range(2)]


def picked(rows, cells):
    return lax.dot_general(
        rows,
        cells,
        (((1,), (1,)), ((), ())),
        precision=lax.Precision.HIGHEST,
        preferred_element_type=F32,
    )


def destinations(sums, coarse, raw, mixed, rest, send, b):
    even = iota((8, 128), 1) % 2 == 0

    def alone(value, shift):
        value = jnp.where(even, 16.0 * value, 0.0)
        return pltpu.roll(value, 2 * shift % 128, 1) if shift else value

    for t in range(3):
        cells = []
        for q in range(19):
            start = 40 * q + 16 * t
            value = sums[pl.ds(start, 8, stride=2)] + sums[pl.ds(start + 1, 8, stride=2)]
            if t < 2:
                place = 16 * q + 8 * t
                if q < 16:
                    raw[place : place + 8] = value
                else:
                    mixed[0, place - 256 : place - 248] = value
                    mixed[1, place - 256 : place - 248] = value
            cells.append((value + pltpu.roll(value, 127, 1)) * 0.0625)
        post = collide(cells, coarse)
        if t < 2:
            for i in range(5):
                place = 48 + 16 * i + 8 * t
                mixed[0, place : place + 8] = alone(post[ZP[i]], 1)
                mixed[1, place : place + 8] = alone(post[ZM[i]], -1)
        else:
            last = [alone(post[q], 0)[3:4] for q in YP] + [alone(post[q], 0)[0:1] for q in YM]
            for k in range(2):
                corners = ((15, 18), (17, 16))[k]
                shift = (1, -1)[k]
                here = last + [alone(post[corners[0]], shift)[3:4], alone(post[corners[1]], shift)[0:1]]
                for i in range(12):
                    rest[pl.ds(64 * k + 12 * b + i, 1)] = here[i]
    planes = own_planes()
    both = jnp.concatenate(planes, axis=0)
    for n in range(2):
        got = picked(both, raw[128 * n : 128 * n + 128])
        for k in range(2):
            send[pl.ds(6 * b + 2 * k + n, 32, stride=CHUNK)] = got[32 * k : 32 * k + 32]
    for k in range(2):
        send[pl.ds(6 * b + 4 + k, 32, stride=CHUNK)] = picked(planes[k], mixed[k])


def inner_kernel(
    frate, ext, crate, first, src2, planes, send, rest, sums, raw, mixed
):
    fine = read_rates(frate)
    lane = iota((40, 128), 1)
    rest[...] = jnp.zeros(rest.shape, F32)

    def substep_one(x, carry):
        step_plane(x, ext, first, src2, fine, lane)
        return carry

    lax.fori_loop(1, 7, substep_one, 0)

    def pair(b, carry):
        for e in range(2):
            x = 2 * b + e

            def emit(q, value, before):
                planes[q, x - 2] = value[0:32]
                rows = pl.ds(40 * q, 40)
                total = value + before
                sums[b - 1, rows] = total if e == 0 else sums[b - 1, rows] + total

            second_plane(x, ext, first, src2, lane, emit)
        return carry

    lax.fori_loop(1, 3, pair, 0)
    coarse = read_rates(crate)
    for b in (1, 2):
        destinations(sums.at[b - 1], coarse, raw, mixed, rest, send, b)


def side(
    left, message, inside, frate, ext, crate, first, src2, send, rest, planes,
    sums, raw, mixed, before, outside,
):
    fine = read_rates(frate)
    lane = iota((40, 128), 1)
    entering, leaving = (XP, XM) if left else (XM, XP)
    cx = 1 if left else -1
    x, near, b = (0, 1, 0) if left else (7, 6, 3)

    def arrived(i):
        return message[5 * i : 5 * i + 5].reshape(40, 128)

    def part(i):
        return jnp.where(inside > 0.5, arrived(i), WALL)

    for i, q in enumerate(entering):
        before[q] = arrived(3 + i)
    open_cells = ext[19, x] > 0.5
    for q in leaving:
        _, cy, cz = VEL[q]
        value = jnp.where(open_cells, ext[q, x], WALL)
        if cy:
            value = pltpu.roll(value, cy % 40, 0)
        if cz:
            value = pltpu.roll(value, cz % 128, 1)
        open_ = value < WALL_TEST
        if cz:
            open_ = open_ & (lane != (0 if cz == 1 else 127))
        before[q] = jnp.where(open_, value, arrived(8 + entering.index(OPP[q])))
    for t in range(5):
        rows = pl.ds(8 * t, 8)
        code_t = message[65 + t] * inside
        old = [before[q, rows] if VEL[q][0] else None for q in range(19)]
        total, along_y, along_z = message[t], message[5 + t], message[10 + t]
        for q in ACROSS:
            old[q] = jnp.zeros((8, 128), F32)
        old[0], old[3], old[5] = total - along_y - along_z, along_y, along_z
        post = collide(old, fine)
        for i, q in enumerate(entering):
            value = jnp.where(code_t > 1.5, post[q], old[q])
            outside[i, rows] = wall_where(code_t, value)
    step_plane(
        x, ext, first, src2, fine, lane, (cx, lambda q: part(8 + entering.index(q)))
    )
    for e, (plane, outer) in enumerate(
        ((x, (cx, lambda q: outside[entering.index(q)])), (near, None))
    ):

        def emit(q, value, earlier):
            planes[q, plane % 2] = value[0:32]
            rows = pl.ds(40 * q, 40)
            total = value + earlier
            sums[rows] = total if e == 0 else sums[rows] + total

        second_plane(plane, ext, first, src2, lane, emit, outer)
    destinations(sums, read_rates(crate), raw, mixed, rest, send, b)


def first_plane(second):
    return jnp.where(upwards() == second, 0, 6)


def sides(second, message, *refs):
    _, _, has_left, has_right = edges()
    on_left = upwards() == second

    @pl.when(on_left)
    def _():
        side(True, message, has_left, *refs)

    @pl.when(jnp.logical_not(on_left))
    def _():
        side(False, message, has_right, *refs)


def first_side_kernel(
    done, frate, ext, crate, message, first_in, src2_in, send_in, rest_in,
    first, src2, send, rest, fine_out, planes, sums, raw, mixed, before, outside, sem,
):
    copy = pltpu.make_async_copy(done, fine_out.at[:, 2:6], sem)
    copy.start()
    sides(
        False, message, frate, ext, crate, first, src2, send, rest, planes,
        sums, raw, mixed, before, outside,
    )
    copy.wait()


def second_side_kernel(
    done, fine_in, frate, ext, crate, message, first_in, src2_in, send_in, rest_in,
    first, src2, send, rest, fine_out, planes, sums, raw, mixed, before, outside, sem,
):
    copy = pltpu.make_async_copy(done, fine_out.at[:, pl.ds(first_plane(False), 2)], sem)
    copy.start()
    sides(
        True, message, frate, ext, crate, first, src2, send, rest, planes,
        sums, raw, mixed, before, outside,
    )
    of_first, of_second = (picked(plane, rest[...]) for plane in own_planes())
    send[pl.ds(CHUNK - 1, 32, stride=CHUNK)] = jnp.where(
        iota((32, 128), 1) < 64, of_first, of_second
    )
    copy.wait()


def coarse_kernel(
    done, fine_in, got, crate, cp, c_solid, c_cov, ru, rd, ra, rb, out, fine_out,
    mesh, turned, rest, walled, source, message, result, sems,
):
    copy = pltpu.make_async_copy(done, fine_out.at[:, pl.ds(first_plane(True), 2)], sems.at[0])
    copy.start()
    has_prev, has_next, has_left, has_right = edges()
    coarse = read_rates(crate)
    for m in range(6):
        for b in range(4):
            mesh[m, pl.ds(b, 32, stride=4)] = got[pl.ds(6 * b + m, 32, stride=CHUNK)]
    left = got[pl.ds(CHUNK - 1, 32, stride=CHUNK)]
    for b in range(4):
        mesh[6, pl.ds(b, 32, stride=4)] = pltpu.roll(left, -12 * b % 128, 1) if b else left
    for k in range(2):
        for n, m in enumerate((2 * k, 2 * k + 1, 4 + k)):
            turned[k, 128 * n : 128 * n + 128] = mesh[m].T
    rest[...] = mesh[6].T

    goes_up = upwards()
    for i in range(13):
        first, second = ra[X_COARSE + i], rb[X_COARSE + i]
        message[0, i] = jnp.where(goes_up, second, first)
        message[1, i] = jnp.where(goes_up, first, second)

    def pick(code, here, there):
        return jnp.where(code > 1.5, here, jnp.where(code > 0.5, there, WALL))

    def arrived(from_, place):
        return from_[Y_COARSE + place : Y_COARSE + place + 1]

    for k in range(2):
        for t in range(2):
            rows = pl.ds(8 * t, 8)
            fluid = c_solid[k, rows] == 0
            covered = c_cov[k, rows] == 1
            old = []
            for q in range(19):
                start = 16 * q + 8 * t
                old.append(jnp.where(covered, turned[k, start : start + 8], cp[q, k, rows]))
            post = collide(old, coarse)
            for q in range(19):
                value = jnp.where(fluid, post[q], old[q])
                source[q, k + 1, rows] = value
                walled[q, k + 1, rows] = jnp.where(fluid, value, WALL)
        prev_code = arrived(ru, 6 * k + 5) * has_prev
        next_code = arrived(rd, 6 * k + 5) * has_next
        for i in range(5):
            walled[YP[i], k + 1, 23:24] = pick(
                prev_code, rest[64 * k + i : 64 * k + i + 1], arrived(ru, 6 * k + i)
            )
            walled[YM[i], k + 1, 16:17] = pick(
                next_code, rest[64 * k + 5 + i : 64 * k + 6 + i], arrived(rd, 6 * k + i)
            )
        values, from_, z, inside = ((ZP, message.at[0], 0, has_left), (ZM, message.at[1], 3, has_right))[k]
        prev_q, next_q = ((15, 18), (17, 16))[k]
        for t in range(2):
            code = from_[10 + t] * inside
            for i in range(5):
                start = 304 + 16 * i + 8 * t
                walled[values[i], z, 8 * t : 8 * t + 8] = pick(
                    code, turned[k, start : start + 8], from_[2 * i + t]
                )
        walled[prev_q, z, 23:24] = pick(
            from_[12, 2:3] * inside, rest[64 * k + 10 : 64 * k + 11], from_[12, 0:1]
        )
        walled[next_q, z, 16:17] = pick(
            from_[12, 3:4] * inside, rest[64 * k + 11 : 64 * k + 12], from_[12, 1:2]
        )

    lane = iota((16, 128), 1)
    copies = [copy]
    for z in (1, 2):
        fluid = c_solid[z - 1] == 0
        for q in range(19):
            cx, cy, cz = VEL[q]
            value = walled[q, z - cz]
            if cy:
                value = pltpu.roll(value, cy % 24, 0)
            value = value[0:16]
            if cx:
                value = pltpu.roll(value, cx % 128, 1)
            open_ = value < WALL_TEST
            if cx:
                open_ = open_ & (lane != (0 if cx == 1 else 127))
            bounced = jnp.where(open_, value, source[OPP[q], z, 0:16])
            result[q, z - 1] = jnp.where(fluid, bounced, source[q, z, 0:16])
        copies.append(pltpu.make_async_copy(result.at[:, z - 1], out.at[:, z - 1], sems.at[z]))
        copies[-1].start()
    for copy in copies:
        copy.wait()


VMEM = pl.BlockSpec(memory_space=pltpu.VMEM)
HBM = pl.BlockSpec(memory_space=pltpu.HBM)


def call(kernel, name, ins, outs, scratch=(), aliases=None, weight=1):
    return pl.pallas_call(
        kernel,
        out_shape=[jax.ShapeDtypeStruct(out[0], (out + (F32,))[2]) for out in outs],
        in_specs=ins,
        out_specs=[out[1] for out in outs],
        scratch_shapes=[s if not isinstance(s, tuple) else pltpu.VMEM(s, F32) for s in scratch],
        input_output_aliases=aliases or {},
        compiler_params=pltpu.CompilerParams(vmem_limit_bytes=24 * MIB),
        cost_estimate=pl.CostEstimate(
            flops=weight * 1_000_000_000, bytes_accessed=0, transcendentals=0
        ),
        name=name,
    )


def over_quad(first, second):
    wide, quad = lax.axis_size("wide"), lax.axis_size("quad")
    near, far = [], []
    for w in range(wide):
        for q in range(quad):
            near.append((w * quad + q, w * quad + (q ^ 1)))
            if q in (0, quad - 1):
                far.append((w * quad + q, (w ^ 1) * quad + q))
            else:
                far.append((w * quad + q, w * quad + (q + 1 if q % 2 else q - 1)))
    axes = ("wide", "quad")
    return lax.ppermute(first, axes, near), lax.ppermute(second, axes, far)


def over_wide(first, second):
    wide, quad = lax.axis_size("wide"), lax.axis_size("quad")
    near, far = [], []
    for w in range(wide):
        for q in range(quad):
            near.append((w * quad + q, (w ^ 1) * quad + q))
            if w in (0, wide - 1):
                far.append((w * quad + q, w * quad + (q ^ 1)))
            else:
                far.append((w * quad + q, (w + 1 if w % 2 else w - 1) * quad + q))
    axes = ("wide", "quad")
    second = lax.ppermute(second, axes, far)
    return lax.ppermute(first, axes, near), second


def shards(fine_pops, coarse_pops, fine_solid, coarse_solid, fine_active, coarse_covered, rates):
    i32 = jnp.int32
    dma = pltpu.SemaphoreType.DMA
    ext_shape, pops_shape = (20, 8, 40, 128), (19, 8, 40, 128)
    def in_hbm(*arrays):
        return [pltpu.with_memory_space_constraint(a, pltpu.HBM) for a in arrays]

    ext, ya, yb, zu, zd, solid, on, frate, crate = call(
        faces_first_kernel,
        "collide_faces",
        [HBM] * 7,
        [(ext_shape, VMEM)]
        + [((Y_FACES, 128), VMEM)] * 2
        + [((6, 16, 128), VMEM)] * 2
        + [((8, 32, 128), VMEM, i32), ((2, 32, 128), VMEM)]
        + [((15, 8, 128), VMEM)] * 2,
        [
            pltpu.SMEM((15,), F32),
            (4, 19, 32, 128),
            pltpu.VMEM((2, 8, 32), i32),
            (19, 2, 16, 128),
            pltpu.VMEM((2, 16, 128), i32),
            pltpu.VMEM((2, 16, 128), i32),
            (Y_FACES, 128),
            (Y_FACES, 128),
            dma((10,)),
        ],
    )(
        *in_hbm(
            rates, fine_pops, fine_solid, fine_active, coarse_pops, coarse_solid, coarse_covered
        )
    )
    qa, qb = over_quad(ya, yb)
    ext, ya, yb = call(
        inner_first_kernel,
        "collide_inner",
        [VMEM] * 5,
        [(ext_shape, VMEM)] + [((Y_INNER, 128), VMEM)] * 2,
        [(Y_INNER, 128)] * 2,
        aliases={4: 0},
        weight=2,
    )(frate, lax.slice_in_dim(fine_pops, 2, 6, axis=1), solid, on, ext)
    qa2, qb2 = over_quad(ya, yb)
    (face_planes,) = call(
        face_planes_kernel,
        "copy_faces",
        [VMEM],
        [((25, 2, 32, 128), VMEM)],
        weight=20,
    )(ext)
    pa, pb, ru, rd = call(
        faces_kernel,
        "substep_one_faces",
        [VMEM] * 5,
        [((X_ALL, 8, 128), VMEM)] * 2 + [((Y_FACES, 128), VMEM)] * 2,
        [(20, 1, 40, 128), (5, 40, 128), (8, 128), (2, X_ALL, 8, 128)],
    )(face_planes, zu, zd, qa, qb)
    ra, rb = over_wide(pa, pb)
    (ext,) = call(
        fill_kernel,
        "fill_rows",
        [VMEM] * 5,
        [(ext_shape, VMEM)],
        [(Y_INNER, 128)] * 2,
        aliases={0: 0},
    )(ext, ru, rd, qa2, qb2)
    kept = [(pops_shape, VMEM)] * 2
    sent = [((32 * CHUNK, 128), VMEM), ((128, 128), VMEM)]
    out_shape = ((19, 8, 32, 128), HBM)
    two_planes = ((19, 2, 32, 128), VMEM)
    work = [(256, 128), (2, 128, 128)]
    side_work = [(768, 128)] + work + [(19, 40, 128), (5, 40, 128), dma]
    first, src2, done, send, rest = call(
        inner_kernel,
        "substeps_inner",
        [VMEM] * 3,
        kept + [((19, 4, 32, 128), VMEM)] + sent,
        [(2, 768, 128)] + work,
        weight=50,
    )(frate, ext, crate)
    first, src2, send, rest, fine_out, done = call(
        first_side_kernel,
        "substeps_first_side",
        [VMEM] * 9,
        kept + sent + [out_shape, two_planes],
        side_work,
        aliases={5: 0, 6: 1, 7: 2, 8: 3},
        weight=2,
    )(done, frate, ext, crate, ra, first, src2, send, rest)
    first, src2, send, rest, fine_out, done = call(
        second_side_kernel,
        "substeps_second_side",
        [VMEM, HBM] + [VMEM] * 8,
        kept + sent + [out_shape, two_planes],
        side_work,
        aliases={1: 4, 6: 0, 7: 1, 8: 2, 9: 3},
        weight=2,
    )(done, fine_out, frate, ext, crate, rb, first, src2, send, rest)
    count = lax.axis_size("wide")
    got = lax.all_to_all(
        send.reshape(count, 1, CHUNK * 128), "wide", split_axis=0, concat_axis=0, tiled=True
    ).reshape(count * CHUNK, 128)
    coarse_out, fine_out = call(
        coarse_kernel,
        "coarse_step",
        [VMEM, HBM] + [VMEM] * 9,
        [((19, 2, 16, 128), HBM), out_shape],
        [(7, 128, 128), (2, 384, 128), (128, 128), (19, 4, 24, 128), (19, 4, 24, 128), (2, 13, 8, 128), (19, 2, 16, 128), dma((3,))],
        aliases={1: 1},
    )(done, fine_out, got, crate, coarse_pops, coarse_solid, coarse_covered, ru, rd, ra, rb)
    return (fine_out, coarse_out)


def solution(mesh):
    in_specs = (
        P(None, "wide", "quad", None),
        P(None, "wide", "quad", None),
        P("wide", "quad", None),
        P("wide", "quad", None),
        P("wide", "quad", None),
        P("wide", "quad", None),
        P(),
    )
    out_specs = (P(None, "wide", "quad", None), P(None, "wide", "quad", None))
    return jax.shard_map(shards, mesh=mesh, in_specs=in_specs, out_specs=out_specs, check_vma=False)
```

```python
import functools

import jax
import jax.numpy as jnp
from jax import lax
from jax.experimental import pallas as pl
from jax.experimental.pallas import tpu as pltpu
from jax.sharding import PartitionSpec as P

VEL = [
    (0, 0, 0),
    (1, 0, 0),
    (-1, 0, 0),
    (0, 1, 0),
    (0, -1, 0),
    (0, 0, 1),
    (0, 0, -1),
    (1, 1, 0),
    (-1, -1, 0),
    (1, -1, 0),
    (-1, 1, 0),
    (1, 0, 1),
    (-1, 0, -1),
    (1, 0, -1),
    (-1, 0, 1),
    (0, 1, 1),
    (0, -1, -1),
    (0, 1, -1),
    (0, -1, 1),
]
OPP = [0, 2, 1, 4, 3, 6, 5, 8, 7, 10, 9, 12, 11, 14, 13, 16, 15, 18, 17]


def moving(axis, sign):
    return [q for q in range(19) if VEL[q][axis] == sign]


XP, XM = moving(0, 1), moving(0, -1)
YP, YM = moving(1, 1), moving(1, -1)
ZP, ZM = moving(2, 1), moving(2, -1)
WALL = 1e30
WALL_TEST = 1e29
F32 = jnp.float32
MIB = 1 << 20

FACES = (0, 7)
INNER = (1, 2, 3, 4, 5, 6)
NEXT = ((1, XM), (6, XP))
ACROSS = [q for q in range(19) if VEL[q][0] == 0]
Y_COARSE = 130
Y_NEXT = 142
Y_FACES = 176
Y_INNER = 392
X_COARSE = 65
X_ALL = X_COARSE + 11
CHUNK = 25

FACTOR = [0.25] * 3 + [0.5] * 3 + [0.25] * 9

def collide(f, rate):
    r_xy, r_xz, r_yz, r_xx, r_yy, r_zz = rate[:6]
    r_xyy, r_xzz, r_yxx, r_yzz, r_zxx, r_zyy, r_xxyy, r_xxzz, r_yyzz = rate[6:]
    sx, dx = f[1] + f[2], f[1] - f[2]
    sy, dy = f[3] + f[4], f[3] - f[4]
    sz, dz = f[5] + f[6], f[5] - f[6]

    def plane(i):
        a, b = f[i] + f[i + 1], f[i + 2] + f[i + 3]
        c, d = f[i] - f[i + 1], f[i + 2] - f[i + 3]
        return a + b, a - b, c + d, c - d

    m_xxyy, m_xy, m_xyy, m_yxx = plane(7)
    m_xxzz, m_xz, m_xzz, m_zxx = plane(11)
    m_yyzz, m_yz, m_yzz, m_zyy = plane(15)
    m_xx = sx + (m_xxyy + m_xxzz)
    m_yy = sy + (m_xxyy + m_yyzz)
    m_zz = sz + (m_xxzz + m_yyzz)
    jx = dx + (m_xyy + m_xzz)
    jy = dy + (m_yxx + m_yzz)
    jz = dz + (m_zxx + m_zyy)
    rho = (f[0] + sx) + (sy + sz) + ((m_xxyy + m_xxzz) + m_yyzz)
    inv = 1.0 / rho
    ux, uy, uz = jx * inv, jy * inv, jz * inv
    xx, yy, zz = jx * ux, jy * uy, jz * uz
    third = rho * (1.0 / 3.0)
    ninth = rho * (1.0 / 9.0)
    jx3, jy3, jz3 = jx * (1.0 / 3.0), jy * (1.0 / 3.0), jz * (1.0 / 3.0)
    xx3, yy3, zz3 = xx * (1.0 / 3.0), yy * (1.0 / 3.0), zz * (1.0 / 3.0)
    h_xx = (m_xx - third - xx) * r_xx
    h_yy = (m_yy - third - yy) * r_yy
    h_zz = (m_zz - third - zz) * r_zz
    post = [None] * 19

    def diagonal(i, fourth, cross, first, second):
        p, m = fourth + cross, fourth - cross
        s, d = first + second, first - second
        post[i] = f[i] - (p + s)
        post[i + 1] = f[i + 1] - (p - s)
        post[i + 2] = f[i + 2] - (m + d)
        post[i + 3] = f[i + 3] - (m - d)

    a_xy = (m_xxyy - ninth - (xx3 + yy3 - 0.5 * zz3)) * r_xxyy
    a_xz = (m_xxzz - ninth - (xx3 + zz3 - 0.5 * yy3)) * r_xxzz
    a_yz = (m_yyzz - ninth - (yy3 + zz3 - 0.5 * xx3)) * r_yyzz
    c_xyy, c_yxx = (m_xyy - jx3) * r_xyy, (m_yxx - jy3) * r_yxx
    c_xzz, c_zxx = (m_xzz - jx3) * r_xzz, (m_zxx - jz3) * r_zxx
    c_yzz, c_zyy = (m_yzz - jy3) * r_yzz, (m_zyy - jz3) * r_zyy
    diagonal(7, a_xy, (m_xy - jx * uy) * r_xy, c_xyy, c_yxx)
    diagonal(11, a_xz, (m_xz - jx * uz) * r_xz, c_xzz, c_zxx)
    diagonal(15, a_yz, (m_yz - jy * uz) * r_yz, c_yzz, c_zyy)

    def straight(i, h, a, c):
        p, n = h - 2.0 * a, 2.0 * c
        post[i] = f[i] - (p - n)
        post[i + 1] = f[i + 1] - (p + n)

    straight(1, h_xx, a_xy + a_xz, c_xyy + c_xzz)
    straight(3, h_yy, a_xy + a_yz, c_yxx + c_yzz)
    straight(5, h_zz, a_xz + a_yz, c_zxx + c_zyy)
    post[0] = f[0] + (2.0 * (h_xx + h_yy + h_zz) - 4.0 * (a_xy + a_xz + a_yz))
    return post


def iota(shape, axis):
    return lax.broadcasted_iota(jnp.int32, shape, axis)


def write_rates(rates, fine, coarse):
    for i in range(15):
        rate = jnp.full((8, 128), rates[i], F32)
        fine[i] = rate * FACTOR[i]
        coarse[i] = FACTOR[i] / (2.0 / rate - 0.5)


def read_rates(ref):
    return [ref[i] for i in range(15)]


def wall_where(code, value):
    return jnp.where(code > 0.5, value, WALL)


def grown_blocks(active):
    grow = (iota((32, 128), 1) // 4 == iota((32, 128), 0)).astype(F32)
    return jnp.dot(active.astype(F32), grow, preferred_element_type=F32)


def edges():
    quad, wide = lax.axis_index("quad"), lax.axis_index("wide")
    return (
        (quad > 0).astype(F32),
        (quad < lax.axis_size("quad") - 1).astype(F32),
        (wide > 0).astype(F32),
        (wide < lax.axis_size("wide") - 1).astype(F32),
    )


def collide_plane(x, f, solid, on, fine, ext):
    for t in range(4):
        rows = pl.ds(8 * t, 8)
        old = [f[q, rows] for q in range(19)]
        fluid = solid[x, rows] == 0
        live = fluid & (on[x // 4, rows] > 0.5)
        post = collide(old, fine)
        for q in range(19):
            ext[q, x, rows] = jnp.where(live, post[q], old[q])
        ext[19, x, rows] = jnp.where(fluid, 1.0 + on[x // 4, rows], 0.0)


def grow(active, on):
    grow_y = (iota((32, 8), 0) // 4 == iota((32, 8), 1)).astype(F32)
    for b in range(2):
        on[b] = jnp.dot(grow_y, grown_blocks(active[b]), preferred_element_type=F32)


def pack_rows(planes, ext, yu, yd):
    fourth = 60 * len(planes)
    for n, x in enumerate(planes):
        for q in range(20):
            start = 60 * n + 3 * q
            yu[start : start + 3] = ext[q, x, 24:32][5:8]
            yd[start : start + 3] = ext[q, x, 0:8][0:3]
        for i in range(5):
            start = fourth + len(planes) * i + n
            yu[start : start + 1] = wall_where(ext[19, x, 24:32], ext[YP[i], x, 24:32])[4:5]
            yd[start : start + 1] = wall_where(ext[19, x, 0:8], ext[YM[i], x, 0:8])[3:4]


def even_quad():
    return lax.axis_index("quad") % 2 == 0


def order_rows(up, down, first, second):
    first[...] = jnp.where(even_quad(), up[...], down[...])
    second[...] = jnp.where(even_quad(), down[...], up[...])


def rows_first_kernel(
    rates_in, f, solid_in, active_in, cp, c_solid, c_cov,
    ya, yb, solid, on, frate, crate,
    rates, low, high, active, cps, c_solids, c_covs, yu, yd, sems,
):
    small = [
        pltpu.make_async_copy(rates_in, rates, sems.at[0]),
        pltpu.make_async_copy(solid_in, solid, sems.at[1]),
        pltpu.make_async_copy(active_in, active, sems.at[2]),
    ]
    coarse_copies = [
        pltpu.make_async_copy(cp, cps, sems.at[3]),
        pltpu.make_async_copy(c_solid, c_solids, sems.at[4]),
        pltpu.make_async_copy(c_cov, c_covs, sems.at[5]),
    ]
    planes = [
        (
            pltpu.make_async_copy(f.at[:, x, 0:8], low.at[n], sems.at[6 + 2 * n]),
            pltpu.make_async_copy(f.at[:, x, 24:32], high.at[n], sems.at[7 + 2 * n]),
        )
        for n, x in enumerate((0, 7, 1, 6))
    ]
    for copy in small:
        copy.start()
    for pair in planes:
        for copy in pair:
            copy.start()
    for copy in coarse_copies:
        copy.start()
    for copy in small:
        copy.wait()
    write_rates(rates, frate, crate)
    fine = read_rates(frate)
    grow(active, on)
    upper = iota((8, 128), 0) < 4
    for n, x in enumerate((0, 7, 1, 6)):
        for copy in planes[n]:
            copy.wait()
        old = [jnp.where(upper, low[n, q], high[n, q]) for q in range(19)]
        fluid = jnp.where(upper, solid[x, 0:8], solid[x, 24:32]) == 0
        here = jnp.where(upper, on[x // 4, 0:8], on[x // 4, 24:32])
        live = fluid & (here > 0.5)
        post = collide(old, fine)
        source = [jnp.where(live, post[q], old[q]) for q in range(19)]
        source.append(jnp.where(fluid, 1.0 + here, 0.0))
        walled = [jnp.where(fluid, value, WALL) for value in source[:19]]
        if n < 2:
            for q in range(20):
                start = 60 * n + 3 * q
                yu[start : start + 3] = source[q][5:8]
                yd[start : start + 3] = source[q][0:3]
            for i in range(5):
                start = 120 + 2 * i + n
                yu[start : start + 1] = walled[YP[i]][4:5]
                yd[start : start + 1] = walled[YM[i]][3:4]
        else:
            e = n - 2
            for i, q in enumerate(NEXT[e][1]):
                start = Y_NEXT + 15 * e + 3 * i
                fourth = Y_NEXT + 30 + e
                yu[start : start + 3] = walled[q][5:8]
                yd[start : start + 3] = walled[q][0:3]
                if q in YP:
                    yu[fourth : fourth + 1] = walled[q][4:5]
                if q in YM:
                    yd[fourth : fourth + 1] = walled[q][3:4]
    for copy in coarse_copies:
        copy.wait()
    coarse = read_rates(crate)
    for z in range(2):
        old = [jnp.where(upper, cps[q, z, 0:8], cps[q, z, 8:16]) for q in range(19)]
        post = collide(old, coarse)
        fluid = jnp.where(upper, c_solids[z, 0:8], c_solids[z, 8:16]) == 0
        covered = jnp.where(upper, c_covs[z, 0:8], c_covs[z, 8:16]).astype(F32)
        code = jnp.where(fluid, 1.0 + covered, 0.0)
        for i in range(6):
            place = Y_COARSE + 6 * z + i
            yu[place : place + 1] = (code if i == 5 else post[YP[i]])[7:8]
            yd[place : place + 1] = (code if i == 5 else post[YM[i]])[0:1]
    order_rows(yu, yd, ya, yb)


def cells_first_kernel(
    frate, crate, f, solid, on, cp, c_solid, c_cov, ext, ya, yb, zu, zd, yu, yd
):
    fine = read_rates(frate)

    def plane(x, carry):
        collide_plane(x, f.at[:, x], solid, on, fine, ext)
        return carry

    lax.fori_loop(0, 8, plane, 0)
    pack_rows(INNER, ext, yu, yd)
    order_rows(yu, yd, ya, yb)
    coarse = read_rates(crate)
    for z, values, to in ((1, ZP, zu), (0, ZM, zd)):
        for t in range(2):
            rows = pl.ds(8 * t, 8)
            post = collide([cp[q, z, rows] for q in range(19)], coarse)
            for i in range(5):
                to[i, rows] = post[values[i]]
            to[5, rows] = jnp.where(c_solid[z, rows] == 0, 1.0 + c_cov[z, rows].astype(F32), 0.0)


def fill_rows(q, planes, n, ru, rd, to):
    start = 60 * n + 3 * q
    to[0:3] = rd[start : start + 3]
    to[5:8] = ru[start : start + 3]
    fourth = 60 * len(planes) + n
    if q in YM:
        place = fourth + len(planes) * YM.index(q)
        to[3:4] = rd[place : place + 1]
    if q in YP:
        place = fourth + len(planes) * YP.index(q)
        to[4:5] = ru[place : place + 1]


def fill_code(n, ru, rd, to, has_prev, has_next):
    start = 60 * n + 57
    to[0:3] = rd[start : start + 3] * has_next
    to[5:8] = ru[start : start + 3] * has_prev
    to[3:4] = jnp.full((1, 128), has_next, F32)
    to[4:5] = jnp.full((1, 128), has_prev, F32)


def upwards():
    return lax.axis_index("wide") % 2 == 0


def face_planes_kernel(ext, held):
    for face, x in enumerate(FACES):
        for q in range(20):
            held[q, face, 0:32] = ext[q, x, 0:32]
        near, values = NEXT[face]
        for i, q in enumerate(values):
            held[20 + i, face, 0:32] = wall_where(ext[19, near, 0:32], ext[q, near, 0:32])


def copy_kernel(from_, to):
    to[...] = from_[...]


def faces_kernel(planes, zu, zd, qa, qb, pa, pb, ru, rd, held, beyond, tile, both):
    has_prev, has_next, _, _ = edges()
    order_rows(qb, qa, ru, rd)
    lane = iota((40, 128), 1)
    inside = jnp.where(iota((8, 128), 0) < 4, has_next, has_prev) > 0.5
    for face, x in enumerate(FACES):
        place = jnp.where(upwards() == (x == 7), 0, 1)
        for q in range(19):
            held[q, 0, 0:32] = planes[q, face, 0:32]
            fill_rows(q, FACES, face, ru, rd, held.at[q, 0, 32:40])
        held[19, 0, 0:32] = planes[19, face, 0:32]
        fill_code(face, ru, rd, held.at[19, 0, 32:40], has_prev, has_next)
        values = NEXT[face][1]
        for i, q in enumerate(values):
            beyond[i, 0:32] = planes[20 + i, face, 0:32]
            start = Y_NEXT + 15 * face + 3 * i
            fourth = Y_NEXT + 30 + face
            tile[0:3] = rd[start : start + 3]
            tile[5:8] = ru[start : start + 3]
            if q in YM:
                tile[3:4] = rd[fourth : fourth + 1]
            if q in YP:
                tile[4:5] = ru[fourth : fourth + 1]
            beyond[i, 32:40] = jnp.where(inside, tile[...], WALL)
        code = held[19, 0]
        live, open_cells = code > 1.5, {0: code > 0.5}
        outer = (VEL[values[0]][0], lambda q: beyond[values.index(q)])
        staying = {q: streamed(q, 0, held, open_cells, live, lane, outer) for q in ACROSS}
        total = None
        for q, part in staying.items():
            total = part if total is None else total + part
        along_y = (staying[3] - staying[4]) + (staying[15] - staying[16]) + (staying[17] - staying[18])
        along_z = (staying[5] - staying[6]) + (staying[15] - staying[16]) - (staying[17] - staying[18])
        for i in range(13):
            if i < 3:
                part = (jnp.where(live, total, WALL), along_y, along_z)[i]
            elif i < 8:
                part = streamed(values[i - 3], 0, held, open_cells, live, lane, outer)
            else:
                part = wall_where(code, held[values[i - 8], 0])
            for t in range(5):
                both[place, 5 * i + t] = part[8 * t : 8 * t + 8]
        z, arriving, leaving, from_ = ((0, 17, 16, zd), (1, 15, 18, zu))[face]

        def marked(cells, value):
            return wall_where(cells, jnp.where(cells > 1.5, -WALL, value))

        for t in range(2):
            rows = pl.ds(8 * t, 8)
            for i in range(5):
                both[place, X_COARSE + 2 * i + t] = marked(from_[5, rows], from_[i, rows])

        def arrived(rows, i):
            row = Y_COARSE + 6 * z + i
            return rows[row : row + 1]

        tile[0:1] = marked(arrived(ru, 5) * has_prev, arrived(ru, YP.index(arriving)))
        tile[1:2] = marked(arrived(rd, 5) * has_next, arrived(rd, YM.index(leaving)))
        both[place, X_COARSE + 10] = tile[...]
    pa[...] = both[0]
    pb[...] = both[1]


def streamed(q, x, values, open_cells, live, lane, outer=None):
    cx, cy, cz = VEL[q]
    if q == 0:
        return values[0, x]
    if cx and outer is not None and outer[0] == cx:
        value = outer[1](q)
    else:
        value = jnp.where(open_cells[cx], values[q, x - cx], WALL)
    if cy:
        value = pltpu.roll(value, cy % 40, 0)
    if cz:
        value = pltpu.roll(value, cz % 128, 1)
    open_ = value < WALL_TEST
    if cz:
        open_ = open_ & (lane != (0 if cz == 1 else 127))
    return jnp.where(live, jnp.where(open_, value, values[OPP[q], x]), values[q, x])


def step_plane(x, ext, first, src2, fine, lane, outer=None):
    open_cells = {}
    for cx in (-1, 0, 1):
        if outer is None or outer[0] != cx:
            open_cells[cx] = ext[19, x - cx] > 0.5
    live = ext[19, x] > 1.5
    for q in range(19):
        first[q, x] = streamed(q, x, ext, open_cells, live, lane, outer)
    for t in range(5):
        rows = pl.ds(8 * t, 8)
        live_t = ext[19, x, rows] > 1.5
        old = [first[q, x, rows] for q in range(19)]
        post = collide(old, fine)
        for q in range(19):
            src2[q, x, rows] = jnp.where(live_t, post[q], old[q])


def fill_kernel(ext_in, ru, rd, qa, qb, ext, ru2, rd2):
    has_prev, has_next, _, _ = edges()
    order_rows(qb, qa, ru2, rd2)
    for planes, up, down in ((FACES, ru, rd), (INNER, ru2, rd2)):
        for n, x in enumerate(planes):
            for q in range(19):
                fill_rows(q, planes, n, up, down, ext.at[q, x, 32:40])
            fill_code(n, up, down, ext.at[19, x, 32:40], has_prev, has_next)


def second_plane(x, ext, first, src2, lane, emit, outer=None):
    open_cells = {}
    for cx in (-1, 0, 1):
        if outer is None or outer[0] != cx:
            open_cells[cx] = ext[19, x - cx] > 0.5
    live = ext[19, x] > 1.5
    for q in range(19):
        emit(q, streamed(q, x, src2, open_cells, live, lane, outer), first[q, x])


def own_planes():
    z_pair = iota((64, 256), 1) % 128 // 2
    row = iota((64, 256), 0)
    plane = 2 * (row % 32) + row // 32
    return jnp.where(z_pair == plane, 0.0625, 0.0).astype(jnp.bfloat16)


def picked(rows, cells):
    high = cells.astype(jnp.bfloat16)
    low = (cells - high.astype(F32)).astype(jnp.bfloat16)
    return lax.dot_general(
        rows,
        jnp.concatenate([high, low], axis=1),
        (((1,), (1,)), ((), ())),
        preferred_element_type=F32,
    )


def destinations(sums, coarse, raw, mixed, rest, send, b):
    even = iota((8, 128), 1) % 2 == 0

    def alone(value, shift):
        value = jnp.where(even, 16.0 * value, 0.0)
        return pltpu.roll(value, 2 * shift % 128, 1) if shift else value

    for t in range(3):
        cells = []
        for q in range(19):
            start = 40 * q + 16 * t
            value = sums[pl.ds(start, 8, stride=2)] + sums[pl.ds(start + 1, 8, stride=2)]
            if t < 2:
                place = 16 * q + 8 * t
                if q < 16:
                    raw[place : place + 8] = value
                else:
                    mixed[0, place - 256 : place - 248] = value
                    mixed[1, place - 256 : place - 248] = value
            cells.append((value + pltpu.roll(value, 127, 1)) * 0.0625)
        post = collide(cells, coarse)
        if t < 2:
            for i in range(5):
                place = 48 + 16 * i + 8 * t
                mixed[0, place : place + 8] = alone(post[ZP[i]], 1)
                mixed[1, place : place + 8] = alone(post[ZM[i]], -1)
        else:
            last = [alone(post[q], 0)[3:4] for q in YP] + [alone(post[q], 0)[0:1] for q in YM]
            for k in range(2):
                corners = ((15, 18), (17, 16))[k]
                shift = (1, -1)[k]
                here = last + [alone(post[corners[0]], shift)[3:4], alone(post[corners[1]], shift)[0:1]]
                for i in range(12):
                    rest[pl.ds(64 * k + 12 * b + i, 1)] = here[i]
    planes = own_planes()
    got = picked(planes, raw[...])
    for n in range(2):
        for k in range(2):
            send[pl.ds(6 * b + 2 * k + n, 32, stride=CHUNK)] = got[
                32 * k : 32 * k + 32, 128 * n : 128 * n + 128
            ]
    got = picked(planes, mixed[...].reshape(256, 128))
    for k in range(2):
        send[pl.ds(6 * b + 4 + k, 32, stride=CHUNK)] = got[
            32 * k : 32 * k + 32, 128 * k : 128 * k + 128
        ]


def inner_kernel(
    frate, ext, crate, first, src2, planes, send, rest, sums, raw, mixed
):
    fine = read_rates(frate)
    lane = iota((40, 128), 1)
    rest[...] = jnp.zeros(rest.shape, F32)

    def substep_one(x, carry):
        step_plane(x, ext, first, src2, fine, lane)
        return carry

    lax.fori_loop(1, 7, substep_one, 0)

    def pair(b, carry):
        for e in range(2):
            x = 2 * b + e

            def emit(q, value, before):
                planes[q, x - 2] = value[0:32]
                rows = pl.ds(40 * q, 40)
                total = value + before
                sums[b - 1, rows] = total if e == 0 else sums[b - 1, rows] + total

            second_plane(x, ext, first, src2, lane, emit)
        return carry

    lax.fori_loop(1, 3, pair, 0)
    coarse = read_rates(crate)
    for b in (1, 2):
        destinations(sums.at[b - 1], coarse, raw, mixed, rest, send, b)


def side(
    left, message, inside, frate, ext, crate, first, src2, send, rest, planes,
    sums, raw, mixed, before, outside,
):
    fine = read_rates(frate)
    lane = iota((40, 128), 1)
    entering, leaving = (XP, XM) if left else (XM, XP)
    cx = 1 if left else -1
    x, near, b = (0, 1, 0) if left else (7, 6, 3)

    def arrived(i):
        return message[5 * i : 5 * i + 5].reshape(40, 128)

    def part(i):
        return jnp.where(inside > 0.5, arrived(i), WALL)

    for i, q in enumerate(entering):
        before[q] = arrived(3 + i)
    open_cells = ext[19, x] > 0.5
    for q in leaving:
        _, cy, cz = VEL[q]
        value = jnp.where(open_cells, ext[q, x], WALL)
        if cy:
            value = pltpu.roll(value, cy % 40, 0)
        if cz:
            value = pltpu.roll(value, cz % 128, 1)
        open_ = value < WALL_TEST
        if cz:
            open_ = open_ & (lane != (0 if cz == 1 else 127))
        before[q] = jnp.where(open_, value, arrived(8 + entering.index(OPP[q])))
    for t in range(5):
        rows = pl.ds(8 * t, 8)
        old = [before[q, rows] if VEL[q][0] else None for q in range(19)]
        total, along_y, along_z = message[t], message[5 + t], message[10 + t]
        for q in ACROSS:
            old[q] = jnp.zeros((8, 128), F32)
        old[0], old[3], old[5] = total - along_y - along_z, along_y, along_z
        post = collide(old, fine)
        for i, q in enumerate(entering):
            value = jnp.where(total < WALL_TEST, post[q], old[q])
            fluid = message[40 + 5 * i + t] < WALL_TEST
            outside[i, rows] = jnp.where(fluid & (inside > 0.5), value, WALL)
    step_plane(
        x, ext, first, src2, fine, lane, (cx, lambda q: part(8 + entering.index(q)))
    )
    for e, (plane, outer) in enumerate(
        ((x, (cx, lambda q: outside[entering.index(q)])), (near, None))
    ):

        def emit(q, value, earlier):
            planes[q, plane % 2] = value[0:32]
            rows = pl.ds(40 * q, 40)
            total = value + earlier
            sums[rows] = total if e == 0 else sums[rows] + total

        second_plane(plane, ext, first, src2, lane, emit, outer)
    destinations(sums, read_rates(crate), raw, mixed, rest, send, b)


def first_plane(second):
    return jnp.where(upwards() == second, 0, 6)


def sides(second, message, *refs):
    _, _, has_left, has_right = edges()
    on_left = upwards() == second

    @pl.when(on_left)
    def _():
        side(True, message, has_left, *refs)

    @pl.when(jnp.logical_not(on_left))
    def _():
        side(False, message, has_right, *refs)


def first_side_kernel(
    done, frate, ext, crate, message, first_in, src2_in, send_in, rest_in,
    first, src2, send, rest, fine_out, planes, sums, raw, mixed, before, outside, sem,
):
    copy = pltpu.make_async_copy(done, fine_out.at[:, 2:6], sem)
    copy.start()
    sides(
        False, message, frate, ext, crate, first, src2, send, rest, planes,
        sums, raw, mixed, before, outside,
    )
    copy.wait()


def second_side_kernel(
    done, fine_in, frate, ext, crate, message, first_in, src2_in, send_in, rest_in,
    first, src2, send, rest, fine_out, planes, sums, raw, mixed, before, outside, sem,
):
    copy = pltpu.make_async_copy(done, fine_out.at[:, pl.ds(first_plane(False), 2)], sem)
    copy.start()
    sides(
        True, message, frate, ext, crate, first, src2, send, rest, planes,
        sums, raw, mixed, before, outside,
    )
    got = picked(own_planes(), rest[...])
    send[pl.ds(CHUNK - 1, 32, stride=CHUNK)] = jnp.where(
        iota((32, 128), 1) < 64, got[0:32], got[32:64]
    )
    copy.wait()


def coarse_kernel(
    done, fine_in, got, crate, cp, c_solid, c_cov, ru, rd, ra, rb, out, fine_out,
    mesh, turned, rest, walled, source, message, result, sems,
):
    copy = pltpu.make_async_copy(done, fine_out.at[:, pl.ds(first_plane(True), 2)], sems.at[0])
    copy.start()
    has_prev, has_next, has_left, has_right = edges()
    coarse = read_rates(crate)
    for m in range(6):
        for b in range(4):
            mesh[m, pl.ds(b, 32, stride=4)] = got[pl.ds(6 * b + m, 32, stride=CHUNK)]
    left = got[pl.ds(CHUNK - 1, 32, stride=CHUNK)]
    for b in range(4):
        mesh[6, pl.ds(b, 32, stride=4)] = pltpu.roll(left, -12 * b % 128, 1) if b else left
    for k in range(2):
        for n, m in enumerate((2 * k, 2 * k + 1, 4 + k)):
            turned[k, 128 * n : 128 * n + 128] = mesh[m].T
    rest[...] = mesh[6].T

    goes_up = upwards()
    for i in range(11):
        first, second = ra[X_COARSE + i], rb[X_COARSE + i]
        message[0, i] = jnp.where(goes_up, second, first)
        message[1, i] = jnp.where(goes_up, first, second)

    def pick(code, here, there):
        return jnp.where(code > 1.5, here, jnp.where(code > 0.5, there, WALL))

    def arrived(from_, place):
        return from_[Y_COARSE + place : Y_COARSE + place + 1]

    for k in range(2):
        for t in range(2):
            rows = pl.ds(8 * t, 8)
            fluid = c_solid[k, rows] == 0
            covered = c_cov[k, rows] == 1
            old = []
            for q in range(19):
                start = 16 * q + 8 * t
                old.append(jnp.where(covered, turned[k, start : start + 8], cp[q, k, rows]))
            post = collide(old, coarse)
            for q in range(19):
                value = jnp.where(fluid, post[q], old[q])
                source[q, k + 1, rows] = value
                walled[q, k + 1, rows] = jnp.where(fluid, value, WALL)
        prev_code = arrived(ru, 6 * k + 5) * has_prev
        next_code = arrived(rd, 6 * k + 5) * has_next
        for i in range(5):
            walled[YP[i], k + 1, 23:24] = pick(
                prev_code, rest[64 * k + i : 64 * k + i + 1], arrived(ru, 6 * k + i)
            )
            walled[YM[i], k + 1, 16:17] = pick(
                next_code, rest[64 * k + 5 + i : 64 * k + 6 + i], arrived(rd, 6 * k + i)
            )
        values, from_, z, inside = ((ZP, message.at[0], 0, has_left), (ZM, message.at[1], 3, has_right))[k]
        prev_q, next_q = ((15, 18), (17, 16))[k]

        def from_beyond(value, here):
            return jnp.where(inside > 0.5, jnp.where(value < -WALL_TEST, here, value), WALL)

        for t in range(2):
            for i in range(5):
                start = 304 + 16 * i + 8 * t
                walled[values[i], z, 8 * t : 8 * t + 8] = from_beyond(
                    from_[2 * i + t], turned[k, start : start + 8]
                )
        walled[prev_q, z, 23:24] = from_beyond(
            from_[10, 0:1], rest[64 * k + 10 : 64 * k + 11]
        )
        walled[next_q, z, 16:17] = from_beyond(
            from_[10, 1:2], rest[64 * k + 11 : 64 * k + 12]
        )

    lane = iota((16, 128), 1)
    copies = [copy]
    for z in (1, 2):
        fluid = c_solid[z - 1] == 0
        for q in range(19):
            cx, cy, cz = VEL[q]
            value = walled[q, z - cz]
            if cy:
                value = pltpu.roll(value, cy % 24, 0)
            value = value[0:16]
            if cx:
                value = pltpu.roll(value, cx % 128, 1)
            open_ = value < WALL_TEST
            if cx:
                open_ = open_ & (lane != (0 if cx == 1 else 127))
            bounced = jnp.where(open_, value, source[OPP[q], z, 0:16])
            result[q, z - 1] = jnp.where(fluid, bounced, source[q, z, 0:16])
        copies.append(pltpu.make_async_copy(result.at[:, z - 1], out.at[:, z - 1], sems.at[z]))
        copies[-1].start()
    for copy in copies:
        copy.wait()


VMEM = pl.BlockSpec(memory_space=pltpu.VMEM)
HBM = pl.BlockSpec(memory_space=pltpu.HBM)


def call(kernel, name, ins, outs, scratch=(), aliases=None, weight=1):
    return pl.pallas_call(
        kernel,
        out_shape=[jax.ShapeDtypeStruct(out[0], (out + (F32,))[2]) for out in outs],
        in_specs=ins,
        out_specs=[out[1] for out in outs],
        scratch_shapes=[s if not isinstance(s, tuple) else pltpu.VMEM(s, F32) for s in scratch],
        input_output_aliases=aliases or {},
        compiler_params=pltpu.CompilerParams(vmem_limit_bytes=24 * MIB),
        cost_estimate=pl.CostEstimate(
            flops=weight * 1_000_000_000, bytes_accessed=0, transcendentals=0
        ),
        name=name,
    )


def over_quad(first, second):
    wide, quad = lax.axis_size("wide"), lax.axis_size("quad")
    near, far = [], []
    for w in range(wide):
        for q in range(quad):
            near.append((w * quad + q, w * quad + (q ^ 1)))
            if q in (0, quad - 1):
                far.append((w * quad + q, (w ^ 1) * quad + q))
            else:
                far.append((w * quad + q, w * quad + (q + 1 if q % 2 else q - 1)))
    axes = ("wide", "quad")
    return lax.ppermute(first, axes, near), lax.ppermute(second, axes, far)


def over_wide(first, second):
    wide, quad = lax.axis_size("wide"), lax.axis_size("quad")
    near, far = [], []
    for w in range(wide):
        for q in range(quad):
            near.append((w * quad + q, (w ^ 1) * quad + q))
            if w in (0, wide - 1):
                far.append((w * quad + q, w * quad + (q ^ 1)))
            else:
                far.append((w * quad + q, (w + 1 if w % 2 else w - 1) * quad + q))
    axes = ("wide", "quad")
    second = lax.ppermute(second, axes, far)
    return lax.ppermute(first, axes, near), second


def shards(fine_pops, coarse_pops, fine_solid, coarse_solid, fine_active, coarse_covered, rates):
    i32 = jnp.int32
    dma = pltpu.SemaphoreType.DMA
    ext_shape, pops_shape = (20, 8, 40, 128), (19, 8, 40, 128)
    def in_hbm(*arrays):
        return [pltpu.with_memory_space_constraint(a, pltpu.HBM) for a in arrays]

    ya, yb, solid, on, frate, crate = call(
        rows_first_kernel,
        "collide_rows",
        [HBM] * 7,
        [((Y_FACES, 128), VMEM)] * 2
        + [((8, 32, 128), VMEM, i32), ((2, 32, 128), VMEM)]
        + [((15, 8, 128), VMEM)] * 2,
        [
            pltpu.SMEM((15,), F32),
            (4, 19, 8, 128),
            (4, 19, 8, 128),
            pltpu.VMEM((2, 8, 32), i32),
            (19, 2, 16, 128),
            pltpu.VMEM((2, 16, 128), i32),
            pltpu.VMEM((2, 16, 128), i32),
            (Y_FACES, 128),
            (Y_FACES, 128),
            dma((14,)),
        ],
    )(
        *in_hbm(
            rates, fine_pops, fine_solid, fine_active, coarse_pops, coarse_solid, coarse_covered
        )
    )
    qa, qb = over_quad(ya, yb)
    ext, ya, yb, zu, zd = call(
        cells_first_kernel,
        "collide_cells",
        [VMEM] * 8,
        [(ext_shape, VMEM)] + [((Y_INNER, 128), VMEM)] * 2 + [((6, 16, 128), VMEM)] * 2,
        [(Y_INNER, 128)] * 2,
        weight=2,
    )(frate, crate, fine_pops, solid, on, coarse_pops, coarse_solid, coarse_covered)
    qa2, qb2 = over_quad(ya, yb)
    (face_planes,) = call(
        face_planes_kernel,
        "copy_faces",
        [VMEM],
        [((25, 2, 32, 128), VMEM)],
        weight=20,
    )(ext)
    pa, pb, ru, rd = call(
        faces_kernel,
        "substep_one_faces",
        [VMEM] * 5,
        [((X_ALL, 8, 128), VMEM)] * 2 + [((Y_FACES, 128), VMEM)] * 2,
        [(20, 1, 40, 128), (5, 40, 128), (8, 128), (2, X_ALL, 8, 128)],
    )(face_planes, zu, zd, qa, qb)
    (pb,) = call(
        copy_kernel, "copy_message", [VMEM], [((X_ALL, 8, 128), VMEM)], weight=20
    )(pb)
    ra, rb = over_wide(pa, pb)
    (ext,) = call(
        fill_kernel,
        "fill_rows",
        [VMEM] * 5,
        [(ext_shape, VMEM)],
        [(Y_INNER, 128)] * 2,
        aliases={0: 0},
    )(ext, ru, rd, qa2, qb2)
    kept = [(pops_shape, VMEM)] * 2
    sent = [((32 * CHUNK, 128), VMEM), ((128, 128), VMEM)]
    out_shape = ((19, 8, 32, 128), HBM)
    two_planes = ((19, 2, 32, 128), VMEM)
    work = [(256, 128), (2, 128, 128)]
    side_work = [(768, 128)] + work + [(19, 40, 128), (5, 40, 128), dma]
    first, src2, done, send, rest = call(
        inner_kernel,
        "substeps_inner",
        [VMEM] * 3,
        kept + [((19, 4, 32, 128), VMEM)] + sent,
        [(2, 768, 128)] + work,
        weight=50,
    )(frate, ext, crate)
    first, src2, send, rest, fine_out, done = call(
        first_side_kernel,
        "substeps_first_side",
        [VMEM] * 9,
        kept + sent + [out_shape, two_planes],
        side_work,
        aliases={5: 0, 6: 1, 7: 2, 8: 3},
        weight=2,
    )(done, frate, ext, crate, ra, first, src2, send, rest)
    first, src2, send, rest, fine_out, done = call(
        second_side_kernel,
        "substeps_second_side",
        [VMEM, HBM] + [VMEM] * 8,
        kept + sent + [out_shape, two_planes],
        side_work,
        aliases={1: 4, 6: 0, 7: 1, 8: 2, 9: 3},
        weight=2,
    )(done, fine_out, frate, ext, crate, rb, first, src2, send, rest)
    count = lax.axis_size("wide")
    got = lax.all_to_all(
        send.reshape(count, 1, CHUNK * 128), "wide", split_axis=0, concat_axis=0, tiled=True
    ).reshape(count * CHUNK, 128)
    coarse_out, fine_out = call(
        coarse_kernel,
        "coarse_step",
        [VMEM, HBM] + [VMEM] * 9,
        [((19, 2, 16, 128), HBM), out_shape],
        [(7, 128, 128), (2, 384, 128), (128, 128), (19, 4, 24, 128), (19, 4, 24, 128), (2, 11, 8, 128), (19, 2, 16, 128), dma((3,))],
        aliases={1: 1},
    )(done, fine_out, got, crate, coarse_pops, coarse_solid, coarse_covered, ru, rd, ra, rb)
    return (fine_out, coarse_out)


def solution(mesh):
    in_specs = (
        P(None, "wide", "quad", None),
        P(None, "wide", "quad", None),
        P("wide", "quad", None),
        P("wide", "quad", None),
        P("wide", "quad", None),
        P("wide", "quad", None),
        P(),
    )
    out_specs = (P(None, "wide", "quad", None), P(None, "wide", "quad", None))
    return jax.shard_map(shards, mesh=mesh, in_specs=in_specs, out_specs=out_specs, check_vma=False)
```

```python
import functools

import jax
import jax.numpy as jnp
from jax import lax
from jax.experimental import pallas as pl
from jax.experimental.pallas import tpu as pltpu
from jax.sharding import PartitionSpec as P

VEL = [
    (0, 0, 0),
    (1, 0, 0),
    (-1, 0, 0),
    (0, 1, 0),
    (0, -1, 0),
    (0, 0, 1),
    (0, 0, -1),
    (1, 1, 0),
    (-1, -1, 0),
    (1, -1, 0),
    (-1, 1, 0),
    (1, 0, 1),
    (-1, 0, -1),
    (1, 0, -1),
    (-1, 0, 1),
    (0, 1, 1),
    (0, -1, -1),
    (0, 1, -1),
    (0, -1, 1),
]
OPP = [0, 2, 1, 4, 3, 6, 5, 8, 7, 10, 9, 12, 11, 14, 13, 16, 15, 18, 17]


def moving(axis, sign):
    return [q for q in range(19) if VEL[q][axis] == sign]


XP, XM = moving(0, 1), moving(0, -1)
YP, YM = moving(1, 1), moving(1, -1)
ZP, ZM = moving(2, 1), moving(2, -1)
WALL = 1e30
WALL_TEST = 1e29
F32 = jnp.float32
MIB = 1 << 20

FACES = (0, 7)
INNER = (1, 2, 3, 4, 5, 6)
NEXT = ((1, XM), (6, XP))
ACROSS = [q for q in range(19) if VEL[q][0] == 0]
Y_COARSE = 130
Y_NEXT = 142
Y_FACES = 176
Y_INNER = 392
X_COARSE = 65
X_ALL = X_COARSE + 11
CHUNK = 25

FACTOR = [0.25] * 3 + [0.5] * 3 + [0.25] * 9

def collide(f, rate):
    r_xy, r_xz, r_yz, r_xx, r_yy, r_zz = rate[:6]
    r_xyy, r_xzz, r_yxx, r_yzz, r_zxx, r_zyy, r_xxyy, r_xxzz, r_yyzz = rate[6:]
    sx, dx = f[1] + f[2], f[1] - f[2]
    sy, dy = f[3] + f[4], f[3] - f[4]
    sz, dz = f[5] + f[6], f[5] - f[6]

    def plane(i):
        a, b = f[i] + f[i + 1], f[i + 2] + f[i + 3]
        c, d = f[i] - f[i + 1], f[i + 2] - f[i + 3]
        return a + b, a - b, c + d, c - d

    m_xxyy, m_xy, m_xyy, m_yxx = plane(7)
    m_xxzz, m_xz, m_xzz, m_zxx = plane(11)
    m_yyzz, m_yz, m_yzz, m_zyy = plane(15)
    m_xx = sx + (m_xxyy + m_xxzz)
    m_yy = sy + (m_xxyy + m_yyzz)
    m_zz = sz + (m_xxzz + m_yyzz)
    jx = dx + (m_xyy + m_xzz)
    jy = dy + (m_yxx + m_yzz)
    jz = dz + (m_zxx + m_zyy)
    rho = (f[0] + sx) + (sy + sz) + ((m_xxyy + m_xxzz) + m_yyzz)
    inv = 1.0 / rho
    ux, uy, uz = jx * inv, jy * inv, jz * inv
    xx, yy, zz = jx * ux, jy * uy, jz * uz
    third = rho * (1.0 / 3.0)
    ninth = rho * (1.0 / 9.0)
    jx3, jy3, jz3 = jx * (1.0 / 3.0), jy * (1.0 / 3.0), jz * (1.0 / 3.0)
    xx3, yy3, zz3 = xx * (1.0 / 3.0), yy * (1.0 / 3.0), zz * (1.0 / 3.0)
    h_xx = (m_xx - third - xx) * r_xx
    h_yy = (m_yy - third - yy) * r_yy
    h_zz = (m_zz - third - zz) * r_zz
    post = [None] * 19

    def diagonal(i, fourth, cross, first, second):
        p, m = fourth + cross, fourth - cross
        s, d = first + second, first - second
        post[i] = f[i] - (p + s)
        post[i + 1] = f[i + 1] - (p - s)
        post[i + 2] = f[i + 2] - (m + d)
        post[i + 3] = f[i + 3] - (m - d)

    a_xy = (m_xxyy - ninth - (xx3 + yy3 - 0.5 * zz3)) * r_xxyy
    a_xz = (m_xxzz - ninth - (xx3 + zz3 - 0.5 * yy3)) * r_xxzz
    a_yz = (m_yyzz - ninth - (yy3 + zz3 - 0.5 * xx3)) * r_yyzz
    c_xyy, c_yxx = (m_xyy - jx3) * r_xyy, (m_yxx - jy3) * r_yxx
    c_xzz, c_zxx = (m_xzz - jx3) * r_xzz, (m_zxx - jz3) * r_zxx
    c_yzz, c_zyy = (m_yzz - jy3) * r_yzz, (m_zyy - jz3) * r_zyy
    diagonal(7, a_xy, (m_xy - jx * uy) * r_xy, c_xyy, c_yxx)
    diagonal(11, a_xz, (m_xz - jx * uz) * r_xz, c_xzz, c_zxx)
    diagonal(15, a_yz, (m_yz - jy * uz) * r_yz, c_yzz, c_zyy)

    def straight(i, h, a, c):
        p, n = h - 2.0 * a, 2.0 * c
        post[i] = f[i] - (p - n)
        post[i + 1] = f[i + 1] - (p + n)

    straight(1, h_xx, a_xy + a_xz, c_xyy + c_xzz)
    straight(3, h_yy, a_xy + a_yz, c_yxx + c_yzz)
    straight(5, h_zz, a_xz + a_yz, c_zxx + c_zyy)
    post[0] = f[0] + (2.0 * (h_xx + h_yy + h_zz) - 4.0 * (a_xy + a_xz + a_yz))
    return post


def iota(shape, axis):
    return lax.broadcasted_iota(jnp.int32, shape, axis)


def write_rates(rates, fine, coarse):
    for i in range(15):
        rate = jnp.full((8, 128), rates[i], F32)
        fine[i] = rate * FACTOR[i]
        coarse[i] = FACTOR[i] / (2.0 / rate - 0.5)


def read_rates(ref):
    return [ref[i] for i in range(15)]


def wall_where(code, value):
    return jnp.where(code > 0.5, value, WALL)


def grown_blocks(active):
    grow = (iota((32, 128), 1) // 4 == iota((32, 128), 0)).astype(F32)
    return jnp.dot(active.astype(F32), grow, preferred_element_type=F32)


def edges():
    quad, wide = lax.axis_index("quad"), lax.axis_index("wide")
    return (
        (quad > 0).astype(F32),
        (quad < lax.axis_size("quad") - 1).astype(F32),
        (wide > 0).astype(F32),
        (wide < lax.axis_size("wide") - 1).astype(F32),
    )


def collide_plane(x, f, solid, on, fine, ext):
    for t in range(4):
        rows = pl.ds(8 * t, 8)
        old = [f[q, rows] for q in range(19)]
        fluid = solid[x, rows] == 0
        live = fluid & (on[x // 4, rows] > 0.5)
        post = collide(old, fine)
        for q in range(19):
            ext[q, x, rows] = jnp.where(live, post[q], old[q])
        ext[19, x, rows] = jnp.where(fluid, 1.0 + on[x // 4, rows], 0.0)


def grow(active, on):
    grow_y = (iota((32, 8), 0) // 4 == iota((32, 8), 1)).astype(F32)
    for b in range(2):
        on[b] = jnp.dot(grow_y, grown_blocks(active[b]), preferred_element_type=F32)


def pack_rows(planes, ext, yu, yd):
    fourth = 60 * len(planes)
    for n, x in enumerate(planes):
        for q in range(20):
            start = 60 * n + 3 * q
            yu[start : start + 3] = ext[q, x, 24:32][5:8]
            yd[start : start + 3] = ext[q, x, 0:8][0:3]
        for i in range(5):
            start = fourth + len(planes) * i + n
            yu[start : start + 1] = wall_where(ext[19, x, 24:32], ext[YP[i], x, 24:32])[4:5]
            yd[start : start + 1] = wall_where(ext[19, x, 0:8], ext[YM[i], x, 0:8])[3:4]


def even_quad():
    return lax.axis_index("quad") % 2 == 0


def order_rows(up, down, first, second):
    first[...] = jnp.where(even_quad(), up[...], down[...])
    second[...] = jnp.where(even_quad(), down[...], up[...])


def rows_first_kernel(
    rates_in, f, solid_in, active_in, cp, c_solid, c_cov,
    ya, yb, solid, on, frate, crate,
    rates, low, high, active, cps, c_solids, c_covs, yu, yd, sems,
):
    small = [
        pltpu.make_async_copy(rates_in, rates, sems.at[0]),
        pltpu.make_async_copy(solid_in, solid, sems.at[1]),
        pltpu.make_async_copy(active_in, active, sems.at[2]),
    ]
    coarse_copies = [
        pltpu.make_async_copy(cp, cps, sems.at[3]),
        pltpu.make_async_copy(c_solid, c_solids, sems.at[4]),
        pltpu.make_async_copy(c_cov, c_covs, sems.at[5]),
    ]
    planes = [
        (
            pltpu.make_async_copy(f.at[:, x, 0:8], low.at[n], sems.at[6 + 2 * n]),
            pltpu.make_async_copy(f.at[:, x, 24:32], high.at[n], sems.at[7 + 2 * n]),
        )
        for n, x in enumerate((0, 7, 1, 6))
    ]
    for copy in small:
        copy.start()
    for pair in planes:
        for copy in pair:
            copy.start()
    for copy in coarse_copies:
        copy.start()
    for copy in small:
        copy.wait()
    write_rates(rates, frate, crate)
    fine = read_rates(frate)
    grow(active, on)
    upper = iota((8, 128), 0) < 4
    for n, x in enumerate((0, 7, 1, 6)):
        for copy in planes[n]:
            copy.wait()
        old = [jnp.where(upper, low[n, q], high[n, q]) for q in range(19)]
        fluid = jnp.where(upper, solid[x, 0:8], solid[x, 24:32]) == 0
        here = jnp.where(upper, on[x // 4, 0:8], on[x // 4, 24:32])
        live = fluid & (here > 0.5)
        post = collide(old, fine)
        source = [jnp.where(live, post[q], old[q]) for q in range(19)]
        source.append(jnp.where(fluid, 1.0 + here, 0.0))
        walled = [jnp.where(fluid, value, WALL) for value in source[:19]]
        if n < 2:
            for q in range(20):
                start = 60 * n + 3 * q
                yu[start : start + 3] = source[q][5:8]
                yd[start : start + 3] = source[q][0:3]
            for i in range(5):
                start = 120 + 2 * i + n
                yu[start : start + 1] = walled[YP[i]][4:5]
                yd[start : start + 1] = walled[YM[i]][3:4]
        else:
            e = n - 2
            for i, q in enumerate(NEXT[e][1]):
                start = Y_NEXT + 15 * e + 3 * i
                fourth = Y_NEXT + 30 + e
                yu[start : start + 3] = walled[q][5:8]
                yd[start : start + 3] = walled[q][0:3]
                if q in YP:
                    yu[fourth : fourth + 1] = walled[q][4:5]
                if q in YM:
                    yd[fourth : fourth + 1] = walled[q][3:4]
    for copy in coarse_copies:
        copy.wait()
    coarse = read_rates(crate)
    for z in range(2):
        old = [jnp.where(upper, cps[q, z, 0:8], cps[q, z, 8:16]) for q in range(19)]
        post = collide(old, coarse)
        fluid = jnp.where(upper, c_solids[z, 0:8], c_solids[z, 8:16]) == 0
        covered = jnp.where(upper, c_covs[z, 0:8], c_covs[z, 8:16]).astype(F32)
        code = jnp.where(fluid, 1.0 + covered, 0.0)
        for i in range(6):
            place = Y_COARSE + 6 * z + i
            yu[place : place + 1] = (code if i == 5 else post[YP[i]])[7:8]
            yd[place : place + 1] = (code if i == 5 else post[YM[i]])[0:1]
    order_rows(yu, yd, ya, yb)


def cells_first_kernel(
    frate, crate, f, solid, on, cp, c_solid, c_cov, ext, ya, yb, zu, zd, yu, yd
):
    fine = read_rates(frate)

    def plane(x, carry):
        collide_plane(x, f.at[:, x], solid, on, fine, ext)
        return carry

    lax.fori_loop(0, 8, plane, 0)
    pack_rows(INNER, ext, yu, yd)
    order_rows(yu, yd, ya, yb)
    coarse = read_rates(crate)
    for z, values, to in ((1, ZP, zu), (0, ZM, zd)):
        for t in range(2):
            rows = pl.ds(8 * t, 8)
            post = collide([cp[q, z, rows] for q in range(19)], coarse)
            for i in range(5):
                to[i, rows] = post[values[i]]
            to[5, rows] = jnp.where(c_solid[z, rows] == 0, 1.0 + c_cov[z, rows].astype(F32), 0.0)


def fill_rows(q, planes, n, ru, rd, to):
    start = 60 * n + 3 * q
    to[0:3] = rd[start : start + 3]
    to[5:8] = ru[start : start + 3]
    fourth = 60 * len(planes) + n
    if q in YM:
        place = fourth + len(planes) * YM.index(q)
        to[3:4] = rd[place : place + 1]
    if q in YP:
        place = fourth + len(planes) * YP.index(q)
        to[4:5] = ru[place : place + 1]


def fill_code(n, ru, rd, to, has_prev, has_next):
    start = 60 * n + 57
    to[0:3] = rd[start : start + 3] * has_next
    to[5:8] = ru[start : start + 3] * has_prev
    to[3:4] = jnp.full((1, 128), has_next, F32)
    to[4:5] = jnp.full((1, 128), has_prev, F32)


def upwards():
    return lax.axis_index("wide") % 2 == 0


def face_planes_kernel(ext, held):
    for face, x in enumerate(FACES):
        for q in range(20):
            held[q, face, 0:32] = ext[q, x, 0:32]
        near, values = NEXT[face]
        for i, q in enumerate(values):
            held[20 + i, face, 0:32] = wall_where(ext[19, near, 0:32], ext[q, near, 0:32])


def copy_kernel(from_, to):
    to[...] = from_[...]


def faces_kernel(planes, zu, zd, qa, qb, pa, pb, ru, rd, held, beyond, tile, both):
    has_prev, has_next, _, _ = edges()
    order_rows(qb, qa, ru, rd)
    lane = iota((40, 128), 1)
    inside = jnp.where(iota((8, 128), 0) < 4, has_next, has_prev) > 0.5
    for face, x in enumerate(FACES):
        place = jnp.where(upwards() == (x == 7), 0, 1)
        for q in range(19):
            held[q, 0, 0:32] = planes[q, face, 0:32]
            fill_rows(q, FACES, face, ru, rd, held.at[q, 0, 32:40])
        held[19, 0, 0:32] = planes[19, face, 0:32]
        fill_code(face, ru, rd, held.at[19, 0, 32:40], has_prev, has_next)
        values = NEXT[face][1]
        for i, q in enumerate(values):
            beyond[i, 0:32] = planes[20 + i, face, 0:32]
            start = Y_NEXT + 15 * face + 3 * i
            fourth = Y_NEXT + 30 + face
            tile[0:3] = rd[start : start + 3]
            tile[5:8] = ru[start : start + 3]
            if q in YM:
                tile[3:4] = rd[fourth : fourth + 1]
            if q in YP:
                tile[4:5] = ru[fourth : fourth + 1]
            beyond[i, 32:40] = jnp.where(inside, tile[...], WALL)
        code = held[19, 0]
        live, open_cells = code > 1.5, {0: code > 0.5}
        outer = (VEL[values[0]][0], lambda q: beyond[values.index(q)])
        staying = {q: streamed(q, 0, held, open_cells, live, lane, outer) for q in ACROSS}
        total = None
        for q, part in staying.items():
            total = part if total is None else total + part
        along_y = (staying[3] - staying[4]) + (staying[15] - staying[16]) + (staying[17] - staying[18])
        along_z = (staying[5] - staying[6]) + (staying[15] - staying[16]) - (staying[17] - staying[18])
        for i in range(13):
            if i < 3:
                part = (jnp.where(live, total, WALL), along_y, along_z)[i]
            elif i < 8:
                part = streamed(values[i - 3], 0, held, open_cells, live, lane, outer)
            else:
                part = wall_where(code, held[values[i - 8], 0])
            for t in range(5):
                both[place, 5 * i + t] = part[8 * t : 8 * t + 8]
        z, arriving, leaving, from_ = ((0, 17, 16, zd), (1, 15, 18, zu))[face]

        def marked(cells, value):
            return wall_where(cells, jnp.where(cells > 1.5, -WALL, value))

        for t in range(2):
            rows = pl.ds(8 * t, 8)
            for i in range(5):
                both[place, X_COARSE + 2 * i + t] = marked(from_[5, rows], from_[i, rows])

        def arrived(rows, i):
            row = Y_COARSE + 6 * z + i
            return rows[row : row + 1]

        tile[0:1] = marked(arrived(ru, 5) * has_prev, arrived(ru, YP.index(arriving)))
        tile[1:2] = marked(arrived(rd, 5) * has_next, arrived(rd, YM.index(leaving)))
        both[place, X_COARSE + 10] = tile[...]
    pa[...] = both[0]
    pb[...] = both[1]


def streamed(q, x, values, open_cells, live, lane, outer=None):
    cx, cy, cz = VEL[q]
    if q == 0:
        return values[0, x]
    if cx and outer is not None and outer[0] == cx:
        value = outer[1](q)
    else:
        value = jnp.where(open_cells[cx], values[q, x - cx], WALL)
    if cy:
        value = pltpu.roll(value, cy % 40, 0)
    if cz:
        value = pltpu.roll(value, cz % 128, 1)
    open_ = value < WALL_TEST
    if cz:
        open_ = open_ & (lane != (0 if cz == 1 else 127))
    return jnp.where(live, jnp.where(open_, value, values[OPP[q], x]), values[q, x])


def step_plane(x, ext, first, src2, fine, lane, outer=None):
    open_cells = {}
    for cx in (-1, 0, 1):
        if outer is None or outer[0] != cx:
            open_cells[cx] = ext[19, x - cx] > 0.5
    live = ext[19, x] > 1.5
    for q in range(19):
        first[q, x] = streamed(q, x, ext, open_cells, live, lane, outer)
    for t in range(5):
        rows = pl.ds(8 * t, 8)
        live_t = ext[19, x, rows] > 1.5
        old = [first[q, x, rows] for q in range(19)]
        post = collide(old, fine)
        for q in range(19):
            src2[q, x, rows] = jnp.where(live_t, post[q], old[q])


def fill_kernel(ext_in, ru, rd, qa, qb, ext, ru2, rd2):
    has_prev, has_next, _, _ = edges()
    order_rows(qb, qa, ru2, rd2)
    for planes, up, down in ((FACES, ru, rd), (INNER, ru2, rd2)):
        for n, x in enumerate(planes):
            for q in range(19):
                fill_rows(q, planes, n, up, down, ext.at[q, x, 32:40])
            fill_code(n, up, down, ext.at[19, x, 32:40], has_prev, has_next)


def second_plane(x, ext, first, src2, lane, emit, outer=None):
    open_cells = {}
    for cx in (-1, 0, 1):
        if outer is None or outer[0] != cx:
            open_cells[cx] = ext[19, x - cx] > 0.5
    live = ext[19, x] > 1.5
    for q in range(19):
        emit(q, streamed(q, x, src2, open_cells, live, lane, outer), first[q, x])


def own_planes():
    z_pair = iota((64, 256), 1) % 128 // 2
    row = iota((64, 256), 0)
    plane = 2 * (row % 32) + row // 32
    return jnp.where(z_pair == plane, 0.0625, 0.0).astype(jnp.bfloat16)


def picked(rows, cells):
    high = cells.astype(jnp.bfloat16)
    low = (cells - high.astype(F32)).astype(jnp.bfloat16)
    return lax.dot_general(
        rows,
        jnp.concatenate([high, low], axis=1),
        (((1,), (1,)), ((), ())),
        preferred_element_type=F32,
    )


def destinations(sums, coarse, raw, mixed, rest, send, b):
    even = iota((8, 128), 1) % 2 == 0

    def alone(value, shift):
        value = jnp.where(even, 16.0 * value, 0.0)
        return pltpu.roll(value, 2 * shift % 128, 1) if shift else value

    for t in range(3):
        cells = []
        for q in range(19):
            start = 40 * q + 16 * t
            value = sums[pl.ds(start, 8, stride=2)] + sums[pl.ds(start + 1, 8, stride=2)]
            if t < 2:
                place = 16 * q + 8 * t
                if q < 16:
                    raw[place : place + 8] = value
                else:
                    mixed[0, place - 256 : place - 248] = value
                    mixed[1, place - 256 : place - 248] = value
            cells.append((value + pltpu.roll(value, 127, 1)) * 0.0625)
        post = collide(cells, coarse)
        if t < 2:
            for i in range(5):
                place = 48 + 16 * i + 8 * t
                mixed[0, place : place + 8] = alone(post[ZP[i]], 1)
                mixed[1, place : place + 8] = alone(post[ZM[i]], -1)
        else:
            last = [alone(post[q], 0)[3:4] for q in YP] + [alone(post[q], 0)[0:1] for q in YM]
            for k in range(2):
                corners = ((15, 18), (17, 16))[k]
                shift = (1, -1)[k]
                here = last + [alone(post[corners[0]], shift)[3:4], alone(post[corners[1]], shift)[0:1]]
                for i in range(12):
                    rest[pl.ds(64 * k + 12 * b + i, 1)] = here[i]
    planes = own_planes()
    got = picked(planes, raw[...])
    for n in range(2):
        for k in range(2):
            send[pl.ds(6 * b + 2 * k + n, 32, stride=CHUNK)] = got[
                32 * k : 32 * k + 32, 128 * n : 128 * n + 128
            ]
    got = picked(planes, mixed[...].reshape(256, 128))
    for k in range(2):
        send[pl.ds(6 * b + 4 + k, 32, stride=CHUNK)] = got[
            32 * k : 32 * k + 32, 128 * k : 128 * k + 128
        ]


def inner_kernel(
    frate, ext, crate, first, src2, planes, send, rest, sums, raw, mixed
):
    fine = read_rates(frate)
    lane = iota((40, 128), 1)
    rest[...] = jnp.zeros(rest.shape, F32)

    def substep_one(x, carry):
        step_plane(x, ext, first, src2, fine, lane)
        return carry

    lax.fori_loop(1, 7, substep_one, 0)

    def pair(b, carry):
        for e in range(2):
            x = 2 * b + e

            def emit(q, value, before):
                planes[q, x - 2] = value[0:32]
                rows = pl.ds(40 * q, 40)
                total = value + before
                sums[b - 1, rows] = total if e == 0 else sums[b - 1, rows] + total

            second_plane(x, ext, first, src2, lane, emit)
        return carry

    lax.fori_loop(1, 3, pair, 0)
    coarse = read_rates(crate)
    for b in (1, 2):
        destinations(sums.at[b - 1], coarse, raw, mixed, rest, send, b)


def side(
    left, message, inside, frate, ext, crate, first, src2, send, rest, planes,
    sums, raw, mixed, before, outside,
):
    fine = read_rates(frate)
    lane = iota((40, 128), 1)
    entering, leaving = (XP, XM) if left else (XM, XP)
    cx = 1 if left else -1
    x, near, b = (0, 1, 0) if left else (7, 6, 3)

    def arrived(i):
        return message[5 * i : 5 * i + 5].reshape(40, 128)

    def part(i):
        return jnp.where(inside > 0.5, arrived(i), WALL)

    for i, q in enumerate(entering):
        before[q] = arrived(3 + i)
    open_cells = ext[19, x] > 0.5
    for q in leaving:
        _, cy, cz = VEL[q]
        value = jnp.where(open_cells, ext[q, x], WALL)
        if cy:
            value = pltpu.roll(value, cy % 40, 0)
        if cz:
            value = pltpu.roll(value, cz % 128, 1)
        open_ = value < WALL_TEST
        if cz:
            open_ = open_ & (lane != (0 if cz == 1 else 127))
        before[q] = jnp.where(open_, value, arrived(8 + entering.index(OPP[q])))
    for t in range(5):
        rows = pl.ds(8 * t, 8)
        old = [before[q, rows] if VEL[q][0] else None for q in range(19)]
        total, along_y, along_z = message[t], message[5 + t], message[10 + t]
        for q in ACROSS:
            old[q] = jnp.zeros((8, 128), F32)
        old[0], old[3], old[5] = total - along_y - along_z, along_y, along_z
        post = collide(old, fine)
        for i, q in enumerate(entering):
            value = jnp.where(total < WALL_TEST, post[q], old[q])
            fluid = message[40 + 5 * i + t] < WALL_TEST
            outside[i, rows] = jnp.where(fluid & (inside > 0.5), value, WALL)
    step_plane(
        x, ext, first, src2, fine, lane, (cx, lambda q: part(8 + entering.index(q)))
    )
    for e, (plane, outer) in enumerate(
        ((x, (cx, lambda q: outside[entering.index(q)])), (near, None))
    ):

        def emit(q, value, earlier):
            planes[q, plane % 2] = value[0:32]
            rows = pl.ds(40 * q, 40)
            total = value + earlier
            sums[rows] = total if e == 0 else sums[rows] + total

        second_plane(plane, ext, first, src2, lane, emit, outer)
    destinations(sums, read_rates(crate), raw, mixed, rest, send, b)


def first_plane(second):
    return jnp.where(upwards() == second, 0, 6)


def sides(second, message, *refs):
    _, _, has_left, has_right = edges()
    on_left = upwards() == second

    @pl.when(on_left)
    def _():
        side(True, message, has_left, *refs)

    @pl.when(jnp.logical_not(on_left))
    def _():
        side(False, message, has_right, *refs)


def first_side_kernel(
    done, frate, ext, crate, message, first_in, src2_in, send_in, rest_in,
    first, src2, send, rest, fine_out, planes, sums, raw, mixed, before, outside, sem,
):
    copy = pltpu.make_async_copy(done, fine_out.at[:, 2:6], sem)
    copy.start()
    sides(
        False, message, frate, ext, crate, first, src2, send, rest, planes,
        sums, raw, mixed, before, outside,
    )
    copy.wait()


def second_side_kernel(
    done, fine_in, frate, ext, crate, message, first_in, src2_in, send_in, rest_in,
    first, src2, send, rest, fine_out, planes, sums, raw, mixed, before, outside, sem,
):
    copy = pltpu.make_async_copy(done, fine_out.at[:, pl.ds(first_plane(False), 2)], sem)
    copy.start()
    sides(
        True, message, frate, ext, crate, first, src2, send, rest, planes,
        sums, raw, mixed, before, outside,
    )
    got = picked(own_planes(), rest[...])
    send[pl.ds(CHUNK - 1, 32, stride=CHUNK)] = jnp.where(
        iota((32, 128), 1) < 64, got[0:32], got[32:64]
    )
    copy.wait()


def coarse_kernel(
    done, fine_in, got, crate, cp, c_solid, c_cov, ru, rd, ra, rb, out, fine_out,
    mesh, turned, rest, walled, source, message, result, sems,
):
    copy = pltpu.make_async_copy(done, fine_out.at[:, pl.ds(first_plane(True), 2)], sems.at[0])
    copy.start()
    has_prev, has_next, has_left, has_right = edges()
    coarse = read_rates(crate)
    for m in range(6):
        for b in range(4):
            mesh[m, pl.ds(b, 32, stride=4)] = got[pl.ds(6 * b + m, 32, stride=CHUNK)]
    left = got[pl.ds(CHUNK - 1, 32, stride=CHUNK)]
    for b in range(4):
        mesh[6, pl.ds(b, 32, stride=4)] = pltpu.roll(left, -12 * b % 128, 1) if b else left
    for k in range(2):
        for n, m in enumerate((2 * k, 2 * k + 1, 4 + k)):
            turned[k, 128 * n : 128 * n + 128] = mesh[m].T
    rest[...] = mesh[6].T

    goes_up = upwards()
    for i in range(11):
        first, second = ra[X_COARSE + i], rb[X_COARSE + i]
        message[0, i] = jnp.where(goes_up, second, first)
        message[1, i] = jnp.where(goes_up, first, second)

    def pick(code, here, there):
        return jnp.where(code > 1.5, here, jnp.where(code > 0.5, there, WALL))

    def arrived(from_, place):
        return from_[Y_COARSE + place : Y_COARSE + place + 1]

    for k in range(2):
        for t in range(2):
            rows = pl.ds(8 * t, 8)
            fluid = c_solid[k, rows] == 0
            covered = c_cov[k, rows] == 1
            old = []
            for q in range(19):
                start = 16 * q + 8 * t
                old.append(jnp.where(covered, turned[k, start : start + 8], cp[q, k, rows]))
            post = collide(old, coarse)
            for q in range(19):
                value = jnp.where(fluid, post[q], old[q])
                source[q, k + 1, rows] = value
                walled[q, k + 1, rows] = jnp.where(fluid, value, WALL)
        prev_code = arrived(ru, 6 * k + 5) * has_prev
        next_code = arrived(rd, 6 * k + 5) * has_next
        for i in range(5):
            walled[YP[i], k + 1, 23:24] = pick(
                prev_code, rest[64 * k + i : 64 * k + i + 1], arrived(ru, 6 * k + i)
            )
            walled[YM[i], k + 1, 16:17] = pick(
                next_code, rest[64 * k + 5 + i : 64 * k + 6 + i], arrived(rd, 6 * k + i)
            )
        values, from_, z, inside = ((ZP, message.at[0], 0, has_left), (ZM, message.at[1], 3, has_right))[k]
        prev_q, next_q = ((15, 18), (17, 16))[k]

        def from_beyond(value, here):
            return jnp.where(inside > 0.5, jnp.where(value < -WALL_TEST, here, value), WALL)

        for t in range(2):
            for i in range(5):
                start = 304 + 16 * i + 8 * t
                walled[values[i], z, 8 * t : 8 * t + 8] = from_beyond(
                    from_[2 * i + t], turned[k, start : start + 8]
                )
        walled[prev_q, z, 23:24] = from_beyond(
            from_[10, 0:1], rest[64 * k + 10 : 64 * k + 11]
        )
        walled[next_q, z, 16:17] = from_beyond(
            from_[10, 1:2], rest[64 * k + 11 : 64 * k + 12]
        )

    lane = iota((16, 128), 1)
    copies = [copy]
    for z in (1, 2):
        fluid = c_solid[z - 1] == 0
        for q in range(19):
            cx, cy, cz = VEL[q]
            value = walled[q, z - cz]
            if cy:
                value = pltpu.roll(value, cy % 24, 0)
            value = value[0:16]
            if cx:
                value = pltpu.roll(value, cx % 128, 1)
            open_ = value < WALL_TEST
            if cx:
                open_ = open_ & (lane != (0 if cx == 1 else 127))
            bounced = jnp.where(open_, value, source[OPP[q], z, 0:16])
            result[q, z - 1] = jnp.where(fluid, bounced, source[q, z, 0:16])
        copies.append(pltpu.make_async_copy(result.at[:, z - 1], out.at[:, z - 1], sems.at[z]))
        copies[-1].start()
    for copy in copies:
        copy.wait()


VMEM = pl.BlockSpec(memory_space=pltpu.VMEM)
HBM = pl.BlockSpec(memory_space=pltpu.HBM)


def call(kernel, name, ins, outs, scratch=(), aliases=None, weight=1):
    return pl.pallas_call(
        kernel,
        out_shape=[jax.ShapeDtypeStruct(out[0], (out + (F32,))[2]) for out in outs],
        in_specs=ins,
        out_specs=[out[1] for out in outs],
        scratch_shapes=[s if not isinstance(s, tuple) else pltpu.VMEM(s, F32) for s in scratch],
        input_output_aliases=aliases or {},
        compiler_params=pltpu.CompilerParams(vmem_limit_bytes=24 * MIB),
        cost_estimate=pl.CostEstimate(
            flops=weight * 1_000_000_000, bytes_accessed=0, transcendentals=0
        ),
        name=name,
    )


def over_quad(first, second):
    wide, quad = lax.axis_size("wide"), lax.axis_size("quad")
    near, far = [], []
    for w in range(wide):
        for q in range(quad):
            near.append((w * quad + q, w * quad + (q ^ 1)))
            if q in (0, quad - 1):
                far.append((w * quad + q, (w ^ 1) * quad + q))
            else:
                far.append((w * quad + q, w * quad + (q + 1 if q % 2 else q - 1)))
    axes = ("wide", "quad")
    return lax.ppermute(first, axes, near), lax.ppermute(second, axes, far)


def over_wide(first, second):
    wide, quad = lax.axis_size("wide"), lax.axis_size("quad")
    near, far = [], []
    for w in range(wide):
        for q in range(quad):
            near.append((w * quad + q, (w ^ 1) * quad + q))
            if w in (0, wide - 1):
                far.append((w * quad + q, w * quad + (q ^ 1)))
            else:
                far.append((w * quad + q, (w + 1 if w % 2 else w - 1) * quad + q))
    axes = ("wide", "quad")
    second = lax.ppermute(second, axes, far)
    return lax.ppermute(first, axes, near), second


def shards(fine_pops, coarse_pops, fine_solid, coarse_solid, fine_active, coarse_covered, rates):
    i32 = jnp.int32
    dma = pltpu.SemaphoreType.DMA
    ext_shape, pops_shape = (20, 8, 40, 128), (19, 8, 40, 128)
    def in_hbm(*arrays):
        return [pltpu.with_memory_space_constraint(a, pltpu.HBM) for a in arrays]

    ya, yb, solid, on, frate, crate = call(
        rows_first_kernel,
        "collide_rows",
        [HBM] * 7,
        [((Y_FACES, 128), VMEM)] * 2
        + [((8, 32, 128), VMEM, i32), ((2, 32, 128), VMEM)]
        + [((15, 8, 128), VMEM)] * 2,
        [
            pltpu.SMEM((15,), F32),
            (4, 19, 8, 128),
            (4, 19, 8, 128),
            pltpu.VMEM((2, 8, 32), i32),
            (19, 2, 16, 128),
            pltpu.VMEM((2, 16, 128), i32),
            pltpu.VMEM((2, 16, 128), i32),
            (Y_FACES, 128),
            (Y_FACES, 128),
            dma((14,)),
        ],
    )(
        *in_hbm(
            rates, fine_pops, fine_solid, fine_active, coarse_pops, coarse_solid, coarse_covered
        )
    )
    qa, qb = over_quad(ya, yb)
    ext, ya, yb, zu, zd = call(
        cells_first_kernel,
        "collide_cells",
        [VMEM] * 8,
        [(ext_shape, VMEM)] + [((Y_INNER, 128), VMEM)] * 2 + [((6, 16, 128), VMEM)] * 2,
        [(Y_INNER, 128)] * 2,
        weight=2,
    )(frate, crate, fine_pops, solid, on, coarse_pops, coarse_solid, coarse_covered)
    qa2, qb2 = over_quad(ya, yb)
    (face_planes,) = call(
        face_planes_kernel,
        "copy_faces",
        [VMEM],
        [((25, 2, 32, 128), VMEM)],
        weight=20,
    )(ext)
    pa, pb, ru, rd = call(
        faces_kernel,
        "substep_one_faces",
        [VMEM] * 5,
        [((X_ALL, 8, 128), VMEM)] * 2 + [((Y_FACES, 128), VMEM)] * 2,
        [(20, 1, 40, 128), (5, 40, 128), (8, 128), (2, X_ALL, 8, 128)],
    )(face_planes, zu, zd, qa, qb)
    ra, rb = over_wide(pa, pb)
    (ext,) = call(
        fill_kernel,
        "fill_rows",
        [VMEM] * 5,
        [(ext_shape, VMEM)],
        [(Y_INNER, 128)] * 2,
        aliases={0: 0},
    )(ext, ru, rd, qa2, qb2)
    kept = [(pops_shape, VMEM)] * 2
    sent = [((32 * CHUNK, 128), VMEM), ((128, 128), VMEM)]
    out_shape = ((19, 8, 32, 128), HBM)
    two_planes = ((19, 2, 32, 128), VMEM)
    work = [(256, 128), (2, 128, 128)]
    side_work = [(768, 128)] + work + [(19, 40, 128), (5, 40, 128), dma]
    first, src2, done, send, rest = call(
        inner_kernel,
        "substeps_inner",
        [VMEM] * 3,
        kept + [((19, 4, 32, 128), VMEM)] + sent,
        [(2, 768, 128)] + work,
        weight=50,
    )(frate, ext, crate)
    first, src2, send, rest, fine_out, done = call(
        first_side_kernel,
        "substeps_first_side",
        [VMEM] * 9,
        kept + sent + [out_shape, two_planes],
        side_work,
        aliases={5: 0, 6: 1, 7: 2, 8: 3},
        weight=2,
    )(done, frate, ext, crate, ra, first, src2, send, rest)
    first, src2, send, rest, fine_out, done = call(
        second_side_kernel,
        "substeps_second_side",
        [VMEM, HBM] + [VMEM] * 8,
        kept + sent + [out_shape, two_planes],
        side_work,
        aliases={1: 4, 6: 0, 7: 1, 8: 2, 9: 3},
        weight=2,
    )(done, fine_out, frate, ext, crate, rb, first, src2, send, rest)
    count = lax.axis_size("wide")
    got = lax.all_to_all(
        send.reshape(count, 1, CHUNK * 128), "wide", split_axis=0, concat_axis=0, tiled=True
    ).reshape(count * CHUNK, 128)
    coarse_out, fine_out = call(
        coarse_kernel,
        "coarse_step",
        [VMEM, HBM] + [VMEM] * 9,
        [((19, 2, 16, 128), HBM), out_shape],
        [(7, 128, 128), (2, 384, 128), (128, 128), (19, 4, 24, 128), (19, 4, 24, 128), (2, 11, 8, 128), (19, 2, 16, 128), dma((3,))],
        aliases={1: 1},
    )(done, fine_out, got, crate, coarse_pops, coarse_solid, coarse_covered, ru, rd, ra, rb)
    return (fine_out, coarse_out)


def solution(mesh):
    in_specs = (
        P(None, "wide", "quad", None),
        P(None, "wide", "quad", None),
        P("wide", "quad", None),
        P("wide", "quad", None),
        P("wide", "quad", None),
        P("wide", "quad", None),
        P(),
    )
    out_specs = (P(None, "wide", "quad", None), P(None, "wide", "quad", None))
    return jax.shard_map(shards, mesh=mesh, in_specs=in_specs, out_specs=out_specs, check_vma=False)
```
